32 devices in a mesh: spec: 2 (over x), tm: 16 (over z, y, core).
Axes of the slice: x: 2, y: 2, z: 4, core: 2. Of those that a mesh axis runs over, the one named last changes fastest.
Arguments:
- series: bfloat16 [64, 32768], P(None, ('spec', 'tm')), parts along dimension 1, may hold values from -8 to 8
- loadings: bfloat16 [32768, 256], P('spec'), parts along dimension 0, may hold values from -0.046875 to 0.046875
- precision: float32 [32768], P('spec'), parts along dimension 0, may hold values from 0.5 to 4
- start_day: int32 [32768], P('spec'), parts along dimension 0, may hold values from 0 to 15
- stop_day: int32 [32768], P('spec'), parts along dimension 0, may hold values from 49 to 64
- off_day: int32 [32768], P('spec'), parts along dimension 0, may hold values from 0 to 6
- decay: float32 [256], replicated, may hold values from 0 to 1
- gain: bfloat16 [256, 256], replicated, may hold values from -1 to 1
- smoother: float32 [256, 256], replicated, may hold values from -1 to 1
Outputs:
- smoothed: float32 [64, 512], P('tm', 'spec'), parts along dimension 1
- scores: bfloat16 [64, 32768], P(None, ('spec', 'tm')), parts along dimension 1
The draws below stay inside these ranges and needn't reach their ends.
There are 2 independent parts, one for each index of `spec`. The reference program is written for one: setup_inputs(seed, part) draws one part's arguments, and reference() takes and returns one part's arrays. A program takes and returns all parts, laid end to end along the dimension named above; an argument that names none is the same for every part. Nothing has to cross between parts.
All inputs are finite; a program needn't handle non-finite values.
Results may differ from the reference program's by a relative error of at most 0.002.
The reference program's roundings to bfloat16 on the way count: a program that leaves them out, or rounds other values in their place, can miss the bound.
Values may be sent and summed in bfloat16 or wider, within the bound.
No kernel may reach another device: no remote copies, remote signals or barrier semaphores. Data moves between devices by JAX's collectives and lax.ppermute only.
A program may use at most 192 MiB of HBM per device.

```python
import math
import jax
import jax.numpy as jnp
from jax import lax

K = 256
PROV = 16384
DAYS = 64


def draw_series(key, part):
    base = jax.random.fold_in(key, 11)
    key_level, key_trend, key_noise = jax.random.split(base, 3)
    levels = jax.random.normal(key_level, (PROV,), jnp.float32)
    trends = 0.6 * jax.random.normal(key_trend, (PROV,), jnp.float32)
    ramp = (2.0 * jnp.arange(DAYS, dtype=jnp.float32) / DAYS - 1.0)[:, None]
    noise = 0.7 * jax.random.normal(key_noise, (DAYS, PROV), jnp.float32)
    values = levels[None, :] + trends[None, :] * ramp + noise
    return jnp.clip(values, -8.0, 8.0).astype(jnp.bfloat16)


def decay_rates(key):
    base = jax.random.fold_in(key, 23)
    low = jnp.log(0.3 / DAYS)
    high = jnp.log(1.0 / 30.0)
    return jnp.exp(jax.random.uniform(base, (K,), jnp.float32, low, high))


def draw_decay(key, part):
    rates = decay_rates(key)
    return (1.0 - rates).astype(jnp.float32)


def symmetric_part(key):
    normal_draw = jax.random.normal(key, (K, K), jnp.float32)
    return (normal_draw + normal_draw.T) * (0.125 / jnp.sqrt(2.0 * K))


def draw_gain(key, part):
    base = jax.random.fold_in(key, 37)
    key_rate, key_mix = jax.random.split(base, 2)
    rates = jnp.exp(jax.random.uniform(key_rate, (K,), jnp.float32, jnp.log(0.3 / DAYS), jnp.log(0.05)))
    roots = jnp.sqrt(rates)
    mixed = jnp.eye(K, dtype=jnp.float32) + symmetric_part(key_mix)
    return (roots[:, None] * roots[None, :] * mixed).astype(jnp.bfloat16)


def draw_smoother(key, part):
    base = jax.random.fold_in(key, 53)
    key_factor, key_mix = jax.random.split(base, 2)
    rates = decay_rates(key) * jax.random.uniform(key_factor, (K,), jnp.float32, 0.5, 1.5)
    uniform_draw = jax.random.uniform(key_mix, (K, K), jnp.float32, -1.0, 1.0)
    coupling = jnp.sqrt(0.1 / DAYS) / K
    skew = 0.5 * (uniform_draw - uniform_draw.T) * coupling
    diagonal = jnp.eye(K, dtype=jnp.float32) * (1.0 - rates)[None, :]
    return (diagonal + skew).astype(jnp.float32)


def place_ends(array, own_key, smallest, largest):
    index_at = [jax.random.randint(jax.random.fold_in(own_key, axis), (), 0, length) for axis, length in enumerate(array.shape)]
    main_axis = array.shape.index(max(array.shape))
    beside = index_at[:main_axis] + [(index_at[main_axis] + 1) % array.shape[main_axis]] + index_at[main_axis + 1:]
    return array.at[tuple(index_at)].set(smallest).at[tuple(beside)].set(largest)


def bell_draw(stream_key, shape, deviation, bound, kind=jnp.bfloat16):
    array = jax.random.normal(stream_key, shape, jnp.float32) * deviation
    return jnp.minimum(jnp.maximum(array, -bound), bound).astype(kind)


def setup_inputs(seed: int = 0, part: int = 0) -> dict:
    key_of = jax.random.split(jax.random.key(seed), 10)
    part_keys = jax.random.split(jax.random.fold_in(key_of[9], part), 10)
    return {
        "series": draw_series(jax.random.fold_in(jax.random.fold_in(key_of[9], part), 71), part),
        "loadings": bell_draw(part_keys[1], (PROV, K), PROV ** -0.5, 0.046875),
        "precision": jnp.clip(jnp.exp(jax.random.uniform(part_keys[2], (PROV,), jnp.float32, math.log(0.5), math.log(4.0))), 0.5, 4.0),
        "start_day": place_ends(jax.random.randint(part_keys[3], (PROV,), 0, DAYS // 4), jax.random.fold_in(part_keys[3], 1), 0, (DAYS // 4) - 1).astype(jnp.int32),
        "stop_day": place_ends(jax.random.randint(part_keys[4], (PROV,), 3 * DAYS // 4 + 1, DAYS + 1), jax.random.fold_in(part_keys[4], 1), 3 * DAYS // 4 + 1, DAYS).astype(jnp.int32),
        "off_day": place_ends(jax.random.randint(part_keys[5], (PROV,), 0, 7), jax.random.fold_in(part_keys[5], 1), 0, 6).astype(jnp.int32),
        "decay": draw_decay(jax.random.fold_in(key_of[9], 71), part),
        "gain": draw_gain(jax.random.fold_in(key_of[9], 71), part),
        "smoother": draw_smoother(jax.random.fold_in(key_of[9], 71), part),
    }


def reference(series, loadings, precision, start_day, stop_day, off_day, decay, gain, smoother):
    high = lax.Precision.HIGHEST
    day_ids = jnp.arange(DAYS, dtype=jnp.int32)
    active = ((day_ids[:, None] >= start_day[None, :]) & (day_ids[:, None] < stop_day[None, :]) & (day_ids[:, None] % 7 != off_day[None, :])).astype(jnp.float32)
    weights = active * precision[None, :]
    loadings_wide = loadings.astype(jnp.float32)
    gain_wide = gain.astype(jnp.float32)

    def forward(carried, inputs):
        weight_row, series_row = inputs
        scaled = (weight_row[:, None] * loadings_wide).astype(jnp.bfloat16)
        information = lax.dot_general(loadings, scaled, (((0,), (0,)), ((), ())), preferred_element_type=jnp.float32)
        weighted = (weight_row * series_row.astype(jnp.float32)).astype(jnp.bfloat16)
        drive_terms = jnp.dot(weighted, loadings, preferred_element_type=jnp.float32)
        damped = (information * decay[None, :]).astype(jnp.bfloat16)
        transition = jnp.diag(decay) - jnp.dot(gain, damped, preferred_element_type=jnp.float32)
        offset = jnp.dot(gain_wide, drive_terms, precision=high)
        updated = jnp.dot(transition, carried, precision=high) + offset
        return (updated, updated)
    filtered = lax.scan(forward, jnp.zeros((K,), jnp.float32), (weights, series))[1]
    pulled = jnp.dot(filtered * decay[None, :], smoother.T, precision=high)
    final_day = (day_ids == DAYS - 1)[:, None]
    back_term = jnp.where(final_day, filtered, filtered - pulled)

    def backward(carried, term_row):
        updated = jnp.dot(smoother, carried, precision=high) + term_row
        return (updated, updated)
    smoothed = lax.scan(backward, jnp.zeros((K,), jnp.float32), back_term, reverse=True)[1]
    rounded = smoothed.astype(jnp.bfloat16)
    fitted = lax.dot_general(rounded, loadings, (((1,), (1,)), ((), ())), preferred_element_type=jnp.float32)
    scores = (active * (series.astype(jnp.float32) - fitted) * jnp.sqrt(precision)[None, :]).astype(jnp.bfloat16)
    return (smoothed, scores)
```

```python
import functools
import jax
import jax.numpy as jnp
from jax import lax
from jax.experimental import pallas as pl
from jax.experimental.pallas import tpu as pltpu
from jax.sharding import PartitionSpec as P

F32 = jnp.float32
BF16 = jnp.bfloat16
HIGH = lax.Precision.HIGHEST
VMEM = pltpu.MemorySpace.VMEM
SMEM = pltpu.MemorySpace.SMEM


def params(grid=True):
    semantics = {"dimension_semantics": ("arbitrary",)} if grid else {}
    return pltpu.CompilerParams(vmem_limit_bytes=48 << 20, **semantics)


def cost(flops, nbytes):
    return pl.CostEstimate(flops=flops, bytes_accessed=nbytes, transcendentals=0)


def whole(count):
    return [pl.BlockSpec(memory_space=VMEM)] * count


def exact(a, b):
    return jnp.dot(a, b, precision=HIGH, preferred_element_type=F32)


def partial_drive(index, series, loadings, precision, start, stop, off):
    days, own = series.shape
    factors = loadings.shape[1]

    def kernel(index_ref, series_ref, load_ref, prec_ref, start_ref, stop_ref, off_ref, out_ref):
        day = lax.broadcasted_iota(jnp.int32, (days, 1), 0)
        active = (
            (day >= start_ref[...]) & (day < stop_ref[...]) & (lax.rem(day, 7) != off_ref[...])
        )
        weights = jnp.where(active, prec_ref[...], 0.0)
        weighted = (weights * series_ref[...].astype(F32)).astype(BF16)
        out_ref[...] = jnp.dot(weighted, load_ref[...], preferred_element_type=F32)

    row = pl.BlockSpec((1, own), lambda i, s: (0, s[0]))
    return pl.pallas_call(
        kernel,
        grid_spec=pltpu.PrefetchScalarGridSpec(
            num_scalar_prefetch=1,
            grid=(1,),
            in_specs=[
                pl.BlockSpec((days, own), lambda i, s: (0, 0)),
                pl.BlockSpec((own, factors), lambda i, s: (s[0], 0)),
                row,
                row,
                row,
                row,
            ],
            out_specs=pl.BlockSpec((days, factors), lambda i, s: (0, 0)),
        ),
        out_shape=jax.ShapeDtypeStruct((days, factors), F32),
        compiler_params=params(),
        cost_estimate=cost(2 * days * own * factors, 1 << 20),
        name="partial_drive",
    )(index, series, loadings, precision, start, stop, off)


def transitions_of(first_day, day_count, loadings, precision, start, stop, off, decay, gain):
    providers, factors = loadings.shape
    chunk = min(4096, providers)
    steps = providers // chunk

    def kernel(
        day_ref, load_ref, prec_ref, start_ref, stop_ref, off_ref, row_ref, col_ref, gain_ref,
        step_ref, run_ref, acc,
    ):
        step = pl.program_id(0)

        @pl.when(step == 0)
        def _():
            acc[...] = jnp.zeros_like(acc)

        block = load_ref[...]
        scaled = (block.T.astype(F32) * prec_ref[...]).astype(BF16)
        for d in range(day_count):
            day = day_ref[0] + d
            active = (
                (start_ref[...] <= day) & (stop_ref[...] > day) & (off_ref[...] != lax.rem(day, 7))
            )
            mask = active.astype(F32).astype(BF16)
            acc[d] += jnp.dot(scaled * mask, block, preferred_element_type=F32)

        @pl.when(step == steps - 1)
        def _():
            shape = (factors, factors)
            diagonal = jnp.where(
                lax.broadcasted_iota(jnp.int32, shape, 0) == lax.broadcasted_iota(jnp.int32, shape, 1),
                row_ref[...],
                0.0,
            )
            for d in range(day_count):
                damped = (acc[d] * col_ref[...]).astype(BF16)
                pulled = lax.dot_general(
                    damped, gain_ref[...], (((1,), (1,)), ((), ())), preferred_element_type=F32
                )
                step_ref[d] = diagonal - pulled
            run_ref[0] = step_ref[0]
            for d in range(1, day_count):
                run_ref[d] = exact(run_ref[d - 1], step_ref[d])

    row = pl.BlockSpec((1, chunk), lambda i: (0, i))
    cube = pl.BlockSpec((day_count, factors, factors), lambda i: (0, 0, 0))
    shape = jax.ShapeDtypeStruct((day_count, factors, factors), F32)
    return pl.pallas_call(
        kernel,
        grid=(steps,),
        in_specs=[
            pl.BlockSpec(memory_space=SMEM),
            pl.BlockSpec((chunk, factors), lambda i: (i, 0)),
            row,
            row,
            row,
            row,
            pl.BlockSpec((1, factors), lambda i: (0, 0)),
            pl.BlockSpec((factors, 1), lambda i: (0, 0)),
            pl.BlockSpec((factors, factors), lambda i: (0, 0)),
        ],
        out_specs=[cube, cube],
        out_shape=[shape, shape],
        scratch_shapes=[pltpu.VMEM((day_count, factors, factors), F32)],
        compiler_params=params(),
        cost_estimate=cost(2 * day_count * providers * factors * factors, 10 << 20),
        name="transitions",
    )(
        first_day, loadings, precision, start, stop, off,
        decay.reshape(1, factors), decay.reshape(factors, 1), gain,
    )


def own_states(terms, steps, gain):
    parts, day_count, factors = terms.shape

    def kernel(terms_ref, step_ref, gain_ref, out_ref):
        drive = terms_ref[0]
        for p in range(1, parts):
            drive = drive + terms_ref[p]
        offsets = lax.dot_general(
            drive, gain_ref[...].astype(F32), (((1,), (1,)), ((), ())), precision=HIGH,
            preferred_element_type=F32,
        )
        state = offsets[0:1]
        out_ref[0:1] = state
        for d in range(1, day_count):
            state = exact(state, step_ref[d]) + offsets[d : d + 1]
            out_ref[d : d + 1] = state

    return pl.pallas_call(
        kernel,
        in_specs=whole(3),
        out_specs=pl.BlockSpec(memory_space=VMEM),
        out_shape=jax.ShapeDtypeStruct((day_count, factors), F32),
        compiler_params=params(False),
        cost_estimate=cost(20 * factors * factors * 8, 1 << 20),
        name="own_states",
    )(terms, steps, gain)


def combined(upper, mine, my_tail, other, other_tail):
    factors = mine.shape[0]

    def kernel(upper_ref, mine_ref, my_ref, other_ref, other_tail_ref, map_ref, tail_ref):
        def write(low, low_tail, high, high_tail):
            map_ref[...] = exact(low[...], high[...])
            tail_ref[...] = exact(low_tail[...], high[...]) + high_tail[...]

        @pl.when(upper_ref[0] == 1)
        def _():
            write(other_ref, other_tail_ref, mine_ref, my_ref)

        @pl.when(upper_ref[0] == 0)
        def _():
            write(mine_ref, my_ref, other_ref, other_tail_ref)

    return pl.pallas_call(
        kernel,
        in_specs=[pl.BlockSpec(memory_space=SMEM)] + whole(4),
        out_specs=whole(2),
        out_shape=[
            jax.ShapeDtypeStruct((factors, factors), F32),
            jax.ShapeDtypeStruct((1, factors), F32),
        ],
        compiler_params=params(False),
        cost_estimate=cost(12 * factors**3, 1 << 20),
        name="combined",
    )(upper, mine, my_tail, other, other_tail)


def advanced(state, matrix, tail):
    factors = matrix.shape[0]

    def kernel(state_ref, matrix_ref, tail_ref, out_ref):
        out_ref[...] = exact(state_ref[...], matrix_ref[...]) + tail_ref[...]

    return pl.pallas_call(
        kernel,
        in_specs=whole(3),
        out_specs=pl.BlockSpec(memory_space=VMEM),
        out_shape=jax.ShapeDtypeStruct((1, factors), F32),
        compiler_params=params(False),
        cost_estimate=cost(12 * factors**2, 1 << 18),
        name="advanced",
    )(state, matrix, tail)


def filtered_of(entering, uppers, levels, running, states):
    day_count, factors = states.shape
    count = len(levels)

    def kernel(upper_ref, enter_ref, *refs):
        out_ref = refs[-1]
        states_ref, run_ref = refs[-2], refs[-3]
        state = enter_ref[...]
        for level in reversed(range(count)):
            matrix_ref, tail_ref = refs[2 * level], refs[2 * level + 1]
            moved = exact(state, matrix_ref[...]) + tail_ref[...]
            state = jnp.where(upper_ref[level] == 1, moved, state)
        for d in range(day_count):
            out_ref[d : d + 1] = exact(state, run_ref[d]) + states_ref[d : d + 1]

    flat = [a for level in levels for a in level]
    return pl.pallas_call(
        kernel,
        in_specs=[pl.BlockSpec(memory_space=SMEM)] + whole(len(flat) + 3),
        out_specs=pl.BlockSpec(memory_space=VMEM),
        out_shape=jax.ShapeDtypeStruct((day_count, factors), F32),
        compiler_params=params(False),
        cost_estimate=cost(80 * factors**2, 2 << 20),
        name="filtered",
    )(uppers, entering, *flat, running, states)


POWERS = 5


def smoother_powers(smoother):
    factors = smoother.shape[0]

    def kernel(in_ref, out_ref):
        out_ref[0] = in_ref[...].T
        for p in range(1, POWERS):
            out_ref[p] = exact(out_ref[p - 1], out_ref[p - 1])

    return pl.pallas_call(
        kernel,
        in_specs=whole(1),
        out_specs=pl.BlockSpec(memory_space=VMEM),
        out_shape=jax.ShapeDtypeStruct((POWERS, factors, factors), F32),
        compiler_params=params(False),
        cost_estimate=cost(48 * factors**3, 2 << 20),
        name="smoother_powers",
    )(smoother)


def finish(index, day_count, filtered, powers, decay, series, loadings, precision, start, stop, off):
    days, own = series.shape
    factors = loadings.shape[1]
    stride = 2 ** (POWERS - 1)

    def kernel(
        index_ref, filt_ref, pow_ref, decay_ref, series_ref, load_ref, prec_ref, start_ref,
        stop_ref, off_ref, smooth_ref, score_ref, work,
    ):
        filtered = filt_ref[...]
        day = lax.broadcasted_iota(jnp.int32, (days, 1), 0)
        pulled = exact(filtered * decay_ref[...], pow_ref[0])
        total = jnp.where(day == days - 1, filtered, filtered - pulled)
        for p in range(POWERS - 1):
            reach = 2**p
            later = jnp.concatenate([total[reach:], jnp.zeros((reach, factors), F32)], 0)
            total = total + exact(later, pow_ref[p])
        blocks = days // stride
        block = total[(blocks - 1) * stride :]
        work[(blocks - 1) * stride :, :] = block
        for b in reversed(range(blocks - 1)):
            block = total[b * stride : (b + 1) * stride] + exact(block, pow_ref[POWERS - 1])
            work[b * stride : (b + 1) * stride, :] = block
        mine = index_ref[0] * day_count
        for d in range(day_count):
            smooth_ref[d : d + 1, :] = work[pl.ds(mine + d, 1), :]
        fitted = lax.dot_general(
            work[...].astype(BF16), load_ref[...], (((1,), (1,)), ((), ())),
            preferred_element_type=F32,
        )
        active = (
            (day >= start_ref[...]) & (day < stop_ref[...]) & (lax.rem(day, 7) != off_ref[...])
        )
        residual = (series_ref[...].astype(F32) - fitted) * jnp.sqrt(prec_ref[...])
        score_ref[...] = jnp.where(active, residual, 0.0).astype(BF16)

    row = pl.BlockSpec((1, own), lambda i, s: (0, s[0]))
    return pl.pallas_call(
        kernel,
        grid_spec=pltpu.PrefetchScalarGridSpec(
            num_scalar_prefetch=1,
            grid=(1,),
            in_specs=[
                pl.BlockSpec((days, factors), lambda i, s: (0, 0)),
                pl.BlockSpec((POWERS, factors, factors), lambda i, s: (0, 0, 0)),
                pl.BlockSpec((1, factors), lambda i, s: (0, 0)),
                pl.BlockSpec((days, own), lambda i, s: (0, 0)),
                pl.BlockSpec((own, factors), lambda i, s: (s[0], 0)),
                row,
                row,
                row,
                row,
            ],
            out_specs=[
                pl.BlockSpec((day_count, factors), lambda i, s: (0, 0)),
                pl.BlockSpec((days, own), lambda i, s: (0, 0)),
            ],
            scratch_shapes=[pltpu.VMEM((days, factors), F32)],
        ),
        out_shape=[
            jax.ShapeDtypeStruct((day_count, factors), F32),
            jax.ShapeDtypeStruct((days, own), BF16),
        ],
        compiler_params=params(),
        cost_estimate=cost(2 * days * own * factors, 2 << 20),
        name="finish",
    )(index, filtered, powers, decay.reshape(1, factors), series, loadings, precision, start, stop, off)


def local(series, loadings, precision, start_day, stop_day, off_day, decay, gain, smoother):
    devices = lax.axis_size("tm")
    place = lax.axis_index("tm").astype(jnp.int32)
    index = place[None]
    days = series.shape[0]
    day_count = days // devices
    factors = loadings.shape[1]
    precision, start, stop, off = (
        a.reshape(1, -1) for a in (precision, start_day, stop_day, off_day)
    )

    partial = partial_drive(index, series, loadings, precision, start, stop, off)
    terms = lax.all_to_all(
        partial.reshape(devices, day_count, factors), "tm", 0, 0, tiled=True
    )
    steps, running = transitions_of(
        index * day_count, day_count, loadings, precision, start, stop, off, decay, gain
    )
    states = own_states(terms, steps, gain)
    powers = smoother_powers(smoother)

    group = min(4, devices)
    matrix, tail = running[day_count - 1], states[day_count - 1 :]
    levels, uppers = [], []
    reach = 1
    while reach < group:
        pairs = [(i, i ^ reach) for i in range(devices)]
        other = lax.ppermute(matrix, "tm", pairs)
        other_tail = lax.ppermute(tail, "tm", pairs)
        upper = (place // reach) % 2
        levels.append((other, other_tail))
        uppers.append(upper)
        matrix, tail = combined(upper[None], matrix, tail, other, other_tail)
        reach *= 2

    state = jnp.zeros((1, factors), F32)
    for g in range(devices // group - 1):
        moved = tail if g == 0 else advanced(state, matrix, tail)
        pairs = [(g * group + j, (g + 1) * group + j) for j in range(group)]
        state = state + lax.ppermute(moved, "tm", pairs)

    filtered = filtered_of(state, jnp.stack(uppers), levels, running, states)
    everyone = lax.all_to_all(
        jnp.broadcast_to(filtered[None], (devices, day_count, factors)), "tm", 0, 0, tiled=True
    ).reshape(days, factors)
    return tuple(
        finish(
            index, day_count, everyone, powers, decay, series, loadings, precision, start, stop, off
        )
    )


def solution(mesh):
    in_specs = (
        P(None, ("spec", "tm")),
        P("spec", None),
        P("spec"),
        P("spec"),
        P("spec"),
        P("spec"),
        P(),
        P(),
        P(),
    )
    out_specs = (P("tm", "spec"), P(None, ("spec", "tm")))
    return jax.shard_map(local, mesh=mesh, in_specs=in_specs, out_specs=out_specs, check_vma=False)
```

```python
import jax
import jax.numpy as jnp
from jax import lax
from jax.experimental import pallas as pl
from jax.experimental.pallas import tpu as pltpu
from jax.sharding import PartitionSpec as P

F32 = jnp.float32
BF16 = jnp.bfloat16
VMEM = pltpu.MemorySpace.VMEM
SMEM = pltpu.MemorySpace.SMEM
HBM = pltpu.MemorySpace.HBM
POWERS = 5


def params(**more):
    return pltpu.CompilerParams(vmem_limit_bytes=48 << 20, **more)


def cost(flops, nbytes):
    return pl.CostEstimate(flops=flops, bytes_accessed=nbytes, transcendentals=0)


def vmem(count):
    return [pl.BlockSpec(memory_space=VMEM)] * count


def hbm(count):
    return [pl.BlockSpec(memory_space=HBM)] * count


def smem():
    return pl.BlockSpec(memory_space=SMEM)


def shape(*dims, dtype=F32):
    return jax.ShapeDtypeStruct(dims, dtype)


def mul(a, b):
    return jnp.dot(a, b, preferred_element_type=F32)


def split(a):
    high = a.astype(BF16)
    return high, (a - high.astype(F32)).astype(BF16)


def product(a, b):
    high, low = split(a)
    return mul(high, b[0]) + mul(low, b[0]) + mul(high, b[1])


def eye(factors):
    dims = (factors, factors)
    return lax.broadcasted_iota(jnp.int32, dims, 0) == lax.broadcasted_iota(jnp.int32, dims, 1)


def activity(day, start, stop, off):
    return (day >= start) & (day < stop) & (lax.rem(day, 7) != off)


def partial_drive(index, series, loadings, tables):
    days, own = series.shape
    factors = loadings.shape[1]

    def kernel(
        index_ref, series_hbm, load_hbm, prec_hbm, start_hbm, stop_hbm, off_hbm, out_ref,
        series_ref, load_ref, prec_ref, start_ref, stop_ref, off_ref, sems,
    ):
        first = pl.multiple_of(index_ref[0] * own, own)
        mine = pl.ds(first, own)
        copies = [
            pltpu.make_async_copy(source, target, sems.at[n])
            for n, (source, target) in enumerate(
                [
                    (prec_hbm.at[:, mine], prec_ref),
                    (start_hbm.at[:, mine], start_ref),
                    (stop_hbm.at[:, mine], stop_ref),
                    (off_hbm.at[:, mine], off_ref),
                    (series_hbm, series_ref),
                    (load_hbm.at[mine], load_ref),
                ]
            )
        ]
        for copy in copies:
            copy.start()
        day = lax.broadcasted_iota(jnp.int32, (days, 1), 0)
        for copy in copies[:5]:
            copy.wait()
        active = activity(day, start_ref[...], stop_ref[...], off_ref[...])
        weights = jnp.where(active, prec_ref[...], 0.0)
        weighted = (weights * series_ref[...].astype(F32)).astype(BF16)
        copies[5].wait()
        out_ref[...] = mul(weighted, load_ref[...])

    return pl.pallas_call(
        kernel,
        in_specs=[smem()] + hbm(6),
        out_specs=pl.BlockSpec(memory_space=VMEM),
        out_shape=shape(days, factors),
        scratch_shapes=[
            pltpu.VMEM((days, own), BF16),
            pltpu.VMEM((own, factors), BF16),
            pltpu.VMEM((1, own), F32),
            pltpu.VMEM((1, own), jnp.int32),
            pltpu.VMEM((1, own), jnp.int32),
            pltpu.VMEM((1, own), jnp.int32),
            pltpu.SemaphoreType.DMA((6,)),
        ],
        compiler_params=params(),
        cost_estimate=cost(2 * days * own * factors, 1 << 20),
        name="partial_drive",
    )(index, series, loadings, *tables)


def transitions_of(first_day, day_count, loadings, tables, decay, gain):
    providers, factors = loadings.shape
    chunk = min(4096, providers)
    steps = providers // chunk

    def kernel(
        day_ref, load_ref, prec_hbm, start_hbm, stop_hbm, off_hbm, decay_hbm, gain_hbm,
        step_ref, run_ref, rest_ref, diag_ref,
        acc, prec_ref, start_ref, stop_ref, off_ref, decay_ref, gain_ref, sems,
    ):
        step = pl.program_id(0)

        @pl.when(step == 0)
        def _():
            copies = [
                pltpu.make_async_copy(source, target, sems.at[n])
                for n, (source, target) in enumerate(
                    [
                        (prec_hbm, prec_ref),
                        (start_hbm, start_ref),
                        (stop_hbm, stop_ref),
                        (off_hbm, off_ref),
                        (decay_hbm, decay_ref),
                        (gain_hbm, gain_ref),
                    ]
                )
            ]
            for copy in copies:
                copy.start()
            acc[...] = jnp.zeros_like(acc)
            for copy in copies:
                copy.wait()

        place = pl.ds(pl.multiple_of(step * chunk, chunk), chunk)
        block = load_ref[...]
        scaled = (block.T.astype(F32) * prec_ref[:, place]).astype(BF16)
        for d in range(day_count):
            active = activity(
                day_ref[0] + d, start_ref[:, place], stop_ref[:, place], off_ref[:, place]
            )
            mask = active.astype(F32).astype(BF16)
            acc[d] += mul(scaled * mask, block)

        @pl.when(step == steps - 1)
        def _():
            same = eye(factors)
            diagonal = jnp.where(same, decay_ref[...], 0.0)
            column = jnp.sum(diagonal, axis=1, keepdims=True)
            for d in range(day_count):
                damped = (acc[d] * column).astype(BF16)
                pulled = lax.dot_general(
                    damped, gain_ref[...], (((1,), (1,)), ((), ())), preferred_element_type=F32
                )
                step_ref[d] = diagonal - pulled
            run_ref[0] = step_ref[0]
            for d in range(1, day_count):
                run_ref[d] = product(run_ref[d - 1], split(step_ref[d]))
            last = run_ref[day_count - 1]
            rest_ref[...] = jnp.where(same, 0.0, last).astype(BF16)
            diag_ref[...] = jnp.sum(jnp.where(same, last, 0.0), axis=0, keepdims=True)

    cube = pl.BlockSpec((day_count, factors, factors), lambda i: (0, 0, 0))
    return pl.pallas_call(
        kernel,
        grid=(steps,),
        in_specs=[smem(), pl.BlockSpec((chunk, factors), lambda i: (i, 0))] + hbm(6),
        out_specs=[
            cube,
            cube,
            pl.BlockSpec((factors, factors), lambda i: (0, 0)),
            pl.BlockSpec((1, factors), lambda i: (0, 0)),
        ],
        out_shape=[
            shape(day_count, factors, factors),
            shape(day_count, factors, factors),
            shape(factors, factors, dtype=BF16),
            shape(1, factors),
        ],
        scratch_shapes=[
            pltpu.VMEM((day_count, factors, factors), F32),
            pltpu.VMEM((1, providers), F32),
            pltpu.VMEM((1, providers), jnp.int32),
            pltpu.VMEM((1, providers), jnp.int32),
            pltpu.VMEM((1, providers), jnp.int32),
            pltpu.VMEM((1, factors), F32),
            pltpu.VMEM((factors, factors), BF16),
            pltpu.SemaphoreType.DMA((6,)),
        ],
        compiler_params=params(dimension_semantics=("arbitrary",)),
        cost_estimate=cost(2 * day_count * providers * factors * factors, 10 << 20),
        name="transitions",
    )(first_day, loadings, *tables, decay, gain)


def own_states(terms, steps, gain, diag):
    parts, day_count, factors = terms.shape

    def kernel(terms_ref, step_ref, gain_ref, diag_ref, out_ref, packet_ref):
        drive = terms_ref[0]
        for p in range(1, parts):
            drive = drive + terms_ref[p]
        high, low = split(drive)
        weights = gain_ref[...]
        dims = (((1,), (1,)), ((), ()))
        rest = (drive - high.astype(F32) - low.astype(F32)).astype(BF16)
        offsets = sum(
            lax.dot_general(part, weights, dims, preferred_element_type=F32)
            for part in (high, low, rest)
        )
        state = offsets[0:1]
        out_ref[0:1] = state
        for d in range(1, day_count):
            state = product(state, split(step_ref[d])) + offsets[d : d + 1]
            out_ref[d : d + 1] = state
        packet_ref[0:1] = state
        packet_ref[1:2] = diag_ref[...]

    return pl.pallas_call(
        kernel,
        in_specs=vmem(4),
        out_specs=vmem(2),
        out_shape=[shape(day_count, factors), shape(2, factors)],
        compiler_params=params(),
        cost_estimate=cost(20 * factors * factors * 8, 1 << 20),
        name="own_states",
    )(terms, steps, gain, diag)


def rebuilt(rest, diag, same):
    return rest.astype(F32) + jnp.where(same, diag, 0.0)


def combined(upper, matrix, packet, other_rest, other_packet):
    factors = matrix.shape[0]

    def kernel(upper_ref, mine_ref, packet_ref, rest_ref, other_ref, map_ref, part_ref, next_ref):
        same = eye(factors)
        other = rebuilt(rest_ref[...], other_ref[1:2], same)

        def write(low, low_tail, high, high_tail):
            high = split(high)
            total = product(low, high)
            map_ref[...] = total
            part_ref[...] = jnp.where(same, 0.0, total).astype(BF16)
            next_ref[0:1] = product(low_tail, high) + high_tail
            next_ref[1:2] = jnp.sum(jnp.where(same, total, 0.0), axis=0, keepdims=True)

        @pl.when(upper_ref[0] == 1)
        def _():
            write(other, other_ref[0:1], mine_ref[...], packet_ref[0:1])

        @pl.when(upper_ref[0] == 0)
        def _():
            write(mine_ref[...], packet_ref[0:1], other, other_ref[0:1])

    return pl.pallas_call(
        kernel,
        in_specs=[smem()] + vmem(4),
        out_specs=vmem(3),
        out_shape=[
            shape(factors, factors),
            shape(factors, factors, dtype=BF16),
            shape(2, factors),
        ],
        compiler_params=params(),
        cost_estimate=cost(12 * factors**3, 1 << 20),
        name="combined",
    )(upper, matrix, packet, other_rest, other_packet)


def advanced(state, matrix, packet):
    factors = matrix.shape[0]

    def kernel(state_ref, matrix_ref, packet_ref, out_ref):
        out_ref[...] = product(state_ref[...], split(matrix_ref[...])) + packet_ref[0:1]

    return pl.pallas_call(
        kernel,
        in_specs=vmem(3),
        out_specs=pl.BlockSpec(memory_space=VMEM),
        out_shape=shape(1, factors),
        compiler_params=params(),
        cost_estimate=cost(12 * factors**2, 1 << 18),
        name="advanced",
    )(state, matrix, packet)


def prefixed(uppers, levels, running, states):
    day_count, factors = states.shape
    count = len(levels)

    def kernel(*refs):
        upper_refs = refs[:count]
        parts = refs[count : 3 * count]
        run_ref, states_ref, high_ref, low_ref, add_ref, work, tail = refs[3 * count :]
        same = eye(factors)
        work[...] = jnp.where(same, 1.0, 0.0)
        tail[...] = jnp.zeros_like(tail)
        for level in reversed(range(count)):

            @pl.when(upper_refs[level][0] == 1)
            def _():
                packet = parts[2 * level + 1]
                step = split(rebuilt(parts[2 * level][...], packet[1:2], same))
                work[...] = product(work[...], step)
                tail[...] = product(tail[...], step) + packet[0:1]

        for d in range(day_count):
            step = split(run_ref[d])
            place = slice(d * factors, (d + 1) * factors)
            high, low = split(product(work[...], step))
            high_ref[:, place] = high
            low_ref[:, place] = low
            add_ref[:, place] = product(tail[...], step) + states_ref[d : d + 1]

    wide = day_count * factors
    return pl.pallas_call(
        kernel,
        in_specs=[smem()] * count + vmem(2 * count + 2),
        out_specs=vmem(3),
        out_shape=[
            shape(factors, wide, dtype=BF16),
            shape(factors, wide, dtype=BF16),
            shape(1, wide),
        ],
        scratch_shapes=[pltpu.VMEM((factors, factors), F32), pltpu.VMEM((1, factors), F32)],
        compiler_params=params(),
        cost_estimate=cost(36 * factors**3, 3 << 20),
        name="prefixed",
    )(*uppers, *[a for level in levels for a in level], running, states)


def filtered_of(state, arrived, high, low, add):
    factors, wide = high.shape
    day_count = wide // factors

    def kernel(state_ref, arrived_ref, high_ref, low_ref, add_ref, out_ref):
        entering = state_ref[...] + arrived_ref[...]
        row = product(entering, (high_ref[...], low_ref[...])) + add_ref[...]
        for d in range(day_count):
            out_ref[d : d + 1] = row[:, d * factors : (d + 1) * factors]

    return pl.pallas_call(
        kernel,
        in_specs=vmem(5),
        out_specs=pl.BlockSpec(memory_space=VMEM),
        out_shape=shape(day_count, factors),
        compiler_params=params(),
        cost_estimate=cost(6 * factors * wide, 1 << 20),
        name="filtered",
    )(state, arrived, high, low, add)


def smoother_powers(smoother):
    factors = smoother.shape[0]

    def kernel(in_ref, high_ref, low_ref):
        power = in_ref[...].T
        for p in range(POWERS):
            parts = split(power)
            high_ref[p], low_ref[p] = parts
            if p < POWERS - 1:
                power = product(power, parts)

    return pl.pallas_call(
        kernel,
        in_specs=vmem(1),
        out_specs=vmem(2),
        out_shape=[shape(POWERS, factors, factors, dtype=BF16)] * 2,
        compiler_params=params(),
        cost_estimate=cost(24 * factors**3, 2 << 20),
        name="smoother_powers",
    )(smoother)


def finish(index, day_count, pieces, powers, decay, series, loadings, tables):
    days, own = series.shape
    factors = loadings.shape[1]
    stride = 2 ** (POWERS - 1)
    blocks = days // stride
    count = len(pieces)

    def kernel(index_ref, *refs):
        piece_refs = refs[:count]
        (
            high_ref, low_ref, decay_ref, series_hbm, load_hbm, prec_hbm, start_hbm, stop_hbm,
            off_hbm, smooth_ref, score_ref, filt, work, series_ref, load_ref, prec_ref, start_ref,
            stop_ref, off_ref, sems,
        ) = refs[count:]
        me = index_ref[0]
        mine = pl.ds(pl.multiple_of(me * own, own), own)
        copies = [
            pltpu.make_async_copy(source, target, sems.at[n])
            for n, (source, target) in enumerate(
                [
                    (load_hbm.at[mine], load_ref),
                    (series_hbm, series_ref),
                    (prec_hbm.at[:, mine], prec_ref),
                    (start_hbm.at[:, mine], start_ref),
                    (stop_hbm.at[:, mine], stop_ref),
                    (off_hbm.at[:, mine], off_ref),
                ]
            )
        ]
        for copy in copies:
            copy.start()
        block = 0
        for piece in piece_refs:
            for b in range(piece.shape[0]):
                first = (me ^ block) * day_count
                for d in range(day_count):
                    filt[pl.ds(first + d, 1), :] = piece[b, d : d + 1]
                block += 1
        filtered = filt[...]
        carried = filtered * decay_ref[...]
        carried = jnp.concatenate([jnp.zeros((1, factors), F32), carried[:-1]], 0)
        total = filtered - carried
        for p in range(POWERS - 1):
            reach = 2**p
            later = jnp.concatenate([total[reach:], jnp.zeros((reach, factors), F32)], 0)
            total = total + product(later, (high_ref[p], low_ref[p]))
        far = (high_ref[POWERS - 1], low_ref[POWERS - 1])
        row = total[(blocks - 1) * stride :]
        work[(blocks - 1) * stride :, :] = row
        for b in reversed(range(blocks - 1)):
            row = total[b * stride : (b + 1) * stride] + product(row, far)
            work[b * stride : (b + 1) * stride, :] = row
        work[...] += carried
        for d in range(day_count):
            smooth_ref[d : d + 1, :] = work[pl.ds(me * day_count + d, 1), :]
        for copy in copies:
            copy.wait()
        fitted = lax.dot_general(
            work[...].astype(BF16), load_ref[...], (((1,), (1,)), ((), ())),
            preferred_element_type=F32,
        )
        day = lax.broadcasted_iota(jnp.int32, (days, 1), 0)
        active = activity(day, start_ref[...], stop_ref[...], off_ref[...])
        residual = (series_ref[...].astype(F32) - fitted) * jnp.sqrt(prec_ref[...])
        score_ref[...] = jnp.where(active, residual, 0.0).astype(BF16)

    return pl.pallas_call(
        kernel,
        in_specs=[smem()] + vmem(count + 3) + hbm(6),
        out_specs=vmem(2),
        out_shape=[shape(day_count, factors), shape(days, own, dtype=BF16)],
        scratch_shapes=[
            pltpu.VMEM((days, factors), F32),
            pltpu.VMEM((days, factors), F32),
            pltpu.VMEM((days, own), BF16),
            pltpu.VMEM((own, factors), BF16),
            pltpu.VMEM((1, own), F32),
            pltpu.VMEM((1, own), jnp.int32),
            pltpu.VMEM((1, own), jnp.int32),
            pltpu.VMEM((1, own), jnp.int32),
            pltpu.SemaphoreType.DMA((6,)),
        ],
        compiler_params=params(),
        cost_estimate=cost(2 * days * own * factors, 2 << 20),
        name="finish",
    )(index, *pieces, *powers, decay, series, loadings, *tables)


def local(series, loadings, precision, start_day, stop_day, off_day, decay, gain, smoother):
    devices = lax.axis_size("tm")
    place = lax.axis_index("tm").astype(jnp.int32)
    index = place[None]
    days = series.shape[0]
    day_count = days // devices
    factors = loadings.shape[1]
    tables = [a.reshape(1, -1) for a in (precision, start_day, stop_day, off_day)]
    decay = decay.reshape(1, factors)

    def swapped(array, distance):
        return lax.ppermute(array, "tm", [(i, i ^ distance) for i in range(devices)])

    partial = partial_drive(index, series, loadings, tables)
    partial, first_day = lax.optimization_barrier((partial, index * day_count))
    terms = lax.all_to_all(
        partial.reshape(devices, day_count, factors), "tm", 0, 0, tiled=True
    )
    steps, running, rest, diag = transitions_of(first_day, day_count, loadings, tables, decay, gain)
    states, packet = own_states(terms, steps, gain, diag)

    group = min(4, devices)
    matrix = running[day_count - 1]
    levels, uppers = [], []
    reach = 1
    while reach < group:
        other_rest = swapped(rest, reach)
        other_packet = swapped(packet, reach)
        upper = jnp.where((place & reach) != 0, 1, 0).astype(jnp.int32)[None]
        levels.append((other_rest, other_packet))
        uppers.append(upper)
        matrix, rest, packet = combined(upper, matrix, packet, other_rest, other_packet)
        reach *= 2

    ahead = prefixed(uppers, levels, running, states)
    state = jnp.zeros((1, factors), F32)
    arrived = jnp.zeros((1, factors), F32)
    for g in range(devices // group - 1):
        state = state + arrived
        moved = packet[0:1] if g == 0 else advanced(state, matrix, packet)
        pairs = [(g * group + j, (g + 1) * group + j) for j in range(group)]
        arrived = lax.ppermute(moved, "tm", pairs)

    pieces = filtered_of(state, arrived, *ahead)[None]
    reach = 1
    while reach * 4 < devices:
        pieces = jnp.concatenate([pieces, swapped(pieces, reach)], 0)
        reach *= 2
    pieces = [pieces] + [
        swapped(pieces, reach * n) for n in range(1, devices // reach)
    ]
    powers = smoother_powers(smoother)
    return tuple(finish(index, day_count, pieces, powers, decay, series, loadings, tables))


def solution(mesh):
    in_specs = (
        P(None, ("spec", "tm")),
        P("spec", None),
        P("spec"),
        P("spec"),
        P("spec"),
        P("spec"),
        P(),
        P(),
        P(),
    )
    out_specs = (P("tm", "spec"), P(None, ("spec", "tm")))
    return jax.shard_map(local, mesh=mesh, in_specs=in_specs, out_specs=out_specs, check_vma=False)
```

```python
import jax
import jax.numpy as jnp
from jax import lax
from jax.experimental import pallas as pl
from jax.experimental.pallas import tpu as pltpu
from jax.sharding import PartitionSpec as P

F32 = jnp.float32
BF16 = jnp.bfloat16
VMEM = pltpu.MemorySpace.VMEM
SMEM = pltpu.MemorySpace.SMEM
HBM = pltpu.MemorySpace.HBM
POWERS = 5


def params(mebibytes=48, **more):
    return pltpu.CompilerParams(vmem_limit_bytes=mebibytes << 20, **more)


def cost(flops, nbytes):
    return pl.CostEstimate(flops=flops, bytes_accessed=nbytes, transcendentals=0)


def vmem(count):
    return [pl.BlockSpec(memory_space=VMEM)] * count


def hbm(count):
    return [pl.BlockSpec(memory_space=HBM)] * count


def smem():
    return pl.BlockSpec(memory_space=SMEM)


def shape(*dims, dtype=F32):
    return jax.ShapeDtypeStruct(dims, dtype)


def mul(a, b):
    return jnp.dot(a, b, preferred_element_type=F32)


def split(a):
    high = a.astype(BF16)
    return high, (a - high.astype(F32)).astype(BF16)


def product(a, b):
    high, low = split(a)
    return mul(high, b[0]) + mul(low, b[0]) + mul(high, b[1])


def eye(factors):
    dims = (factors, factors)
    return lax.broadcasted_iota(jnp.int32, dims, 0) == lax.broadcasted_iota(jnp.int32, dims, 1)


def activity(day, start, stop, off):
    return (day >= start) & (day < stop) & (lax.rem(day, 7) != off)


def partial_drive(index, devices, series, loadings, tables):
    days, own = series.shape
    day_count = days // devices
    factors = loadings.shape[1]

    def kernel(
        index_ref, series_hbm, load_hbm, prec_hbm, start_hbm, stop_hbm, off_hbm, out_ref,
        series_ref, load_ref, prec_ref, start_ref, stop_ref, off_ref, sems,
    ):
        first = pl.multiple_of(index_ref[0] * own, own)
        mine = pl.ds(first, own)
        copies = [
            pltpu.make_async_copy(source, target, sems.at[n])
            for n, (source, target) in enumerate(
                [
                    (prec_hbm.at[:, mine], prec_ref),
                    (start_hbm.at[:, mine], start_ref),
                    (stop_hbm.at[:, mine], stop_ref),
                    (off_hbm.at[:, mine], off_ref),
                    (series_hbm, series_ref),
                    (load_hbm.at[mine], load_ref),
                ]
            )
        ]
        for copy in copies:
            copy.start()
        day = lax.broadcasted_iota(jnp.int32, (days, 1), 0)
        for copy in copies[:5]:
            copy.wait()
        active = activity(day, start_ref[...], stop_ref[...], off_ref[...])
        weights = jnp.where(active, prec_ref[...], 0.0)
        weighted = (weights * series_ref[...].astype(F32)).astype(BF16)
        copies[5].wait()
        drive = mul(weighted, load_ref[...])
        for p in range(devices):
            out_ref[p] = drive[p * day_count : (p + 1) * day_count]

    return pl.pallas_call(
        kernel,
        in_specs=[smem()] + hbm(6),
        out_specs=pl.BlockSpec(memory_space=VMEM),
        out_shape=shape(devices, day_count, factors),
        scratch_shapes=[
            pltpu.VMEM((days, own), BF16),
            pltpu.VMEM((own, factors), BF16),
            pltpu.VMEM((1, own), F32),
            pltpu.VMEM((1, own), jnp.int32),
            pltpu.VMEM((1, own), jnp.int32),
            pltpu.VMEM((1, own), jnp.int32),
            pltpu.SemaphoreType.DMA((6,)),
        ],
        compiler_params=params(63),
        cost_estimate=cost(2 * days * own * factors, 1 << 20),
        name="partial_drive",
    )(index, series, loadings, *tables)


def transitions_of(first_day, day_count, loadings, tables, decay, gain):
    providers, factors = loadings.shape
    chunk = min(4096, providers)
    steps = providers // chunk

    def kernel(
        day_ref, load_ref, prec_hbm, start_hbm, stop_hbm, off_hbm, decay_hbm, gain_hbm,
        step_ref, run_ref, last_ref, rest_ref, diag_ref,
        acc, prec_ref, start_ref, stop_ref, off_ref, decay_ref, gain_ref, sems,
    ):
        step = pl.program_id(0)

        @pl.when(step == 0)
        def _():
            copies = [
                pltpu.make_async_copy(source, target, sems.at[n])
                for n, (source, target) in enumerate(
                    [
                        (prec_hbm, prec_ref),
                        (start_hbm, start_ref),
                        (stop_hbm, stop_ref),
                        (off_hbm, off_ref),
                        (decay_hbm, decay_ref),
                        (gain_hbm, gain_ref),
                    ]
                )
            ]
            for copy in copies:
                copy.start()
            acc[...] = jnp.zeros_like(acc)
            for copy in copies:
                copy.wait()

        place = pl.ds(pl.multiple_of(step * chunk, chunk), chunk)
        block = load_ref[...]
        scaled = (block.T.astype(F32) * prec_ref[:, place]).astype(BF16)
        for d in range(day_count):
            active = activity(
                day_ref[0] + d, start_ref[:, place], stop_ref[:, place], off_ref[:, place]
            )
            mask = active.astype(F32).astype(BF16)
            acc[d] += mul(scaled * mask, block)

        @pl.when(step == steps - 1)
        def _():
            same = eye(factors)
            diagonal = jnp.where(same, decay_ref[...], 0.0)
            column = jnp.sum(diagonal, axis=1, keepdims=True)
            for d in range(day_count):
                damped = (acc[d] * column).astype(BF16)
                pulled = lax.dot_general(
                    damped, gain_ref[...], (((1,), (1,)), ((), ())), preferred_element_type=F32
                )
                step_ref[d] = diagonal - pulled
            running = step_ref[0]
            for d in range(1, day_count):
                run_ref[d - 1] = running
                running = product(running, split(step_ref[d]))
            last = running
            last_ref[...] = last
            rest_ref[...] = jnp.where(same, 0.0, last).astype(BF16)
            diag_ref[...] = jnp.sum(jnp.where(same, last, 0.0), axis=0, keepdims=True)

    cube = pl.BlockSpec((day_count, factors, factors), lambda i: (0, 0, 0))
    return pl.pallas_call(
        kernel,
        grid=(steps,),
        in_specs=[smem(), pl.BlockSpec((chunk, factors), lambda i: (i, 0))] + hbm(6),
        out_specs=[
            cube,
            pl.BlockSpec((day_count - 1, factors, factors), lambda i: (0, 0, 0)),
            pl.BlockSpec((factors, factors), lambda i: (0, 0)),
            pl.BlockSpec((factors, factors), lambda i: (0, 0)),
            pl.BlockSpec((1, factors), lambda i: (0, 0)),
        ],
        out_shape=[
            shape(day_count, factors, factors),
            shape(day_count - 1, factors, factors),
            shape(factors, factors),
            shape(factors, factors, dtype=BF16),
            shape(1, factors),
        ],
        scratch_shapes=[
            pltpu.VMEM((day_count, factors, factors), F32),
            pltpu.VMEM((1, providers), F32),
            pltpu.VMEM((1, providers), jnp.int32),
            pltpu.VMEM((1, providers), jnp.int32),
            pltpu.VMEM((1, providers), jnp.int32),
            pltpu.VMEM((1, factors), F32),
            pltpu.VMEM((factors, factors), BF16),
            pltpu.SemaphoreType.DMA((6,)),
        ],
        compiler_params=params(48, dimension_semantics=("arbitrary",)),
        cost_estimate=cost(2 * day_count * providers * factors * factors, 10 << 20),
        name="transitions",
    )(first_day, loadings, *tables, decay, gain)


def own_states(terms, steps, gain, diag):
    parts, day_count, factors = terms.shape

    def kernel(terms_ref, step_ref, gain_ref, diag_ref, out_ref, packet_ref):
        drive = terms_ref[0]
        for p in range(1, parts):
            drive = drive + terms_ref[p]
        high, low = split(drive)
        weights = gain_ref[...]
        dims = (((1,), (1,)), ((), ()))
        rest = (drive - high.astype(F32) - low.astype(F32)).astype(BF16)
        offsets = sum(
            lax.dot_general(part, weights, dims, preferred_element_type=F32)
            for part in (high, low, rest)
        )
        state = offsets[0:1]
        out_ref[0:1] = state
        for d in range(1, day_count):
            state = product(state, split(step_ref[d])) + offsets[d : d + 1]
            out_ref[d : d + 1] = state
        packet_ref[0:1] = state
        packet_ref[1:2] = diag_ref[...]

    return pl.pallas_call(
        kernel,
        in_specs=vmem(4),
        out_specs=vmem(2),
        out_shape=[shape(day_count, factors), shape(2, factors)],
        compiler_params=params(),
        cost_estimate=cost(20 * factors * factors * 8, 1 << 20),
        name="own_states",
    )(terms, steps, gain, diag)


def rebuilt(rest, diag, same):
    return rest.astype(F32) + jnp.where(same, diag, 0.0)


PACKED = 16


def unpacked(packed_ref, same):
    factors = packed_ref.shape[1]
    rows = packed_ref[factors:].astype(F32)
    matrix = rebuilt(packed_ref[:factors], rows[2:3] + rows[3:4], same)
    return matrix, rows[0:1] + rows[1:2]


def combine_into(low, low_tail, high, high_tail, same, map_ref, tail_ref, packed_ref):
    factors = low.shape[0]
    high = split(high)
    total = None if map_ref is None else product(low, high)
    tail = product(low_tail, high) + high_tail
    if map_ref is not None:
        map_ref[...] = total
    tail_ref[...] = tail
    if packed_ref is not None:
        packed_ref[:factors] = jnp.where(same, 0.0, total).astype(BF16)
        diag = jnp.sum(jnp.where(same, total, 0.0), axis=0, keepdims=True)
        rows = [*split(tail), *split(diag), jnp.zeros((PACKED - 4, factors), BF16)]
        packed_ref[factors:] = jnp.concatenate(rows, 0)


def combined(upper, matrix, tail, other, last, need_map):
    factors = matrix.shape[0]

    def kernel(upper_ref, mine_ref, tail_ref, *refs):
        others, outs = refs[: len(other)], refs[len(other) :]
        outs = list(outs)
        next_ref = outs.pop(0)
        map_ref = outs.pop(0) if need_map else None
        packed_ref = None if last else outs.pop(0)
        same = eye(factors)
        if len(other) == 2:
            theirs = rebuilt(others[0][...], others[1][1:2], same)
            their_tail = others[1][0:1]
        else:
            theirs, their_tail = unpacked(others[0], same)

        @pl.when(upper_ref[0] == 1)
        def _():
            combine_into(
                theirs, their_tail, mine_ref[...], tail_ref[0:1], same, map_ref, next_ref, packed_ref
            )

        @pl.when(upper_ref[0] == 0)
        def _():
            combine_into(
                mine_ref[...], tail_ref[0:1], theirs, their_tail, same, map_ref, next_ref, packed_ref
            )

    out_shape = [shape(1, factors)]
    if need_map:
        out_shape.append(shape(factors, factors))
    if not last:
        out_shape.append(shape(factors + PACKED, factors, dtype=BF16))
    return pl.pallas_call(
        kernel,
        in_specs=[smem()] + vmem(2 + len(other)),
        out_specs=vmem(len(out_shape)),
        out_shape=out_shape,
        compiler_params=params(),
        cost_estimate=cost(12 * factors**3, 1 << 20),
        name="combined",
    )(upper, matrix, tail, *other)


def advanced(state, matrix, tail):
    factors = matrix.shape[0]

    def kernel(state_ref, matrix_ref, tail_ref, out_ref):
        out_ref[...] = product(state_ref[...], split(matrix_ref[...])) + tail_ref[...]

    return pl.pallas_call(
        kernel,
        in_specs=vmem(3),
        out_specs=pl.BlockSpec(memory_space=VMEM),
        out_shape=shape(1, factors),
        compiler_params=params(),
        cost_estimate=cost(12 * factors**2, 1 << 18),
        name="advanced",
    )(state, matrix, tail)


def prefixed(uppers, levels, running, last, states):
    day_count, factors = states.shape
    count = len(levels)

    flat = [a for level in levels for a in level]

    def kernel(*refs):
        upper_refs = refs[:count]
        parts = list(refs[count : count + len(flat)])
        run_ref, last_ref, states_ref, high_ref, low_ref, add_ref, work, tail = refs[count + len(flat) :]
        parts = [[parts.pop(0) for _ in level] for level in levels]
        same = eye(factors)
        work[...] = jnp.where(same, 1.0, 0.0)
        tail[...] = jnp.zeros_like(tail)
        for level in reversed(range(count)):

            @pl.when(upper_refs[level][0] == 1)
            def _():
                if len(parts[level]) == 2:
                    rest, packet = parts[level]
                    matrix, add = rebuilt(rest[...], packet[1:2], same), packet[0:1]
                else:
                    matrix, add = unpacked(parts[level][0], same)
                step = split(matrix)
                work[...] = product(work[...], step)
                tail[...] = product(tail[...], step) + add

        for d in range(day_count):
            step = split(run_ref[d] if d < day_count - 1 else last_ref[...])
            place = slice(d * factors, (d + 1) * factors)
            high, low = split(product(work[...], step))
            high_ref[:, place] = high
            low_ref[:, place] = low
            add_ref[:, place] = product(tail[...], step) + states_ref[d : d + 1]

    wide = day_count * factors
    return pl.pallas_call(
        kernel,
        in_specs=[smem()] * count + vmem(len(flat) + 3),
        out_specs=vmem(3),
        out_shape=[
            shape(factors, wide, dtype=BF16),
            shape(factors, wide, dtype=BF16),
            shape(1, wide),
        ],
        scratch_shapes=[pltpu.VMEM((factors, factors), F32), pltpu.VMEM((1, factors), F32)],
        compiler_params=params(),
        cost_estimate=cost(36 * factors**3, 3 << 20),
        name="prefixed",
    )(*uppers, *flat, running, last, states)


def filtered_of(state, arrived, high, low, add):
    factors, wide = high.shape
    day_count = wide // factors

    def kernel(state_ref, arrived_ref, high_ref, low_ref, add_ref, out_ref):
        entering = state_ref[...] + arrived_ref[...]
        row = product(entering, (high_ref[...], low_ref[...])) + add_ref[...]
        for d in range(day_count):
            out_ref[d : d + 1] = row[:, d * factors : (d + 1) * factors]

    return pl.pallas_call(
        kernel,
        in_specs=vmem(5),
        out_specs=pl.BlockSpec(memory_space=VMEM),
        out_shape=shape(day_count, factors),
        compiler_params=params(),
        cost_estimate=cost(6 * factors * wide, 1 << 20),
        name="filtered",
    )(state, arrived, high, low, add)


def smoother_powers(smoother):
    factors = smoother.shape[0]

    def kernel(in_ref, high_ref, low_ref):
        power = in_ref[...].T
        for p in range(POWERS):
            parts = split(power)
            high_ref[p], low_ref[p] = parts
            if p < POWERS - 1:
                power = product(power, parts)

    return pl.pallas_call(
        kernel,
        in_specs=vmem(1),
        out_specs=vmem(2),
        out_shape=[shape(POWERS, factors, factors, dtype=BF16)] * 2,
        compiler_params=params(),
        cost_estimate=cost(24 * factors**3, 2 << 20),
        name="smoother_powers",
    )(smoother)


def finish(index, day_count, gathered, powers, decay, series, loadings, tables):
    days, own = series.shape
    factors = loadings.shape[1]
    stride = 2 ** (POWERS - 1)
    blocks = days // stride

    def kernel(
        index_ref, gathered_ref, high_ref, low_ref, decay_ref, series_hbm, load_hbm, prec_hbm,
        start_hbm, stop_hbm, off_hbm, smooth_ref, score_ref, filt, work, series_ref, load_ref,
        prec_ref, start_ref, stop_ref, off_ref, sems,
    ):
        me = index_ref[0]
        mine = pl.ds(pl.multiple_of(me * own, own), own)
        copies = [
            pltpu.make_async_copy(source, target, sems.at[n])
            for n, (source, target) in enumerate(
                [
                    (load_hbm.at[mine], load_ref),
                    (series_hbm, series_ref),
                    (prec_hbm.at[:, mine], prec_ref),
                    (start_hbm.at[:, mine], start_ref),
                    (stop_hbm.at[:, mine], stop_ref),
                    (off_hbm.at[:, mine], off_ref),
                ]
            )
        ]
        for copy in copies:
            copy.start()
        for m in range(days // day_count):
            filt[m * day_count : (m + 1) * day_count, :] = gathered_ref[m]
        filtered = filt[...]
        carried = filtered * decay_ref[...]
        carried = jnp.concatenate([jnp.zeros((1, factors), F32), carried[:-1]], 0)
        total = filtered - carried
        for p in range(POWERS - 1):
            reach = 2**p
            later = jnp.concatenate([total[reach:], jnp.zeros((reach, factors), F32)], 0)
            total = total + product(later, (high_ref[p], low_ref[p]))
        far = (high_ref[POWERS - 1], low_ref[POWERS - 1])
        row = total[(blocks - 1) * stride :]
        work[(blocks - 1) * stride :, :] = row
        for b in reversed(range(blocks - 1)):
            row = total[b * stride : (b + 1) * stride] + product(row, far)
            work[b * stride : (b + 1) * stride, :] = row
        work[...] += carried
        for d in range(day_count):
            smooth_ref[d : d + 1, :] = work[pl.ds(me * day_count + d, 1), :]
        for copy in copies:
            copy.wait()
        fitted = lax.dot_general(
            work[...].astype(BF16), load_ref[...], (((1,), (1,)), ((), ())),
            preferred_element_type=F32,
        )
        day = lax.broadcasted_iota(jnp.int32, (days, 1), 0)
        active = activity(day, start_ref[...], stop_ref[...], off_ref[...])
        residual = (series_ref[...].astype(F32) - fitted) * jnp.sqrt(prec_ref[...])
        score_ref[...] = jnp.where(active, residual, 0.0).astype(BF16)

    return pl.pallas_call(
        kernel,
        in_specs=[smem()] + vmem(4) + hbm(6),
        out_specs=vmem(2),
        out_shape=[shape(day_count, factors), shape(days, own, dtype=BF16)],
        scratch_shapes=[
            pltpu.VMEM((days, factors), F32),
            pltpu.VMEM((days, factors), F32),
            pltpu.VMEM((days, own), BF16),
            pltpu.VMEM((own, factors), BF16),
            pltpu.VMEM((1, own), F32),
            pltpu.VMEM((1, own), jnp.int32),
            pltpu.VMEM((1, own), jnp.int32),
            pltpu.VMEM((1, own), jnp.int32),
            pltpu.SemaphoreType.DMA((6,)),
        ],
        compiler_params=params(),
        cost_estimate=cost(2 * days * own * factors, 2 << 20),
        name="finish",
    )(index, gathered, *powers, decay, series, loadings, *tables)


def local(series, loadings, precision, start_day, stop_day, off_day, decay, gain, smoother):
    devices = lax.axis_size("tm")
    place = lax.axis_index("tm").astype(jnp.int32)
    index = place[None]
    days = series.shape[0]
    day_count = days // devices
    factors = loadings.shape[1]
    tables = [a.reshape(1, -1) for a in (precision, start_day, stop_day, off_day)]
    decay = decay.reshape(1, factors)

    def swapped(array, distance):
        return lax.ppermute(array, "tm", [(i, i ^ distance) for i in range(devices)])

    partial = partial_drive(index, devices, series, loadings, tables)
    partial, first_day = lax.optimization_barrier((partial, index * day_count))
    terms = lax.all_to_all(partial, "tm", 0, 0, tiled=True)
    steps, running, mine, rest, diag = transitions_of(first_day, day_count, loadings, tables, decay, gain)
    rest, terms = lax.optimization_barrier((rest, terms))
    states, packet = own_states(terms, steps, gain, diag)

    group = min(8, devices)
    matrix, tail = mine, packet
    sent = (rest, packet)
    levels, uppers = [], []
    reach = 1
    while reach < group:
        other = tuple(swapped(a, reach) for a in sent)
        upper = jnp.where((place & reach) != 0, 1, 0).astype(jnp.int32)[None]
        levels.append(other)
        uppers.append(upper)
        last = reach * 2 == group
        if reach == 2:
            sent, smoother = lax.optimization_barrier((sent, smoother))
            powers = smoother_powers(smoother)
            tail, powers = lax.optimization_barrier((tail, powers))
        need_map = not last or devices // group > 2
        tail, *rest_of = combined(upper, matrix, tail, other, last, need_map)
        matrix, sent = (rest_of[0], rest_of[1:]) if need_map else (None, None)
        reach *= 2

    ahead = prefixed(uppers, levels, running, mine, states)
    state = jnp.zeros((1, factors), F32)
    arrived = jnp.where(place // group == 1, swapped(tail, group), 0.0)
    for g in range(1, devices // group - 1):
        state = state + arrived
        moved = advanced(state, matrix, tail)
        pairs = [(g * group + j, (g + 1) * group + j) for j in range(group)]
        arrived = lax.ppermute(moved, "tm", pairs)

    mine = filtered_of(state, arrived, *ahead)[None]
    gathered = lax.all_to_all(
        jnp.broadcast_to(mine, (devices, day_count, factors)), "tm", 0, 0, tiled=True
    )
    return tuple(finish(index, day_count, gathered, powers, decay, series, loadings, tables))


def solution(mesh):
    in_specs = (
        P(None, ("spec", "tm")),
        P("spec", None),
        P("spec"),
        P("spec"),
        P("spec"),
        P("spec"),
        P(),
        P(),
        P(),
    )
    out_specs = (P("tm", "spec"), P(None, ("spec", "tm")))
    return jax.shard_map(local, mesh=mesh, in_specs=in_specs, out_specs=out_specs, check_vma=False)
```

```python
import jax
import jax.numpy as jnp
from jax import lax
from jax.experimental import pallas as pl
from jax.experimental.pallas import tpu as pltpu
from jax.sharding import PartitionSpec as P

F32 = jnp.float32
BF16 = jnp.bfloat16
VMEM = pltpu.MemorySpace.VMEM
SMEM = pltpu.MemorySpace.SMEM
HBM = pltpu.MemorySpace.HBM
POWERS = 5


def params(mebibytes=48, **more):
    return pltpu.CompilerParams(vmem_limit_bytes=mebibytes << 20, **more)


def cost(flops, nbytes):
    return pl.CostEstimate(flops=flops, bytes_accessed=nbytes, transcendentals=0)


def vmem(count):
    return [pl.BlockSpec(memory_space=VMEM)] * count


def hbm(count):
    return [pl.BlockSpec(memory_space=HBM)] * count


def smem():
    return pl.BlockSpec(memory_space=SMEM)


def shape(*dims, dtype=F32):
    return jax.ShapeDtypeStruct(dims, dtype)


def mul(a, b):
    return jnp.dot(a, b, preferred_element_type=F32)


def split(a):
    high = a.astype(BF16)
    return high, (a - high.astype(F32)).astype(BF16)


def product(a, b):
    high, low = split(a)
    return mul(high, b[0]) + mul(low, b[0]) + mul(high, b[1])


def eye(factors):
    dims = (factors, factors)
    return lax.broadcasted_iota(jnp.int32, dims, 0) == lax.broadcasted_iota(jnp.int32, dims, 1)


def activity(day, start, stop, off):
    return (day >= start) & (day < stop) & (lax.rem(day, 7) != off)


def partial_drive(index, devices, series, loadings, tables):
    days, own = series.shape
    day_count = days // devices
    factors = loadings.shape[1]

    def kernel(
        index_ref, series_hbm, load_hbm, prec_hbm, start_hbm, stop_hbm, off_hbm, out_ref,
        series_ref, load_ref, prec_ref, start_ref, stop_ref, off_ref, sems,
    ):
        first = pl.multiple_of(index_ref[0] * own, own)
        mine = pl.ds(first, own)
        copies = [
            pltpu.make_async_copy(source, target, sems.at[n])
            for n, (source, target) in enumerate(
                [
                    (prec_hbm.at[:, mine], prec_ref),
                    (start_hbm.at[:, mine], start_ref),
                    (stop_hbm.at[:, mine], stop_ref),
                    (off_hbm.at[:, mine], off_ref),
                    (series_hbm, series_ref),
                    (load_hbm.at[mine], load_ref),
                ]
            )
        ]
        for copy in copies:
            copy.start()
        day = lax.broadcasted_iota(jnp.int32, (days, 1), 0)
        for copy in copies[:5]:
            copy.wait()
        active = activity(day, start_ref[...], stop_ref[...], off_ref[...])
        weights = jnp.where(active, prec_ref[...], 0.0)
        weighted = (weights * series_ref[...].astype(F32)).astype(BF16)
        copies[5].wait()
        drive = mul(weighted, load_ref[...])
        for p in range(devices):
            out_ref[p] = drive[p * day_count : (p + 1) * day_count]

    return pl.pallas_call(
        kernel,
        in_specs=[smem()] + hbm(6),
        out_specs=pl.BlockSpec(memory_space=VMEM),
        out_shape=shape(devices, day_count, factors),
        scratch_shapes=[
            pltpu.VMEM((days, own), BF16),
            pltpu.VMEM((own, factors), BF16),
            pltpu.VMEM((1, own), F32),
            pltpu.VMEM((1, own), jnp.int32),
            pltpu.VMEM((1, own), jnp.int32),
            pltpu.VMEM((1, own), jnp.int32),
            pltpu.SemaphoreType.DMA((6,)),
        ],
        compiler_params=params(63),
        cost_estimate=cost(2 * days * own * factors, 1 << 20),
        name="partial_drive",
    )(index, series, loadings, *tables)


def transitions_of(first_day, day_count, loadings, tables, decay, gain):
    providers, factors = loadings.shape
    unit = providers // 16
    sizes = [unit, unit, 2 * unit, 4 * unit, 8 * unit]
    parts = [slice(sum(sizes[:n]), sum(sizes[: n + 1])) for n in range(len(sizes))]

    def kernel(
        day_ref, load_hbm, prec_hbm, start_hbm, stop_hbm, off_hbm, decay_hbm, gain_hbm,
        step_ref, run_ref, last_ref, rest_ref, diag_ref,
        acc, load_ref, prec_ref, start_ref, stop_ref, off_ref, decay_ref, gain_ref, sems,
    ):
        pairs = [
            (prec_hbm, prec_ref),
            (start_hbm, start_ref),
            (stop_hbm, stop_ref),
            (off_hbm, off_ref),
        ]
        pairs += [(load_hbm.at[part], load_ref.at[part]) for part in parts]
        pairs += [(decay_hbm, decay_ref), (gain_hbm, gain_ref)]
        copies = [
            pltpu.make_async_copy(source, target, sems.at[n])
            for n, (source, target) in enumerate(pairs)
        ]
        for copy in copies:
            copy.start()
        for copy in copies[:4]:
            copy.wait()
        for n, part in enumerate(parts):
            copies[4 + n].wait()
            block = load_ref[part]
            scaled = (block.T.astype(F32) * prec_ref[:, part]).astype(BF16)
            for d in range(day_count):
                active = activity(
                    day_ref[0] + d, start_ref[:, part], stop_ref[:, part], off_ref[:, part]
                )
                mask = active.astype(F32).astype(BF16)
                term = mul(scaled * mask, block)
                acc[d] = term if n == 0 else acc[d] + term
        for copy in copies[4 + len(parts) :]:
            copy.wait()
        same = eye(factors)
        diagonal = jnp.where(same, decay_ref[...], 0.0)
        column = jnp.sum(diagonal, axis=1, keepdims=True)
        steps_of = []
        for d in range(day_count):
            damped = (acc[d] * column).astype(BF16)
            pulled = lax.dot_general(
                damped, gain_ref[...], (((1,), (1,)), ((), ())), preferred_element_type=F32
            )
            steps_of.append(diagonal - pulled)
        running = steps_of[0]
        for d in range(1, day_count):
            run_ref[d - 1] = running
            step_ref[d - 1] = steps_of[d]
            running = product(running, split(steps_of[d]))
        last = running
        last_ref[...] = last
        rest_ref[...] = jnp.where(same, 0.0, last).astype(BF16)
        diag_ref[...] = jnp.sum(jnp.where(same, last, 0.0), axis=0, keepdims=True)

    return pl.pallas_call(
        kernel,
        in_specs=[smem()] + hbm(7),
        out_specs=vmem(5),
        out_shape=[
            shape(day_count - 1, factors, factors),
            shape(day_count - 1, factors, factors),
            shape(factors, factors),
            shape(factors, factors, dtype=BF16),
            shape(1, factors),
        ],
        scratch_shapes=[
            pltpu.VMEM((day_count, factors, factors), F32),
            pltpu.VMEM((providers, factors), BF16),
            pltpu.VMEM((1, providers), F32),
            pltpu.VMEM((1, providers), jnp.int32),
            pltpu.VMEM((1, providers), jnp.int32),
            pltpu.VMEM((1, providers), jnp.int32),
            pltpu.VMEM((1, factors), F32),
            pltpu.VMEM((factors, factors), BF16),
            pltpu.SemaphoreType.DMA((6 + len(parts),)),
        ],
        compiler_params=params(),
        cost_estimate=cost(2 * day_count * providers * factors * factors, 10 << 20),
        name="transitions",
    )(first_day, loadings, *tables, decay, gain)


def own_states(terms, steps, gain, diag):
    parts, day_count, factors = terms.shape

    def kernel(terms_ref, step_ref, gain_ref, diag_ref, out_ref, packet_ref):
        drive = terms_ref[0]
        for p in range(1, parts):
            drive = drive + terms_ref[p]
        high, low = split(drive)
        weights = gain_ref[...]
        dims = (((1,), (1,)), ((), ()))
        rest = (drive - high.astype(F32) - low.astype(F32)).astype(BF16)
        offsets = sum(
            lax.dot_general(part, weights, dims, preferred_element_type=F32)
            for part in (high, low, rest)
        )
        state = offsets[0:1]
        out_ref[0:1] = state
        for d in range(1, day_count):
            state = product(state, split(step_ref[d - 1])) + offsets[d : d + 1]
            out_ref[d : d + 1] = state
        packet_ref[0:1] = state
        packet_ref[1:2] = diag_ref[...]

    return pl.pallas_call(
        kernel,
        in_specs=vmem(4),
        out_specs=vmem(2),
        out_shape=[shape(day_count, factors), shape(2, factors)],
        compiler_params=params(),
        cost_estimate=cost(20 * factors * factors * 8, 1 << 20),
        name="own_states",
    )(terms, steps, gain, diag)


PACKED = 16


def unpacked(packed_ref):
    factors = packed_ref.shape[1]
    rows = packed_ref[factors:].astype(F32)
    return packed_ref[:factors], rows[2:3] + rows[3:4], rows[0:1] + rows[1:2]


def through(a, rest, diag):
    high, low = split(a)
    return mul(high, rest) + mul(low, rest) + a * diag


def combined(upper, matrix, packet, other_rest, other_packet):
    factors = matrix.shape[0]

    def kernel(upper_ref, mine_ref, packet_ref, rest_ref, other_ref, packed_ref):
        same = eye(factors)

        def pack(total, tail):
            packed_ref[:factors] = jnp.where(same, 0.0, total).astype(BF16)
            diag = jnp.sum(jnp.where(same, total, 0.0), axis=0, keepdims=True)
            rows = [*split(tail), *split(diag), jnp.zeros((PACKED - 4, factors), BF16)]
            packed_ref[factors:] = jnp.concatenate(rows, 0)

        @pl.when(upper_ref[0] == 1)
        def _():
            mine = split(mine_ref[...])
            theirs = rest_ref[...].astype(F32) + jnp.where(same, other_ref[1:2], 0.0)
            pack(product(theirs, mine), product(other_ref[0:1], mine) + packet_ref[0:1])

        @pl.when(upper_ref[0] == 0)
        def _():
            rest, diag = rest_ref[...], other_ref[1:2]
            pack(
                through(mine_ref[...], rest, diag),
                through(packet_ref[0:1], rest, diag) + other_ref[0:1],
            )

    return pl.pallas_call(
        kernel,
        in_specs=[smem()] + vmem(4),
        out_specs=pl.BlockSpec(memory_space=VMEM),
        out_shape=shape(factors + PACKED, factors, dtype=BF16),
        compiler_params=params(),
        cost_estimate=cost(6 * factors**3, 1 << 20),
        name="combined",
    )(upper, matrix, packet, other_rest, other_packet)


def advanced(pair, state, pieces):
    count = len(pieces)
    factors = pieces[0].shape[1]

    def kernel(pair_ref, state_ref, *refs):
        out_ref = refs[-1]
        out_ref[...] = state_ref[...]
        for turn in range(count):
            for m in range(count):

                @pl.when((pair_ref[0] ^ m) == turn)
                def _():
                    rest, diag, tail = unpacked(refs[m])
                    out_ref[...] = through(out_ref[...], rest, diag) + tail

    return pl.pallas_call(
        kernel,
        in_specs=[smem()] + vmem(count + 1),
        out_specs=pl.BlockSpec(memory_space=VMEM),
        out_shape=shape(1, factors),
        compiler_params=params(),
        cost_estimate=cost(12 * factors**2, 1 << 18),
        name="advanced",
    )(pair, state, *pieces)


def prefixed(pair, upper, pieces, other_rest, other_packet, running, last, states):
    day_count, factors = states.shape
    count = len(pieces)

    def kernel(pair_ref, upper_ref, *refs):
        rest_ref, packet_ref, run_ref, last_ref, states_ref = refs[count : count + 5]
        high_ref, low_ref, add_ref, work, tail = refs[count + 5 :]
        work[...] = jnp.where(eye(factors), 1.0, 0.0)
        tail[...] = jnp.zeros_like(tail)

        def follow(rest, diag, add):
            work[...] = through(work[...], rest, diag)
            tail[...] = through(tail[...], rest, diag) + add

        for turn in range(count - 1):
            for m in range(1, count):

                @pl.when(((pair_ref[0] ^ m) == turn) & (pair_ref[0] > turn))
                def _():
                    follow(*unpacked(refs[m]))

        @pl.when(upper_ref[0] == 1)
        def _():
            follow(rest_ref[...], packet_ref[1:2], packet_ref[0:1])

        for d in range(day_count):
            step = split(run_ref[d] if d < day_count - 1 else last_ref[...])
            place = slice(d * factors, (d + 1) * factors)
            high, low = split(product(work[...], step))
            high_ref[:, place] = high
            low_ref[:, place] = low
            add_ref[:, place] = product(tail[...], step) + states_ref[d : d + 1]

    wide = day_count * factors
    return pl.pallas_call(
        kernel,
        in_specs=[smem()] * 2 + vmem(count + 5),
        out_specs=vmem(3),
        out_shape=[
            shape(factors, wide, dtype=BF16),
            shape(factors, wide, dtype=BF16),
            shape(1, wide),
        ],
        scratch_shapes=[pltpu.VMEM((factors, factors), F32), pltpu.VMEM((1, factors), F32)],
        compiler_params=params(),
        cost_estimate=cost(36 * factors**3, 3 << 20),
        name="prefixed",
    )(pair, upper, *pieces, other_rest, other_packet, running, last, states)


def filtered_of(state, arrived, high, low, add):
    factors, wide = high.shape
    day_count = wide // factors

    def kernel(state_ref, arrived_ref, high_ref, low_ref, add_ref, out_ref):
        entering = state_ref[...] + arrived_ref[...]
        row = product(entering, (high_ref[...], low_ref[...])) + add_ref[...]
        for d in range(day_count):
            out_ref[d : d + 1] = row[:, d * factors : (d + 1) * factors]

    return pl.pallas_call(
        kernel,
        in_specs=vmem(5),
        out_specs=pl.BlockSpec(memory_space=VMEM),
        out_shape=shape(day_count, factors),
        compiler_params=params(),
        cost_estimate=cost(6 * factors * wide, 1 << 20),
        name="filtered",
    )(state, arrived, high, low, add)


def smoother_powers(smoother):
    factors = smoother.shape[0]

    def kernel(in_ref, high_ref, low_ref):
        power = in_ref[...].T
        for p in range(POWERS):
            parts = split(power)
            high_ref[p], low_ref[p] = parts
            if p < POWERS - 1:
                power = product(power, parts)

    return pl.pallas_call(
        kernel,
        in_specs=vmem(1),
        out_specs=vmem(2),
        out_shape=[shape(POWERS, factors, factors, dtype=BF16)] * 2,
        compiler_params=params(),
        cost_estimate=cost(24 * factors**3, 2 << 20),
        name="smoother_powers",
    )(smoother)


def finish(index, day_count, gathered, powers, decay, series, loadings, tables):
    days, own = series.shape
    factors = loadings.shape[1]
    stride = 2 ** (POWERS - 1)
    blocks = days // stride

    def kernel(
        index_ref, gathered_ref, high_ref, low_ref, decay_ref, series_hbm, load_hbm, prec_hbm,
        start_hbm, stop_hbm, off_hbm, smooth_ref, score_ref, filt, work, series_ref, load_ref,
        prec_ref, start_ref, stop_ref, off_ref, sems,
    ):
        me = index_ref[0]
        mine = pl.ds(pl.multiple_of(me * own, own), own)
        copies = [
            pltpu.make_async_copy(source, target, sems.at[n])
            for n, (source, target) in enumerate(
                [
                    (load_hbm.at[mine], load_ref),
                    (series_hbm, series_ref),
                    (prec_hbm.at[:, mine], prec_ref),
                    (start_hbm.at[:, mine], start_ref),
                    (stop_hbm.at[:, mine], stop_ref),
                    (off_hbm.at[:, mine], off_ref),
                ]
            )
        ]
        for copy in copies:
            copy.start()
        for m in range(days // day_count):
            filt[m * day_count : (m + 1) * day_count, :] = gathered_ref[m]
        filtered = filt[...]
        carried = filtered * decay_ref[...]
        carried = jnp.concatenate([jnp.zeros((1, factors), F32), carried[:-1]], 0)
        total = filtered - carried
        for p in range(POWERS - 1):
            reach = 2**p
            later = jnp.concatenate([total[reach:], jnp.zeros((reach, factors), F32)], 0)
            total = total + product(later, (high_ref[p], low_ref[p]))
        far = (high_ref[POWERS - 1], low_ref[POWERS - 1])
        row = total[(blocks - 1) * stride :]
        work[(blocks - 1) * stride :, :] = row
        for b in reversed(range(blocks - 1)):
            row = total[b * stride : (b + 1) * stride] + product(row, far)
            work[b * stride : (b + 1) * stride, :] = row
        work[...] += carried
        for d in range(day_count):
            smooth_ref[d : d + 1, :] = work[pl.ds(me * day_count + d, 1), :]
        for copy in copies:
            copy.wait()
        fitted = lax.dot_general(
            work[...].astype(BF16), load_ref[...], (((1,), (1,)), ((), ())),
            preferred_element_type=F32,
        )
        day = lax.broadcasted_iota(jnp.int32, (days, 1), 0)
        active = activity(day, start_ref[...], stop_ref[...], off_ref[...])
        residual = (series_ref[...].astype(F32) - fitted) * jnp.sqrt(prec_ref[...])
        score_ref[...] = jnp.where(active, residual, 0.0).astype(BF16)

    return pl.pallas_call(
        kernel,
        in_specs=[smem()] + vmem(4) + hbm(6),
        out_specs=vmem(2),
        out_shape=[shape(day_count, factors), shape(days, own, dtype=BF16)],
        scratch_shapes=[
            pltpu.VMEM((days, factors), F32),
            pltpu.VMEM((days, factors), F32),
            pltpu.VMEM((days, own), BF16),
            pltpu.VMEM((own, factors), BF16),
            pltpu.VMEM((1, own), F32),
            pltpu.VMEM((1, own), jnp.int32),
            pltpu.VMEM((1, own), jnp.int32),
            pltpu.VMEM((1, own), jnp.int32),
            pltpu.SemaphoreType.DMA((6,)),
        ],
        compiler_params=params(),
        cost_estimate=cost(2 * days * own * factors, 2 << 20),
        name="finish",
    )(index, gathered, *powers, decay, series, loadings, *tables)


def local(series, loadings, precision, start_day, stop_day, off_day, decay, gain, smoother):
    devices = lax.axis_size("tm")
    place = lax.axis_index("tm").astype(jnp.int32)
    index = place[None]
    days = series.shape[0]
    day_count = days // devices
    factors = loadings.shape[1]
    tables = [a.reshape(1, -1) for a in (precision, start_day, stop_day, off_day)]
    decay = decay.reshape(1, factors)

    def swapped(array, distance):
        return lax.ppermute(array, "tm", [(i, i ^ distance) for i in range(devices)])

    partial = partial_drive(index, devices, series, loadings, tables)
    partial, first_day = lax.optimization_barrier((partial, index * day_count))
    terms = lax.all_to_all(partial, "tm", 0, 0, tiled=True)
    steps, running, mine, rest, diag = transitions_of(first_day, day_count, loadings, tables, decay, gain)
    rest, terms = lax.optimization_barrier((rest, terms))
    states, packet = own_states(terms, steps, gain, diag)

    upper = (place & 1)[None]
    other_rest, other_packet = swapped(rest, 1), swapped(packet, 1)
    packed = combined(upper, mine, packet, other_rest, other_packet)
    group = min(8, devices)
    pair = ((place % group) >> 1)[None]
    pieces = [packed] + [swapped(packed, 2 * m) for m in range(1, group // 2)]
    smoother, packed = lax.optimization_barrier((smoother, packed))
    powers = smoother_powers(smoother)
    nothing = jnp.zeros((1, factors), F32)
    nothing, powers = lax.optimization_barrier((nothing, powers))
    tail = advanced(pair, nothing, pieces)
    ahead = prefixed(pair, upper, pieces, other_rest, other_packet, running, mine, states)

    state = nothing
    arrived = jnp.where(place // group == 1, swapped(tail, group), 0.0)
    for g in range(1, devices // group - 1):
        state = state + arrived
        moved = advanced(pair, state, pieces)
        pairs = [(g * group + j, (g + 1) * group + j) for j in range(group)]
        arrived = lax.ppermute(moved, "tm", pairs)

    own = filtered_of(state, arrived, *ahead)[None]
    gathered = lax.all_to_all(
        jnp.broadcast_to(own, (devices, day_count, factors)), "tm", 0, 0, tiled=True
    )
    return tuple(finish(index, day_count, gathered, powers, decay, series, loadings, tables))


def solution(mesh):
    in_specs = (
        P(None, ("spec", "tm")),
        P("spec", None),
        P("spec"),
        P("spec"),
        P("spec"),
        P("spec"),
        P(),
        P(),
        P(),
    )
    out_specs = (P("tm", "spec"), P(None, ("spec", "tm")))
    return jax.shard_map(local, mesh=mesh, in_specs=in_specs, out_specs=out_specs, check_vma=False)
```

```python
import jax
import jax.numpy as jnp
from jax import lax
from jax.experimental import pallas as pl
from jax.experimental.pallas import tpu as pltpu
from jax.sharding import PartitionSpec as P

F32 = jnp.float32
BF16 = jnp.bfloat16
VMEM = pltpu.MemorySpace.VMEM
SMEM = pltpu.MemorySpace.SMEM
HBM = pltpu.MemorySpace.HBM
POWERS = 5


def params(mebibytes=48, **more):
    return pltpu.CompilerParams(vmem_limit_bytes=mebibytes << 20, **more)


def cost(flops, nbytes):
    return pl.CostEstimate(flops=flops, bytes_accessed=nbytes, transcendentals=0)


def vmem(count):
    return [pl.BlockSpec(memory_space=VMEM)] * count


def hbm(count):
    return [pl.BlockSpec(memory_space=HBM)] * count


def smem():
    return pl.BlockSpec(memory_space=SMEM)


def shape(*dims, dtype=F32):
    return jax.ShapeDtypeStruct(dims, dtype)


def mul(a, b):
    return jnp.dot(a, b, preferred_element_type=F32)


def split(a):
    high = a.astype(BF16)
    return high, (a - high.astype(F32)).astype(BF16)


def product(a, b):
    high, low = split(a)
    return mul(high, b[0]) + mul(low, b[0]) + mul(high, b[1])


def eye(factors):
    dims = (factors, factors)
    return lax.broadcasted_iota(jnp.int32, dims, 0) == lax.broadcasted_iota(jnp.int32, dims, 1)


def activity(day, start, stop, off):
    return (day >= start) & (day < stop) & (lax.rem(day, 7) != off)


def partial_drive(index, devices, series, loadings, tables):
    days, own = series.shape
    day_count = days // devices
    factors = loadings.shape[1]

    def kernel(
        index_ref, series_hbm, load_hbm, prec_hbm, start_hbm, stop_hbm, off_hbm, out_ref,
        series_ref, load_ref, prec_ref, start_ref, stop_ref, off_ref, sems,
    ):
        first = pl.multiple_of(index_ref[0] * own, own)
        mine = pl.ds(first, own)
        copies = [
            pltpu.make_async_copy(source, target, sems.at[n])
            for n, (source, target) in enumerate(
                [
                    (prec_hbm.at[:, mine], prec_ref),
                    (start_hbm.at[:, mine], start_ref),
                    (stop_hbm.at[:, mine], stop_ref),
                    (off_hbm.at[:, mine], off_ref),
                    (series_hbm, series_ref),
                    (load_hbm.at[mine], load_ref),
                ]
            )
        ]
        for copy in copies:
            copy.start()
        day = lax.broadcasted_iota(jnp.int32, (days, 1), 0)
        for copy in copies[:5]:
            copy.wait()
        active = activity(day, start_ref[...], stop_ref[...], off_ref[...])
        weights = jnp.where(active, prec_ref[...], 0.0)
        weighted = (weights * series_ref[...].astype(F32)).astype(BF16)
        copies[5].wait()
        drive = mul(weighted, load_ref[...])
        for p in range(devices):
            out_ref[p] = drive[p * day_count : (p + 1) * day_count]

    return pl.pallas_call(
        kernel,
        in_specs=[smem()] + hbm(6),
        out_specs=pl.BlockSpec(memory_space=VMEM),
        out_shape=shape(devices, day_count, factors),
        scratch_shapes=[
            pltpu.VMEM((days, own), BF16),
            pltpu.VMEM((own, factors), BF16),
            pltpu.VMEM((1, own), F32),
            pltpu.VMEM((1, own), jnp.int32),
            pltpu.VMEM((1, own), jnp.int32),
            pltpu.VMEM((1, own), jnp.int32),
            pltpu.SemaphoreType.DMA((6,)),
        ],
        compiler_params=params(63),
        cost_estimate=cost(2 * days * own * factors, 1 << 20),
        name="partial_drive",
    )(index, series, loadings, *tables)


def damped_of(first_day, day_count, loadings, tables, decay):
    providers, factors = loadings.shape
    unit = providers // 16
    sizes = [unit, unit, 2 * unit, 4 * unit, 8 * unit]
    parts = [slice(sum(sizes[:n]), sum(sizes[: n + 1])) for n in range(len(sizes))]

    def kernel(
        day_ref, decay_ref, load_hbm, prec_hbm, start_hbm, stop_hbm, off_hbm, out_ref, acc, load_ref,
        prec_ref, start_ref, stop_ref, off_ref, sems,
    ):
        pairs = [
            (prec_hbm, prec_ref),
            (start_hbm, start_ref),
            (stop_hbm, stop_ref),
            (off_hbm, off_ref),
        ]
        pairs += [(load_hbm.at[part], load_ref.at[part]) for part in parts]
        copies = [
            pltpu.make_async_copy(source, target, sems.at[n])
            for n, (source, target) in enumerate(pairs)
        ]
        for copy in copies:
            copy.start()
        column = jnp.sum(jnp.where(eye(factors), decay_ref[...], 0.0), axis=1, keepdims=True)
        for copy in copies[:4]:
            copy.wait()
        for n, part in enumerate(parts):
            copies[4 + n].wait()
            block = load_ref[part]
            scaled = (block.T.astype(F32) * prec_ref[:, part]).astype(BF16)
            for d in range(day_count):
                active = activity(
                    day_ref[0] + d, start_ref[:, part], stop_ref[:, part], off_ref[:, part]
                )
                mask = active.astype(F32).astype(BF16)
                term = mul(scaled * mask, block)
                if n == 0:
                    acc[d] = term
                elif n < len(parts) - 1:
                    acc[d] += term
                else:
                    out_ref[d] = ((acc[d] + term) * column).astype(BF16)

    return pl.pallas_call(
        kernel,
        in_specs=[smem()] + vmem(1) + hbm(5),
        out_specs=pl.BlockSpec(memory_space=VMEM),
        out_shape=shape(day_count, factors, factors, dtype=BF16),
        scratch_shapes=[
            pltpu.VMEM((day_count, factors, factors), F32),
            pltpu.VMEM((providers, factors), BF16),
            pltpu.VMEM((1, providers), F32),
            pltpu.VMEM((1, providers), jnp.int32),
            pltpu.VMEM((1, providers), jnp.int32),
            pltpu.VMEM((1, providers), jnp.int32),
            pltpu.SemaphoreType.DMA((4 + len(parts),)),
        ],
        compiler_params=params(),
        cost_estimate=cost(2 * day_count * providers * factors * factors, 10 << 20),
        name="damped",
    )(first_day, decay, loadings, *tables)


PACKED = 16


def unpacked(packed_ref):
    factors = packed_ref.shape[1]
    rows = packed_ref[factors:].astype(F32)
    return packed_ref[:factors], rows[2:3] + rows[3:4], rows[0:1] + rows[1:2]


def pack(packed_ref, total, tail, same):
    factors = total.shape[0]
    packed_ref[:factors] = jnp.where(same, 0.0, total).astype(BF16)
    diag = jnp.sum(jnp.where(same, total, 0.0), axis=0, keepdims=True)
    rows = [*split(tail), *split(diag), jnp.zeros((PACKED - 4, factors), BF16)]
    packed_ref[factors:] = jnp.concatenate(rows, 0)


def through(a, rest, diag):
    high, low = split(a)
    return mul(high, rest) + mul(low, rest) + a * diag


def block_of(damped, terms, decay, gain):
    parts, day_count, factors = terms.shape

    def kernel(
        damped_ref, terms_ref, decay_ref, gain_ref, run_ref, last_ref, states_ref, tail_ref, packed_ref
    ):
        same = eye(factors)
        weights = gain_ref[...]
        dims = (((1,), (1,)), ((), ()))
        drive = terms_ref[0]
        for p in range(1, parts):
            drive = drive + terms_ref[p]
        high, low = split(drive)
        least = (drive - high.astype(F32) - low.astype(F32)).astype(BF16)
        offsets = sum(
            lax.dot_general(part, weights, dims, preferred_element_type=F32)
            for part in (high, low, least)
        )
        diagonal = jnp.where(same, decay_ref[...], 0.0)
        for d in range(day_count):
            step = diagonal - lax.dot_general(
                damped_ref[d], weights, dims, preferred_element_type=F32
            )
            if d == 0:
                running, state = step, offsets[0:1]
            else:
                run_ref[d - 1] = running
                step = split(step)
                running = product(running, step)
                state = product(state, step) + offsets[d : d + 1]
            states_ref[d : d + 1] = state
        last_ref[...] = running
        tail_ref[...] = state
        pack(packed_ref, running, state, same)

    return pl.pallas_call(
        kernel,
        in_specs=vmem(4),
        out_specs=vmem(5),
        out_shape=[
            shape(day_count - 1, factors, factors),
            shape(factors, factors),
            shape(day_count, factors),
            shape(1, factors),
            shape(factors + PACKED, factors, dtype=BF16),
        ],
        compiler_params=params(),
        cost_estimate=cost(50 * factors**3, 3 << 20),
        name="block",
    )(damped, terms, decay, gain)


def combined(upper, matrix, tail, other):
    factors = matrix.shape[0]

    def kernel(upper_ref, mine_ref, tail_ref, other_ref, packed_ref):
        same = eye(factors)
        rest, diag, other_tail = unpacked(other_ref)

        @pl.when(upper_ref[0] == 1)
        def _():
            mine = split(mine_ref[...])
            theirs = rest.astype(F32) + jnp.where(same, diag, 0.0)
            total = product(theirs, mine)
            pack(packed_ref, total, product(other_tail, mine) + tail_ref[...], same)

        @pl.when(upper_ref[0] == 0)
        def _():
            total = through(mine_ref[...], rest, diag)
            pack(packed_ref, total, through(tail_ref[...], rest, diag) + other_tail, same)

    return pl.pallas_call(
        kernel,
        in_specs=[smem()] + vmem(3),
        out_specs=pl.BlockSpec(memory_space=VMEM),
        out_shape=shape(factors + PACKED, factors, dtype=BF16),
        compiler_params=params(),
        cost_estimate=cost(6 * factors**3, 1 << 20),
        name="combined",
    )(upper, matrix, tail, other)


def advanced(pair, state, pieces):
    count = len(pieces)
    factors = pieces[0].shape[1]

    def kernel(pair_ref, state_ref, *refs):
        out_ref = refs[-1]
        out_ref[...] = state_ref[...]
        for turn in range(count):
            for m in range(count):

                @pl.when((pair_ref[0] ^ m) == turn)
                def _():
                    rest, diag, tail = unpacked(refs[m])
                    out_ref[...] = through(out_ref[...], rest, diag) + tail

    return pl.pallas_call(
        kernel,
        in_specs=[smem()] + vmem(count + 1),
        out_specs=pl.BlockSpec(memory_space=VMEM),
        out_shape=shape(1, factors),
        compiler_params=params(),
        cost_estimate=cost(12 * factors**2, 1 << 18),
        name="advanced",
    )(pair, state, *pieces)


def prefixed(pair, upper, pieces, other, running, last, states):
    day_count, factors = states.shape
    count = len(pieces)

    def kernel(pair_ref, upper_ref, *refs):
        other_ref, run_ref, last_ref, states_ref = refs[count : count + 4]
        high_ref, low_ref, add_ref, work, tail = refs[count + 4 :]
        work[...] = jnp.where(eye(factors), 1.0, 0.0)
        tail[...] = jnp.zeros_like(tail)

        def follow(rest, diag, add):
            work[...] = through(work[...], rest, diag)
            tail[...] = through(tail[...], rest, diag) + add

        for turn in range(count - 1):
            for m in range(1, count):

                @pl.when(((pair_ref[0] ^ m) == turn) & (pair_ref[0] > turn))
                def _():
                    follow(*unpacked(refs[m]))

        @pl.when(upper_ref[0] == 1)
        def _():
            follow(*unpacked(other_ref))

        for d in range(day_count):
            step = split(run_ref[d] if d < day_count - 1 else last_ref[...])
            place = slice(d * factors, (d + 1) * factors)
            high, low = split(product(work[...], step))
            high_ref[:, place] = high
            low_ref[:, place] = low
            add_ref[:, place] = product(tail[...], step) + states_ref[d : d + 1]

    wide = day_count * factors
    return pl.pallas_call(
        kernel,
        in_specs=[smem()] * 2 + vmem(count + 4),
        out_specs=vmem(3),
        out_shape=[
            shape(factors, wide, dtype=BF16),
            shape(factors, wide, dtype=BF16),
            shape(1, wide),
        ],
        scratch_shapes=[pltpu.VMEM((factors, factors), F32), pltpu.VMEM((1, factors), F32)],
        compiler_params=params(),
        cost_estimate=cost(36 * factors**3, 3 << 20),
        name="prefixed",
    )(pair, upper, *pieces, other, running, last, states)


def filtered_of(state, arrived, high, low, add):
    factors, wide = high.shape
    day_count = wide // factors

    def kernel(state_ref, arrived_ref, high_ref, low_ref, add_ref, out_ref):
        entering = state_ref[...] + arrived_ref[...]
        row = product(entering, (high_ref[...], low_ref[...])) + add_ref[...]
        for d in range(day_count):
            out_ref[d : d + 1] = row[:, d * factors : (d + 1) * factors]

    return pl.pallas_call(
        kernel,
        in_specs=vmem(5),
        out_specs=pl.BlockSpec(memory_space=VMEM),
        out_shape=shape(day_count, factors),
        compiler_params=params(),
        cost_estimate=cost(6 * factors * wide, 1 << 20),
        name="filtered",
    )(state, arrived, high, low, add)


def smoother_powers(smoother):
    factors = smoother.shape[0]

    def kernel(in_ref, high_ref, low_ref):
        power = in_ref[...].T
        for p in range(POWERS):
            parts = split(power)
            high_ref[p], low_ref[p] = parts
            if p < POWERS - 1:
                power = product(power, parts)

    return pl.pallas_call(
        kernel,
        in_specs=vmem(1),
        out_specs=vmem(2),
        out_shape=[shape(POWERS, factors, factors, dtype=BF16)] * 2,
        compiler_params=params(),
        cost_estimate=cost(24 * factors**3, 2 << 20),
        name="smoother_powers",
    )(smoother)


def finish(index, day_count, gathered, powers, decay, series, loadings, tables):
    days, own = series.shape
    factors = loadings.shape[1]
    stride = 2 ** (POWERS - 1)
    blocks = days // stride

    def kernel(
        index_ref, gathered_ref, high_ref, low_ref, decay_ref, series_hbm, load_hbm, prec_hbm,
        start_hbm, stop_hbm, off_hbm, smooth_ref, score_ref, filt, work, series_ref, load_ref,
        prec_ref, start_ref, stop_ref, off_ref, sems,
    ):
        me = index_ref[0]
        mine = pl.ds(pl.multiple_of(me * own, own), own)
        copies = [
            pltpu.make_async_copy(source, target, sems.at[n])
            for n, (source, target) in enumerate(
                [
                    (load_hbm.at[mine], load_ref),
                    (series_hbm, series_ref),
                    (prec_hbm.at[:, mine], prec_ref),
                    (start_hbm.at[:, mine], start_ref),
                    (stop_hbm.at[:, mine], stop_ref),
                    (off_hbm.at[:, mine], off_ref),
                ]
            )
        ]
        for copy in copies:
            copy.start()
        for m in range(days // day_count):
            filt[m * day_count : (m + 1) * day_count, :] = gathered_ref[m]
        filtered = filt[...]
        carried = filtered * decay_ref[...]
        carried = jnp.concatenate([jnp.zeros((1, factors), F32), carried[:-1]], 0)
        total = filtered - carried
        for p in range(POWERS - 1):
            reach = 2**p
            later = jnp.concatenate([total[reach:], jnp.zeros((reach, factors), F32)], 0)
            total = total + product(later, (high_ref[p], low_ref[p]))
        far = (high_ref[POWERS - 1], low_ref[POWERS - 1])
        row = total[(blocks - 1) * stride :]
        work[(blocks - 1) * stride :, :] = row
        for b in reversed(range(blocks - 1)):
            row = total[b * stride : (b + 1) * stride] + product(row, far)
            work[b * stride : (b + 1) * stride, :] = row
        work[...] += carried
        for d in range(day_count):
            smooth_ref[d : d + 1, :] = work[pl.ds(me * day_count + d, 1), :]
        for copy in copies:
            copy.wait()
        fitted = lax.dot_general(
            work[...].astype(BF16), load_ref[...], (((1,), (1,)), ((), ())),
            preferred_element_type=F32,
        )
        day = lax.broadcasted_iota(jnp.int32, (days, 1), 0)
        active = activity(day, start_ref[...], stop_ref[...], off_ref[...])
        residual = (series_ref[...].astype(F32) - fitted) * jnp.sqrt(prec_ref[...])
        score_ref[...] = jnp.where(active, residual, 0.0).astype(BF16)

    return pl.pallas_call(
        kernel,
        in_specs=[smem()] + vmem(4) + hbm(6),
        out_specs=vmem(2),
        out_shape=[shape(day_count, factors), shape(days, own, dtype=BF16)],
        scratch_shapes=[
            pltpu.VMEM((days, factors), F32),
            pltpu.VMEM((days, factors), F32),
            pltpu.VMEM((days, own), BF16),
            pltpu.VMEM((own, factors), BF16),
            pltpu.VMEM((1, own), F32),
            pltpu.VMEM((1, own), jnp.int32),
            pltpu.VMEM((1, own), jnp.int32),
            pltpu.VMEM((1, own), jnp.int32),
            pltpu.SemaphoreType.DMA((6,)),
        ],
        compiler_params=params(),
        cost_estimate=cost(2 * days * own * factors, 2 << 20),
        name="finish",
    )(index, gathered, *powers, decay, series, loadings, *tables)


def local(series, loadings, precision, start_day, stop_day, off_day, decay, gain, smoother):
    devices = lax.axis_size("tm")
    place = lax.axis_index("tm").astype(jnp.int32)
    index = place[None]
    days = series.shape[0]
    day_count = days // devices
    factors = loadings.shape[1]
    tables = [a.reshape(1, -1) for a in (precision, start_day, stop_day, off_day)]
    decay = decay.reshape(1, factors)

    def swapped(array, distance):
        return lax.ppermute(array, "tm", [(i, i ^ distance) for i in range(devices)])

    partial = partial_drive(index, devices, series, loadings, tables)
    partial, first_day = lax.optimization_barrier((partial, index * day_count))
    terms = lax.all_to_all(partial, "tm", 0, 0, tiled=True)
    damped = damped_of(first_day, day_count, loadings, tables, decay)
    running, last, states, tail, packed = block_of(damped, terms, decay, gain)

    upper = (place & 1)[None]
    other = swapped(packed, 1)
    packed = combined(upper, last, tail, other)
    group = min(8, devices)
    pair = ((place % group) >> 1)[None]
    pieces = [packed] + [swapped(packed, 2 * m) for m in range(1, group // 2)]
    smoother, packed = lax.optimization_barrier((smoother, packed))
    powers = smoother_powers(smoother)
    nothing = jnp.zeros((1, factors), F32)
    nothing, powers = lax.optimization_barrier((nothing, powers))
    tail = advanced(pair, nothing, pieces)
    ahead = prefixed(pair, upper, pieces, other, running, last, states)

    state = nothing
    arrived = jnp.where(place // group == 1, swapped(tail, group), 0.0)
    for g in range(1, devices // group - 1):
        state = state + arrived
        moved = advanced(pair, state, pieces)
        pairs = [(g * group + j, (g + 1) * group + j) for j in range(group)]
        arrived = lax.ppermute(moved, "tm", pairs)

    own = filtered_of(state, arrived, *ahead)[None]
    gathered = lax.all_to_all(
        jnp.broadcast_to(own, (devices, day_count, factors)), "tm", 0, 0, tiled=True
    )
    return tuple(finish(index, day_count, gathered, powers, decay, series, loadings, tables))


def solution(mesh):
    in_specs = (
        P(None, ("spec", "tm")),
        P("spec", None),
        P("spec"),
        P("spec"),
        P("spec"),
        P("spec"),
        P(),
        P(),
        P(),
    )
    out_specs = (P("tm", "spec"), P(None, ("spec", "tm")))
    return jax.shard_map(local, mesh=mesh, in_specs=in_specs, out_specs=out_specs, check_vma=False)
```

```python
import jax
import jax.numpy as jnp
from jax import lax
from jax.experimental import pallas as pl
from jax.experimental.pallas import tpu as pltpu
from jax.sharding import PartitionSpec as P

F32 = jnp.float32
BF16 = jnp.bfloat16
VMEM = pltpu.MemorySpace.VMEM
SMEM = pltpu.MemorySpace.SMEM
HBM = pltpu.MemorySpace.HBM
POWERS = 5


def params(mebibytes=48, **more):
    return pltpu.CompilerParams(vmem_limit_bytes=mebibytes << 20, **more)


def cost(flops, nbytes):
    return pl.CostEstimate(flops=flops, bytes_accessed=nbytes, transcendentals=0)


def vmem(count):
    return [pl.BlockSpec(memory_space=VMEM)] * count


def hbm(count):
    return [pl.BlockSpec(memory_space=HBM)] * count


def smem():
    return pl.BlockSpec(memory_space=SMEM)


def shape(*dims, dtype=F32):
    return jax.ShapeDtypeStruct(dims, dtype)


def mul(a, b):
    return jnp.dot(a, b, preferred_element_type=F32)


def split(a):
    high = a.astype(BF16)
    return high, (a - high.astype(F32)).astype(BF16)


def product(a, b):
    high, low = split(a)
    rows = a.shape[0]
    if rows > 64:
        return mul(high, b[0]) + mul(low, b[0]) + mul(high, b[1])
    both = mul(jnp.concatenate([high, low], 0), b[0])
    return both[:rows] + both[rows:] + mul(high, b[1])


def eye(factors):
    dims = (factors, factors)
    return lax.broadcasted_iota(jnp.int32, dims, 0) == lax.broadcasted_iota(jnp.int32, dims, 1)


def activity(day, start, stop, off):
    return (day >= start) & (day < stop) & (lax.rem(day, 7) != off)


def partial_drive(index, devices, series, loadings, tables):
    days, own = series.shape
    day_count = days // devices
    factors = loadings.shape[1]

    def kernel(
        index_ref, series_hbm, load_hbm, prec_hbm, start_hbm, stop_hbm, off_hbm, out_ref,
        series_ref, load_ref, prec_ref, start_ref, stop_ref, off_ref, sems,
    ):
        first = pl.multiple_of(index_ref[0] * own, own)
        mine = pl.ds(first, own)
        copies = [
            pltpu.make_async_copy(source, target, sems.at[n])
            for n, (source, target) in enumerate(
                [
                    (prec_hbm.at[:, mine], prec_ref),
                    (start_hbm.at[:, mine], start_ref),
                    (stop_hbm.at[:, mine], stop_ref),
                    (off_hbm.at[:, mine], off_ref),
                    (series_hbm, series_ref),
                    (load_hbm.at[mine], load_ref),
                ]
            )
        ]
        for copy in copies:
            copy.start()
        day = lax.broadcasted_iota(jnp.int32, (days, 1), 0)
        for copy in copies[:5]:
            copy.wait()
        active = activity(day, start_ref[...], stop_ref[...], off_ref[...])
        weights = jnp.where(active, prec_ref[...], 0.0)
        weighted = (weights * series_ref[...].astype(F32)).astype(BF16)
        copies[5].wait()
        drive = mul(weighted, load_ref[...])
        for p in range(devices):
            out_ref[p] = drive[p * day_count : (p + 1) * day_count]

    return pl.pallas_call(
        kernel,
        in_specs=[smem()] + hbm(6),
        out_specs=pl.BlockSpec(memory_space=VMEM),
        out_shape=shape(devices, day_count, factors),
        scratch_shapes=[
            pltpu.VMEM((days, own), BF16),
            pltpu.VMEM((own, factors), BF16),
            pltpu.VMEM((1, own), F32),
            pltpu.VMEM((1, own), jnp.int32),
            pltpu.VMEM((1, own), jnp.int32),
            pltpu.VMEM((1, own), jnp.int32),
            pltpu.SemaphoreType.DMA((6,)),
        ],
        compiler_params=params(63),
        cost_estimate=cost(2 * days * own * factors, 1 << 20),
        name="partial_drive",
    )(index, series, loadings, *tables)


def damped_of(first_day, day_count, loadings, tables, decay):
    providers, factors = loadings.shape
    unit = providers // 16
    sizes = [unit, unit, 2 * unit, 4 * unit, 8 * unit]
    parts = [slice(sum(sizes[:n]), sum(sizes[: n + 1])) for n in range(len(sizes))]

    def kernel(
        day_ref, decay_ref, load_hbm, prec_hbm, start_hbm, stop_hbm, off_hbm, out_ref, acc, load_ref,
        prec_ref, start_ref, stop_ref, off_ref, sems,
    ):
        pairs = [
            (prec_hbm, prec_ref),
            (start_hbm, start_ref),
            (stop_hbm, stop_ref),
            (off_hbm, off_ref),
        ]
        pairs += [(load_hbm.at[part], load_ref.at[part]) for part in parts]
        copies = [
            pltpu.make_async_copy(source, target, sems.at[n])
            for n, (source, target) in enumerate(pairs)
        ]
        for copy in copies:
            copy.start()
        column = jnp.sum(jnp.where(eye(factors), decay_ref[...], 0.0), axis=1, keepdims=True)
        for copy in copies[:4]:
            copy.wait()
        for n, part in enumerate(parts):
            copies[4 + n].wait()
            block = load_ref[part]
            scaled = (block.T.astype(F32) * prec_ref[:, part]).astype(BF16)
            for d in range(day_count):
                active = activity(
                    day_ref[0] + d, start_ref[:, part], stop_ref[:, part], off_ref[:, part]
                )
                mask = active.astype(F32).astype(BF16)
                term = mul(scaled * mask, block)
                if n == 0:
                    acc[d] = term
                elif n < len(parts) - 1:
                    acc[d] += term
                else:
                    out_ref[d] = ((acc[d] + term) * column).astype(BF16)

    return pl.pallas_call(
        kernel,
        in_specs=[smem()] + vmem(1) + hbm(5),
        out_specs=pl.BlockSpec(memory_space=VMEM),
        out_shape=shape(day_count, factors, factors, dtype=BF16),
        scratch_shapes=[
            pltpu.VMEM((day_count, factors, factors), F32),
            pltpu.VMEM((providers, factors), BF16),
            pltpu.VMEM((1, providers), F32),
            pltpu.VMEM((1, providers), jnp.int32),
            pltpu.VMEM((1, providers), jnp.int32),
            pltpu.VMEM((1, providers), jnp.int32),
            pltpu.SemaphoreType.DMA((4 + len(parts),)),
        ],
        compiler_params=params(),
        cost_estimate=cost(2 * day_count * providers * factors * factors, 10 << 20),
        name="damped",
    )(first_day, decay, loadings, *tables)


PACKED = 16


def unpacked(packed_ref):
    factors = packed_ref.shape[1]
    rows = packed_ref[factors:].astype(F32)
    return packed_ref[:factors], rows[2:3] + rows[3:4], rows[0:1] + rows[1:2]


def pack(packed_ref, total, tail, same):
    factors = total.shape[0]
    packed_ref[:factors] = jnp.where(same, 0.0, total).astype(BF16)
    diag = jnp.sum(jnp.where(same, total, 0.0), axis=0, keepdims=True)
    rows = [*split(tail), *split(diag), jnp.zeros((PACKED - 4, factors), BF16)]
    packed_ref[factors:] = jnp.concatenate(rows, 0)


def through(a, rest, diag):
    rows = a.shape[0]
    high, low = split(a)
    if rows > 64:
        return mul(high, rest) + mul(low, rest) + a * diag
    both = mul(jnp.concatenate([high, low], 0), rest)
    return both[:rows] + both[rows:] + a * diag


def block_of(damped, terms, decay, gain):
    parts, day_count, factors = terms.shape

    def kernel(
        damped_ref, terms_ref, decay_ref, gain_ref, run_ref, last_ref, states_ref, tail_ref, packed_ref
    ):
        same = eye(factors)
        weights = gain_ref[...]
        dims = (((1,), (1,)), ((), ()))
        drive = terms_ref[0]
        for p in range(1, parts):
            drive = drive + terms_ref[p]
        high, low = split(drive)
        least = (drive - high.astype(F32) - low.astype(F32)).astype(BF16)
        offsets = sum(
            lax.dot_general(part, weights, dims, preferred_element_type=F32)
            for part in (high, low, least)
        )
        diagonal = jnp.where(same, decay_ref[...], 0.0)
        for d in range(day_count):
            step = diagonal - lax.dot_general(
                damped_ref[d], weights, dims, preferred_element_type=F32
            )
            if d == 0:
                running, state = step, offsets[0:1]
            else:
                run_ref[d - 1] = running
                step = split(step)
                running = product(running, step)
                state = product(state, step) + offsets[d : d + 1]
            states_ref[d : d + 1] = state
        last_ref[...] = running
        tail_ref[...] = state
        pack(packed_ref, running, state, same)

    return pl.pallas_call(
        kernel,
        in_specs=vmem(4),
        out_specs=vmem(5),
        out_shape=[
            shape(day_count - 1, factors, factors),
            shape(factors, factors),
            shape(day_count, factors),
            shape(1, factors),
            shape(factors + PACKED, factors, dtype=BF16),
        ],
        compiler_params=params(),
        cost_estimate=cost(50 * factors**3, 3 << 20),
        name="block",
    )(damped, terms, decay, gain)


def combined(upper, matrix, tail, other):
    factors = matrix.shape[0]

    def kernel(upper_ref, mine_ref, tail_ref, other_ref, packed_ref):
        same = eye(factors)
        rest, diag, other_tail = unpacked(other_ref)

        @pl.when(upper_ref[0] == 1)
        def _():
            mine = split(mine_ref[...])
            theirs = rest.astype(F32) + jnp.where(same, diag, 0.0)
            total = product(theirs, mine)
            pack(packed_ref, total, product(other_tail, mine) + tail_ref[...], same)

        @pl.when(upper_ref[0] == 0)
        def _():
            total = through(mine_ref[...], rest, diag)
            pack(packed_ref, total, through(tail_ref[...], rest, diag) + other_tail, same)

    return pl.pallas_call(
        kernel,
        in_specs=[smem()] + vmem(3),
        out_specs=pl.BlockSpec(memory_space=VMEM),
        out_shape=shape(factors + PACKED, factors, dtype=BF16),
        compiler_params=params(),
        cost_estimate=cost(6 * factors**3, 1 << 20),
        name="combined",
    )(upper, matrix, tail, other)


def advanced(pair, state, pieces, nothing=False):
    count = len(pieces)
    factors = pieces[0].shape[1]

    def kernel(pair_ref, state_ref, *refs):
        out_ref = refs[-1]
        out_ref[...] = state_ref[...]
        for turn in range(count):
            for m in range(count):

                @pl.when((pair_ref[0] ^ m) == turn)
                def _():
                    rest, diag, tail = unpacked(refs[m])
                    if nothing and turn == 0:
                        out_ref[...] = tail
                    else:
                        out_ref[...] = through(out_ref[...], rest, diag) + tail

    return pl.pallas_call(
        kernel,
        in_specs=[smem()] + vmem(count + 1),
        out_specs=pl.BlockSpec(memory_space=VMEM),
        out_shape=shape(1, factors),
        compiler_params=params(),
        cost_estimate=cost(12 * factors**2, 1 << 18),
        name="advanced",
    )(pair, state, *pieces)


def prefixed(pair, upper, pieces, other, running, last, states):
    day_count, factors = states.shape
    count = len(pieces)

    def kernel(pair_ref, upper_ref, *refs):
        other_ref, run_ref, last_ref, states_ref = refs[count : count + 4]
        high_ref, low_ref, add_ref, work, tail = refs[count + 4 :]
        work[...] = jnp.where(eye(factors), 1.0, 0.0)
        tail[...] = jnp.zeros_like(tail)

        def follow(rest, diag, add):
            work[...] = through(work[...], rest, diag)
            tail[...] = through(tail[...], rest, diag) + add

        for turn in range(count - 1):
            for m in range(1, count):

                @pl.when(((pair_ref[0] ^ m) == turn) & (pair_ref[0] > turn))
                def _():
                    follow(*unpacked(refs[m]))

        @pl.when(upper_ref[0] == 1)
        def _():
            follow(*unpacked(other_ref))

        for d in range(day_count):
            step = split(run_ref[d] if d < day_count - 1 else last_ref[...])
            place = slice(d * factors, (d + 1) * factors)
            high_ref[:, place], low_ref[:, place] = split(product(work[...], step))
            add_ref[:, place] = product(tail[...], step) + states_ref[d : d + 1]

    wide = day_count * factors
    return pl.pallas_call(
        kernel,
        in_specs=[smem()] * 2 + vmem(count + 4),
        out_specs=vmem(3),
        out_shape=[
            shape(factors, wide, dtype=BF16),
            shape(factors, wide, dtype=BF16),
            shape(1, wide),
        ],
        scratch_shapes=[pltpu.VMEM((factors, factors), F32), pltpu.VMEM((1, factors), F32)],
        compiler_params=params(),
        cost_estimate=cost(36 * factors**3, 3 << 20),
        name="prefixed",
    )(pair, upper, *pieces, other, running, last, states)


def filtered_of(state, arrived, high, low, add):
    factors, wide = high.shape
    day_count = wide // factors

    def kernel(state_ref, arrived_ref, high_ref, low_ref, add_ref, out_ref):
        entering = state_ref[...] + arrived_ref[...]
        row = product(entering, (high_ref[...], low_ref[...])) + add_ref[...]
        for d in range(day_count):
            out_ref[d : d + 1] = row[:, d * factors : (d + 1) * factors]

    return pl.pallas_call(
        kernel,
        in_specs=vmem(5),
        out_specs=pl.BlockSpec(memory_space=VMEM),
        out_shape=shape(day_count, factors),
        compiler_params=params(),
        cost_estimate=cost(6 * factors * wide, 1 << 20),
        name="filtered",
    )(state, arrived, high, low, add)


def prepared(index, days, own, smoother, loadings, tables):
    factors = smoother.shape[0]

    def kernel(
        index_ref, in_ref, load_hbm, prec_hbm, start_hbm, stop_hbm, off_hbm, high_ref, low_ref,
        load_ref, scale_ref, prec_ref, start_ref, stop_ref, off_ref, sems,
    ):
        mine = pl.ds(pl.multiple_of(index_ref[0] * own, own), own)
        copies = [
            pltpu.make_async_copy(source, target, sems.at[n])
            for n, (source, target) in enumerate(
                [
                    (prec_hbm.at[:, mine], prec_ref),
                    (start_hbm.at[:, mine], start_ref),
                    (stop_hbm.at[:, mine], stop_ref),
                    (off_hbm.at[:, mine], off_ref),
                    (load_hbm.at[mine], load_ref),
                ]
            )
        ]
        for copy in copies:
            copy.start()
        power = in_ref[...].T
        for p in range(POWERS):
            parts = split(power)
            high_ref[p], low_ref[p] = parts
            if p < POWERS - 1:
                power = product(power, parts)
        for copy in copies:
            copy.wait()
        day = lax.broadcasted_iota(jnp.int32, (days, 1), 0)
        active = activity(day, start_ref[...], stop_ref[...], off_ref[...])
        scale_ref[...] = jnp.where(active, jnp.sqrt(prec_ref[...]), 0.0)

    return pl.pallas_call(
        kernel,
        in_specs=[smem()] + vmem(1) + hbm(5),
        out_specs=vmem(4),
        out_shape=[
            shape(POWERS, factors, factors, dtype=BF16),
            shape(POWERS, factors, factors, dtype=BF16),
            shape(own, factors, dtype=BF16),
            shape(days, own),
        ],
        scratch_shapes=[
            pltpu.VMEM((1, own), F32),
            pltpu.VMEM((1, own), jnp.int32),
            pltpu.VMEM((1, own), jnp.int32),
            pltpu.VMEM((1, own), jnp.int32),
            pltpu.SemaphoreType.DMA((5,)),
        ],
        compiler_params=params(),
        cost_estimate=cost(24 * factors**3, 3 << 20),
        name="prepared",
    )(index, smoother, loadings, *tables)


def finish(index, day_count, gathered, ready, decay, series):
    days, own = series.shape
    factors = decay.shape[1]
    stride = 2 ** (POWERS - 1)
    blocks = days // stride

    def kernel(
        index_ref, gathered_ref, high_ref, low_ref, load_ref, scale_ref, decay_ref, series_ref,
        smooth_ref, score_ref, filt, work,
    ):
        me = index_ref[0]
        for m in range(days // day_count):
            filt[m * day_count : (m + 1) * day_count, :] = gathered_ref[m]
        filtered = filt[...]
        carried = filtered * decay_ref[...]
        carried = jnp.concatenate([jnp.zeros((1, factors), F32), carried[:-1]], 0)
        total = filtered - carried
        for p in range(POWERS - 1):
            reach = 2**p
            later = jnp.concatenate([total[reach:], jnp.zeros((reach, factors), F32)], 0)
            total = total + product(later, (high_ref[p], low_ref[p]))
        far = (high_ref[POWERS - 1], low_ref[POWERS - 1])
        row = total[(blocks - 1) * stride :]
        work[(blocks - 1) * stride :, :] = row
        for b in reversed(range(blocks - 1)):
            row = total[b * stride : (b + 1) * stride] + product(row, far)
            work[b * stride : (b + 1) * stride, :] = row
        work[...] += carried
        for d in range(day_count):
            smooth_ref[d : d + 1, :] = work[pl.ds(me * day_count + d, 1), :]
        fitted = lax.dot_general(
            work[...].astype(BF16), load_ref[...], (((1,), (1,)), ((), ())),
            preferred_element_type=F32,
        )
        residual = series_ref[...].astype(F32) - fitted
        score_ref[...] = (residual * scale_ref[...]).astype(BF16)

    return pl.pallas_call(
        kernel,
        in_specs=[smem()] + vmem(7),
        out_specs=vmem(2),
        out_shape=[shape(day_count, factors), shape(days, own, dtype=BF16)],
        scratch_shapes=[
            pltpu.VMEM((days, factors), F32),
            pltpu.VMEM((days, factors), F32),
        ],
        compiler_params=params(),
        cost_estimate=cost(2 * days * own * factors, 2 << 20),
        name="finish",
    )(index, gathered, *ready, decay, series)


def local(series, loadings, precision, start_day, stop_day, off_day, decay, gain, smoother):
    devices = lax.axis_size("tm")
    place = lax.axis_index("tm").astype(jnp.int32)
    index = place[None]
    days = series.shape[0]
    day_count = days // devices
    factors = loadings.shape[1]
    tables = [a.reshape(1, -1) for a in (precision, start_day, stop_day, off_day)]
    decay = decay.reshape(1, factors)

    def swapped(array, distance):
        return lax.ppermute(array, "tm", [(i, i ^ distance) for i in range(devices)])

    partial = partial_drive(index, devices, series, loadings, tables)
    partial, first_day = lax.optimization_barrier((partial, index * day_count))
    terms = lax.all_to_all(partial, "tm", 0, 0, tiled=True)
    damped = damped_of(first_day, day_count, loadings, tables, decay)
    running, last, states, tail, packed = block_of(damped, terms, decay, gain)

    upper = (place & 1)[None]
    other = swapped(packed, 1)
    packed = combined(upper, last, tail, other)
    group = min(8, devices)
    pair = ((place % group) >> 1)[None]
    pieces = [packed] + [swapped(packed, 2 * m) for m in range(1, group // 2)]
    smoother, packed = lax.optimization_barrier((smoother, packed))
    ready = prepared(index, days, series.shape[1], smoother, loadings, tables)
    nothing = jnp.zeros((1, factors), F32)
    nothing, ready = lax.optimization_barrier((nothing, ready))
    tail = advanced(pair, nothing, pieces, True)
    ahead = prefixed(pair, upper, pieces, other, running, last, states)

    state = nothing
    arrived = jnp.where(place // group == 1, swapped(tail, group), 0.0)
    for g in range(1, devices // group - 1):
        state = state + arrived
        moved = advanced(pair, state, pieces)
        pairs = [(g * group + j, (g + 1) * group + j) for j in range(group)]
        arrived = lax.ppermute(moved, "tm", pairs)

    own = filtered_of(state, arrived, *ahead)[None]
    gathered = lax.all_to_all(
        jnp.broadcast_to(own, (devices, day_count, factors)), "tm", 0, 0, tiled=True
    )
    return tuple(finish(index, day_count, gathered, ready, decay, series))


def solution(mesh):
    in_specs = (
        P(None, ("spec", "tm")),
        P("spec", None),
        P("spec"),
        P("spec"),
        P("spec"),
        P("spec"),
        P(),
        P(),
        P(),
    )
    out_specs = (P("tm", "spec"), P(None, ("spec", "tm")))
    return jax.shard_map(local, mesh=mesh, in_specs=in_specs, out_specs=out_specs, check_vma=False)
```

```python
import itertools

import jax
import jax.numpy as jnp
from jax import lax
from jax.experimental import pallas as pl
from jax.experimental.pallas import tpu as pltpu
from jax.sharding import PartitionSpec as P

F32 = jnp.float32
BF16 = jnp.bfloat16
VMEM = pltpu.MemorySpace.VMEM
SMEM = pltpu.MemorySpace.SMEM
HBM = pltpu.MemorySpace.HBM
POWERS = 5


def params(mebibytes=48, **more):
    return pltpu.CompilerParams(vmem_limit_bytes=mebibytes << 20, **more)


def cost(flops, nbytes):
    return pl.CostEstimate(flops=flops, bytes_accessed=nbytes, transcendentals=0)


def vmem(count):
    return [pl.BlockSpec(memory_space=VMEM)] * count


def hbm(count):
    return [pl.BlockSpec(memory_space=HBM)] * count


def smem():
    return pl.BlockSpec(memory_space=SMEM)


def shape(*dims, dtype=F32):
    return jax.ShapeDtypeStruct(dims, dtype)


def mul(a, b):
    return jnp.dot(a, b, preferred_element_type=F32)


def split(a):
    high = a.astype(BF16)
    return high, (a - high.astype(F32)).astype(BF16)


def product(a, b):
    high, low = split(a)
    rows = a.shape[0]
    if rows > 64:
        return mul(high, b[0]) + mul(low, b[0]) + mul(high, b[1])
    both = mul(jnp.concatenate([high, low], 0), b[0])
    return both[:rows] + both[rows:] + mul(high, b[1])


def eye(factors):
    dims = (factors, factors)
    return lax.broadcasted_iota(jnp.int32, dims, 0) == lax.broadcasted_iota(jnp.int32, dims, 1)


def activity(day, start, stop, off):
    return (day >= start) & (day < stop) & (lax.rem(day, 7) != off)


def partial_drive(index, devices, series, loadings, tables):
    days, own = series.shape
    day_count = days // devices
    factors = loadings.shape[1]

    def kernel(
        index_ref, series_hbm, load_hbm, prec_hbm, start_hbm, stop_hbm, off_hbm, out_ref,
        series_ref, load_ref, prec_ref, start_ref, stop_ref, off_ref, sems,
    ):
        first = pl.multiple_of(index_ref[0] * own, own)
        mine = pl.ds(first, own)
        copies = [
            pltpu.make_async_copy(source, target, sems.at[n])
            for n, (source, target) in enumerate(
                [
                    (prec_hbm.at[:, mine], prec_ref),
                    (start_hbm.at[:, mine], start_ref),
                    (stop_hbm.at[:, mine], stop_ref),
                    (off_hbm.at[:, mine], off_ref),
                    (series_hbm, series_ref),
                    (load_hbm.at[mine], load_ref),
                ]
            )
        ]
        for copy in copies:
            copy.start()
        day = lax.broadcasted_iota(jnp.int32, (days, 1), 0)
        for copy in copies[:5]:
            copy.wait()
        active = activity(day, start_ref[...], stop_ref[...], off_ref[...])
        weights = jnp.where(active, prec_ref[...], 0.0)
        weighted = (weights * series_ref[...].astype(F32)).astype(BF16)
        copies[5].wait()
        drive = mul(weighted, load_ref[...])
        for p in range(devices):
            out_ref[p] = drive[p * day_count : (p + 1) * day_count]

    return pl.pallas_call(
        kernel,
        in_specs=[smem()] + hbm(6),
        out_specs=pl.BlockSpec(memory_space=VMEM),
        out_shape=shape(devices, day_count, factors),
        scratch_shapes=[
            pltpu.VMEM((days, own), BF16),
            pltpu.VMEM((own, factors), BF16),
            pltpu.VMEM((1, own), F32),
            pltpu.VMEM((1, own), jnp.int32),
            pltpu.VMEM((1, own), jnp.int32),
            pltpu.VMEM((1, own), jnp.int32),
            pltpu.SemaphoreType.DMA((6,)),
        ],
        compiler_params=params(63),
        cost_estimate=cost(2 * days * own * factors, 1 << 20),
        name="partial_drive",
    )(index, series, loadings, *tables)


def damped_of(first_day, day_count, loadings, tables, decay):
    providers, factors = loadings.shape
    unit = providers // 16
    sizes = [unit, unit, 2 * unit, 4 * unit, 8 * unit]
    parts = [slice(sum(sizes[:n]), sum(sizes[: n + 1])) for n in range(len(sizes))]

    def kernel(
        day_ref, decay_ref, load_hbm, prec_hbm, start_hbm, stop_hbm, off_hbm, out_ref, acc, load_ref,
        prec_ref, start_ref, stop_ref, off_ref, sems,
    ):
        pairs = [
            (prec_hbm, prec_ref),
            (start_hbm, start_ref),
            (stop_hbm, stop_ref),
            (off_hbm, off_ref),
        ]
        pairs += [(load_hbm.at[part], load_ref.at[part]) for part in parts]
        copies = [
            pltpu.make_async_copy(source, target, sems.at[n])
            for n, (source, target) in enumerate(pairs)
        ]
        for copy in copies:
            copy.start()
        column = jnp.sum(jnp.where(eye(factors), decay_ref[...], 0.0), axis=1, keepdims=True)
        for copy in copies[:4]:
            copy.wait()
        for n, part in enumerate(parts):
            copies[4 + n].wait()
            block = load_ref[part]
            scaled = (block.T.astype(F32) * prec_ref[:, part]).astype(BF16)
            for d in range(day_count):
                active = activity(
                    day_ref[0] + d, start_ref[:, part], stop_ref[:, part], off_ref[:, part]
                )
                mask = active.astype(F32).astype(BF16)
                term = mul(scaled * mask, block)
                if n == 0:
                    acc[d] = term
                elif n < len(parts) - 1:
                    acc[d] += term
                else:
                    out_ref[d] = ((acc[d] + term) * column).astype(BF16)

    return pl.pallas_call(
        kernel,
        in_specs=[smem()] + vmem(1) + hbm(5),
        out_specs=pl.BlockSpec(memory_space=VMEM),
        out_shape=shape(day_count, factors, factors, dtype=BF16),
        scratch_shapes=[
            pltpu.VMEM((day_count, factors, factors), F32),
            pltpu.VMEM((providers, factors), BF16),
            pltpu.VMEM((1, providers), F32),
            pltpu.VMEM((1, providers), jnp.int32),
            pltpu.VMEM((1, providers), jnp.int32),
            pltpu.VMEM((1, providers), jnp.int32),
            pltpu.SemaphoreType.DMA((4 + len(parts),)),
        ],
        compiler_params=params(),
        cost_estimate=cost(2 * day_count * providers * factors * factors, 10 << 20),
        name="damped",
    )(first_day, decay, loadings, *tables)


PACKED = 16


def unpacked(packed_ref):
    factors = packed_ref.shape[1]
    rows = packed_ref[factors:].astype(F32)
    return (packed_ref[:factors],), rows[2:3] + rows[3:4], rows[0:1] + rows[1:2]


def joined(top_ref, bottom_ref):
    half = top_ref.shape[0] - PACKED
    rows = top_ref[half:].astype(F32)
    return (top_ref[:half], bottom_ref[:half]), rows[2:3] + rows[3:4], rows[0:1] + rows[1:2]


def pack(refs, total, tail, same):
    factors = total.shape[0]
    half = factors // len(refs)
    rest = jnp.where(same, 0.0, total).astype(BF16)
    diag = jnp.sum(jnp.where(same, total, 0.0), axis=0, keepdims=True)
    rows = [*split(tail), *split(diag), jnp.zeros((PACKED - 4, factors), BF16)]
    for n, ref in enumerate(refs):
        ref[:half] = rest[n * half : (n + 1) * half]
        ref[half:] = jnp.concatenate(rows, 0)


def through(a, rests, diag):
    rows = a.shape[0]
    high, low = split(a)
    depth = a.shape[1] // len(rests)

    def times(x):
        return sum(mul(x[:, n * depth : (n + 1) * depth], r) for n, r in enumerate(rests))

    if rows > 64:
        return times(high) + times(low) + a * diag
    both = times(jnp.concatenate([high, low], 0))
    return both[:rows] + both[rows:] + a * diag


def block_of(damped, terms, decay, gain):
    parts, day_count, factors = terms.shape

    def kernel(
        damped_ref, terms_ref, decay_ref, gain_ref, run_ref, last_ref, states_ref, tail_ref, packed_ref
    ):
        same = eye(factors)
        weights = gain_ref[...]
        dims = (((1,), (1,)), ((), ()))
        drive = terms_ref[0]
        for p in range(1, parts):
            drive = drive + terms_ref[p]
        high, low = split(drive)
        least = (drive - high.astype(F32) - low.astype(F32)).astype(BF16)
        offsets = sum(
            lax.dot_general(part, weights, dims, preferred_element_type=F32)
            for part in (high, low, least)
        )
        diagonal = jnp.where(same, decay_ref[...], 0.0)
        for d in range(day_count):
            step = diagonal - lax.dot_general(
                damped_ref[d], weights, dims, preferred_element_type=F32
            )
            if d == 0:
                running, state = step, offsets[0:1]
            else:
                run_ref[d - 1] = running
                step = split(step)
                running = product(running, step)
                state = product(state, step) + offsets[d : d + 1]
            states_ref[d : d + 1] = state
        last_ref[...] = running
        tail_ref[...] = state
        pack([packed_ref], running, state, same)

    return pl.pallas_call(
        kernel,
        in_specs=vmem(4),
        out_specs=vmem(5),
        out_shape=[
            shape(day_count - 1, factors, factors),
            shape(factors, factors),
            shape(day_count, factors),
            shape(1, factors),
            shape(factors + PACKED, factors, dtype=BF16),
        ],
        compiler_params=params(),
        cost_estimate=cost(50 * factors**3, 3 << 20),
        name="block",
    )(damped, terms, decay, gain)


def combined(upper, matrix, tail, other):
    factors = matrix.shape[0]

    def kernel(upper_ref, mine_ref, tail_ref, other_ref, sent_ref, kept_ref):
        same = eye(factors)
        rest, diag, other_tail = unpacked(other_ref)

        @pl.when(upper_ref[0] == 1)
        def _():
            mine = split(mine_ref[...])
            theirs = rest[0].astype(F32) + jnp.where(same, diag, 0.0)
            total = product(theirs, mine)
            pack([kept_ref, sent_ref], total, product(other_tail, mine) + tail_ref[...], same)

        @pl.when(upper_ref[0] == 0)
        def _():
            total = through(mine_ref[...], rest, diag)
            tail = through(tail_ref[...], rest, diag) + other_tail
            pack([sent_ref, kept_ref], total, tail, same)

    return pl.pallas_call(
        kernel,
        in_specs=[smem()] + vmem(3),
        out_specs=vmem(2),
        out_shape=[shape(factors // 2 + PACKED, factors, dtype=BF16)] * 2,
        compiler_params=params(),
        cost_estimate=cost(6 * factors**3, 1 << 20),
        name="combined",
    )(upper, matrix, tail, other)


def advanced(pair, upper, state, pieces, nothing=False):
    count = len(pieces)
    factors = state.shape[1]

    def kernel(pair_ref, upper_ref, state_ref, *refs):
        out_ref = refs[-1]
        out_ref[...] = state_ref[...]
        for turn in range(count):
            for m, core in itertools.product(range(count), range(2)):

                @pl.when(((pair_ref[0] ^ m) == turn) & (upper_ref[0] == core))
                def _():
                    rest, diag, tail = joined(refs[2 * m + core], refs[2 * m + 1 - core])
                    if nothing and turn == 0:
                        out_ref[...] = tail
                    else:
                        out_ref[...] = through(out_ref[...], rest, diag) + tail

    return pl.pallas_call(
        kernel,
        in_specs=[smem()] * 2 + vmem(2 * count + 1),
        out_specs=pl.BlockSpec(memory_space=VMEM),
        out_shape=shape(1, factors),
        compiler_params=params(),
        cost_estimate=cost(12 * factors**2, 1 << 18),
        name="advanced",
    )(pair, upper, state, *[a for piece in pieces for a in piece])


def prefixed(pair, upper, pieces, other, running, last, states):
    day_count, factors = states.shape
    count = len(pieces)

    def kernel(pair_ref, upper_ref, *refs):
        other_ref, run_ref, last_ref, states_ref = refs[2 * count : 2 * count + 4]
        high_ref, low_ref, add_ref, work, tail = refs[2 * count + 4 :]
        work[...] = jnp.where(eye(factors), 1.0, 0.0)
        tail[...] = jnp.zeros_like(tail)

        def follow(rest, diag, add):
            work[...] = through(work[...], rest, diag)
            tail[...] = through(tail[...], rest, diag) + add

        for turn in range(count - 1):
            for m, core in itertools.product(range(1, count), range(2)):
                now = ((pair_ref[0] ^ m) == turn) & (pair_ref[0] > turn)

                @pl.when(now & (upper_ref[0] == core))
                def _():
                    follow(*joined(refs[2 * m + core], refs[2 * m + 1 - core]))

        @pl.when(upper_ref[0] == 1)
        def _():
            follow(*unpacked(other_ref))

        for d in range(day_count):
            step = split(run_ref[d] if d < day_count - 1 else last_ref[...])
            place = slice(d * factors, (d + 1) * factors)
            high_ref[:, place], low_ref[:, place] = split(product(work[...], step))
            add_ref[:, place] = product(tail[...], step) + states_ref[d : d + 1]

    wide = day_count * factors
    return pl.pallas_call(
        kernel,
        in_specs=[smem()] * 2 + vmem(2 * count + 4),
        out_specs=vmem(3),
        out_shape=[
            shape(factors, wide, dtype=BF16),
            shape(factors, wide, dtype=BF16),
            shape(1, wide),
        ],
        scratch_shapes=[pltpu.VMEM((factors, factors), F32), pltpu.VMEM((1, factors), F32)],
        compiler_params=params(),
        cost_estimate=cost(36 * factors**3, 3 << 20),
        name="prefixed",
    )(pair, upper, *[a for piece in pieces for a in piece], other, running, last, states)


def filtered_of(state, arrived, high, low, add):
    factors, wide = high.shape
    day_count = wide // factors

    def kernel(state_ref, arrived_ref, high_ref, low_ref, add_ref, out_ref):
        entering = state_ref[...] + arrived_ref[...]
        row = product(entering, (high_ref[...], low_ref[...])) + add_ref[...]
        for d in range(day_count):
            out_ref[d : d + 1] = row[:, d * factors : (d + 1) * factors]

    return pl.pallas_call(
        kernel,
        in_specs=vmem(5),
        out_specs=pl.BlockSpec(memory_space=VMEM),
        out_shape=shape(day_count, factors),
        compiler_params=params(),
        cost_estimate=cost(6 * factors * wide, 1 << 20),
        name="filtered",
    )(state, arrived, high, low, add)


def prepared(index, days, own, smoother, loadings, tables):
    factors = smoother.shape[0]

    def kernel(
        index_ref, in_ref, load_hbm, prec_hbm, start_hbm, stop_hbm, off_hbm, high_ref, low_ref,
        load_ref, scale_ref, prec_ref, start_ref, stop_ref, off_ref, sems,
    ):
        mine = pl.ds(pl.multiple_of(index_ref[0] * own, own), own)
        copies = [
            pltpu.make_async_copy(source, target, sems.at[n])
            for n, (source, target) in enumerate(
                [
                    (prec_hbm.at[:, mine], prec_ref),
                    (start_hbm.at[:, mine], start_ref),
                    (stop_hbm.at[:, mine], stop_ref),
                    (off_hbm.at[:, mine], off_ref),
                    (load_hbm.at[mine], load_ref),
                ]
            )
        ]
        for copy in copies:
            copy.start()
        power = in_ref[...].T
        for p in range(POWERS):
            parts = split(power)
            high_ref[p], low_ref[p] = parts
            if p < POWERS - 1:
                power = product(power, parts)
        for copy in copies:
            copy.wait()
        day = lax.broadcasted_iota(jnp.int32, (days, 1), 0)
        active = activity(day, start_ref[...], stop_ref[...], off_ref[...])
        scale_ref[...] = jnp.where(active, jnp.sqrt(prec_ref[...]), 0.0)

    return pl.pallas_call(
        kernel,
        in_specs=[smem()] + vmem(1) + hbm(5),
        out_specs=vmem(4),
        out_shape=[
            shape(POWERS, factors, factors, dtype=BF16),
            shape(POWERS, factors, factors, dtype=BF16),
            shape(own, factors, dtype=BF16),
            shape(days, own),
        ],
        scratch_shapes=[
            pltpu.VMEM((1, own), F32),
            pltpu.VMEM((1, own), jnp.int32),
            pltpu.VMEM((1, own), jnp.int32),
            pltpu.VMEM((1, own), jnp.int32),
            pltpu.SemaphoreType.DMA((5,)),
        ],
        compiler_params=params(),
        cost_estimate=cost(24 * factors**3, 3 << 20),
        name="prepared",
    )(index, smoother, loadings, *tables)


def finish(index, day_count, gathered, ready, decay, series):
    days, own = series.shape
    factors = decay.shape[1]
    stride = 2 ** (POWERS - 1)
    blocks = days // stride

    def kernel(
        index_ref, gathered_ref, high_ref, low_ref, load_ref, scale_ref, decay_ref, series_ref,
        smooth_ref, score_ref, filt, work,
    ):
        me = index_ref[0]
        for m in range(days // day_count):
            filt[m * day_count : (m + 1) * day_count, :] = gathered_ref[m]
        filtered = filt[...]
        carried = filtered * decay_ref[...]
        carried = jnp.concatenate([jnp.zeros((1, factors), F32), carried[:-1]], 0)
        total = filtered - carried
        for p in range(POWERS - 1):
            reach = 2**p
            later = jnp.concatenate([total[reach:], jnp.zeros((reach, factors), F32)], 0)
            total = total + product(later, (high_ref[p], low_ref[p]))
        far = (high_ref[POWERS - 1], low_ref[POWERS - 1])
        row = total[(blocks - 1) * stride :]
        work[(blocks - 1) * stride :, :] = row
        for b in reversed(range(blocks - 1)):
            row = total[b * stride : (b + 1) * stride] + product(row, far)
            work[b * stride : (b + 1) * stride, :] = row
        work[...] += carried
        for d in range(day_count):
            smooth_ref[d : d + 1, :] = work[pl.ds(me * day_count + d, 1), :]
        fitted = lax.dot_general(
            work[...].astype(BF16), load_ref[...], (((1,), (1,)), ((), ())),
            preferred_element_type=F32,
        )
        residual = series_ref[...].astype(F32) - fitted
        score_ref[...] = (residual * scale_ref[...]).astype(BF16)

    return pl.pallas_call(
        kernel,
        in_specs=[smem()] + vmem(7),
        out_specs=vmem(2),
        out_shape=[shape(day_count, factors), shape(days, own, dtype=BF16)],
        scratch_shapes=[
            pltpu.VMEM((days, factors), F32),
            pltpu.VMEM((days, factors), F32),
        ],
        compiler_params=params(),
        cost_estimate=cost(2 * days * own * factors, 2 << 20),
        name="finish",
    )(index, gathered, *ready, decay, series)


def local(series, loadings, precision, start_day, stop_day, off_day, decay, gain, smoother):
    devices = lax.axis_size("tm")
    place = lax.axis_index("tm").astype(jnp.int32)
    index = place[None]
    days = series.shape[0]
    day_count = days // devices
    factors = loadings.shape[1]
    tables = [a.reshape(1, -1) for a in (precision, start_day, stop_day, off_day)]
    decay = decay.reshape(1, factors)

    def swapped(array, distance):
        return lax.ppermute(array, "tm", [(i, i ^ distance) for i in range(devices)])

    partial = partial_drive(index, devices, series, loadings, tables)
    partial, first_day = lax.optimization_barrier((partial, index * day_count))
    terms = lax.all_to_all(partial, "tm", 0, 0, tiled=True)
    damped = damped_of(first_day, day_count, loadings, tables, decay)
    running, last, states, tail, packed = block_of(damped, terms, decay, gain)

    upper = (place & 1)[None]
    other = swapped(packed, 1)
    sent, kept = combined(upper, last, tail, other)
    group = min(8, devices)
    pair = ((place % group) >> 1)[None]
    came = [swapped(sent, 2 * m) for m in range(1, group // 2)]
    pieces = [(sent, kept)] + [(half, swapped(half, 1)) for half in came]
    smoother, sent = lax.optimization_barrier((smoother, sent))
    ready = prepared(index, days, series.shape[1], smoother, loadings, tables)
    nothing = jnp.zeros((1, factors), F32)
    nothing, ready = lax.optimization_barrier((nothing, ready))
    tail = advanced(pair, upper, nothing, pieces, True)
    ahead = prefixed(pair, upper, pieces, other, running, last, states)

    state = nothing
    arrived = jnp.where(place // group == 1, swapped(tail, group), 0.0)
    for g in range(1, devices // group - 1):
        state = state + arrived
        moved = advanced(pair, upper, state, pieces)
        pairs = [(g * group + j, (g + 1) * group + j) for j in range(group)]
        arrived = lax.ppermute(moved, "tm", pairs)

    own = filtered_of(state, arrived, *ahead)[None]
    gathered = lax.all_to_all(
        jnp.broadcast_to(own, (devices, day_count, factors)), "tm", 0, 0, tiled=True
    )
    return tuple(finish(index, day_count, gathered, ready, decay, series))


def solution(mesh):
    in_specs = (
        P(None, ("spec", "tm")),
        P("spec", None),
        P("spec"),
        P("spec"),
        P("spec"),
        P("spec"),
        P(),
        P(),
        P(),
    )
    out_specs = (P("tm", "spec"), P(None, ("spec", "tm")))
    return jax.shard_map(local, mesh=mesh, in_specs=in_specs, out_specs=out_specs, check_vma=False)
```

```python
import itertools

import jax
import jax.numpy as jnp
from jax import lax
from jax.experimental import pallas as pl
from jax.experimental.pallas import tpu as pltpu
from jax.sharding import PartitionSpec as P

F32 = jnp.float32
BF16 = jnp.bfloat16
VMEM = pltpu.MemorySpace.VMEM
SMEM = pltpu.MemorySpace.SMEM
HBM = pltpu.MemorySpace.HBM
POWERS = 5


def params(mebibytes=48, **more):
    return pltpu.CompilerParams(vmem_limit_bytes=mebibytes << 20, **more)


def cost(flops, nbytes):
    return pl.CostEstimate(flops=flops, bytes_accessed=nbytes, transcendentals=0)


def vmem(count):
    return [pl.BlockSpec(memory_space=VMEM)] * count


def hbm(count):
    return [pl.BlockSpec(memory_space=HBM)] * count


def smem():
    return pl.BlockSpec(memory_space=SMEM)


def shape(*dims, dtype=F32):
    return jax.ShapeDtypeStruct(dims, dtype)


def mul(a, b):
    return jnp.dot(a, b, preferred_element_type=F32)


def split(a):
    high = a.astype(BF16)
    return high, (a - high.astype(F32)).astype(BF16)


def product(a, b):
    high, low = split(a)
    rows = a.shape[0]
    if rows > 64:
        return mul(high, b[0]) + mul(low, b[0]) + mul(high, b[1])
    both = mul(jnp.concatenate([high, low], 0), b[0])
    return both[:rows] + both[rows:] + mul(high, b[1])


def eye(factors):
    dims = (factors, factors)
    return lax.broadcasted_iota(jnp.int32, dims, 0) == lax.broadcasted_iota(jnp.int32, dims, 1)


def activity(day, start, stop, off):
    return (day >= start) & (day < stop) & (lax.rem(day, 7) != off)


def partial_drive(index, devices, series, loadings, tables):
    days, own = series.shape
    day_count = days // devices
    factors = loadings.shape[1]

    def kernel(
        index_ref, series_hbm, load_hbm, prec_hbm, start_hbm, stop_hbm, off_hbm, out_ref,
        series_ref, load_ref, prec_ref, start_ref, stop_ref, off_ref, sems,
    ):
        first = pl.multiple_of(index_ref[0] * own, own)
        mine = pl.ds(first, own)
        copies = [
            pltpu.make_async_copy(source, target, sems.at[n])
            for n, (source, target) in enumerate(
                [
                    (prec_hbm.at[:, mine], prec_ref),
                    (start_hbm.at[:, mine], start_ref),
                    (stop_hbm.at[:, mine], stop_ref),
                    (off_hbm.at[:, mine], off_ref),
                    (series_hbm, series_ref),
                    (load_hbm.at[mine], load_ref),
                ]
            )
        ]
        for copy in copies:
            copy.start()
        day = lax.broadcasted_iota(jnp.int32, (days, 1), 0)
        for copy in copies[:5]:
            copy.wait()
        active = activity(day, start_ref[...], stop_ref[...], off_ref[...])
        weights = jnp.where(active, prec_ref[...], 0.0)
        weighted = (weights * series_ref[...].astype(F32)).astype(BF16)
        copies[5].wait()
        drive = mul(weighted, load_ref[...])
        for p in range(devices):
            out_ref[p] = drive[p * day_count : (p + 1) * day_count]

    return pl.pallas_call(
        kernel,
        in_specs=[smem()] + hbm(6),
        out_specs=pl.BlockSpec(memory_space=VMEM),
        out_shape=shape(devices, day_count, factors),
        scratch_shapes=[
            pltpu.VMEM((days, own), BF16),
            pltpu.VMEM((own, factors), BF16),
            pltpu.VMEM((1, own), F32),
            pltpu.VMEM((1, own), jnp.int32),
            pltpu.VMEM((1, own), jnp.int32),
            pltpu.VMEM((1, own), jnp.int32),
            pltpu.SemaphoreType.DMA((6,)),
        ],
        compiler_params=params(63),
        cost_estimate=cost(2 * days * own * factors, 1 << 20),
        name="partial_drive",
    )(index, series, loadings, *tables)


def damped_of(first_day, day_count, loadings, tables, decay):
    providers, factors = loadings.shape
    unit = providers // 16
    sizes = [unit, unit, 2 * unit, 4 * unit, 8 * unit]
    parts = [slice(sum(sizes[:n]), sum(sizes[: n + 1])) for n in range(len(sizes))]

    def kernel(
        day_ref, decay_ref, load_hbm, prec_hbm, start_hbm, stop_hbm, off_hbm, out_ref, acc, load_ref,
        prec_ref, start_ref, stop_ref, off_ref, sems,
    ):
        pairs = [
            (prec_hbm, prec_ref),
            (start_hbm, start_ref),
            (stop_hbm, stop_ref),
            (off_hbm, off_ref),
        ]
        pairs += [(load_hbm.at[part], load_ref.at[part]) for part in parts]
        copies = [
            pltpu.make_async_copy(source, target, sems.at[n])
            for n, (source, target) in enumerate(pairs)
        ]
        for copy in copies:
            copy.start()
        column = jnp.sum(jnp.where(eye(factors), decay_ref[...], 0.0), axis=1, keepdims=True)
        for copy in copies[:4]:
            copy.wait()
        for n, part in enumerate(parts):
            copies[4 + n].wait()
            block = load_ref[part]
            scaled = (block.T.astype(F32) * prec_ref[:, part]).astype(BF16)
            for d in range(day_count):
                active = activity(
                    day_ref[0] + d, start_ref[:, part], stop_ref[:, part], off_ref[:, part]
                )
                mask = active.astype(F32).astype(BF16)
                term = mul(scaled * mask, block)
                if n == 0:
                    acc[d] = term
                elif n < len(parts) - 1:
                    acc[d] += term
                else:
                    out_ref[d] = ((acc[d] + term) * column).astype(BF16)

    return pl.pallas_call(
        kernel,
        in_specs=[smem()] + vmem(1) + hbm(5),
        out_specs=pl.BlockSpec(memory_space=VMEM),
        out_shape=shape(day_count, factors, factors, dtype=BF16),
        scratch_shapes=[
            pltpu.VMEM((day_count, factors, factors), F32),
            pltpu.VMEM((providers, factors), BF16),
            pltpu.VMEM((1, providers), F32),
            pltpu.VMEM((1, providers), jnp.int32),
            pltpu.VMEM((1, providers), jnp.int32),
            pltpu.VMEM((1, providers), jnp.int32),
            pltpu.SemaphoreType.DMA((4 + len(parts),)),
        ],
        compiler_params=params(),
        cost_estimate=cost(2 * day_count * providers * factors * factors, 10 << 20),
        name="damped",
    )(first_day, decay, loadings, *tables)


PACKED = 16


def unpacked(packed_ref):
    factors = packed_ref.shape[1]
    rows = packed_ref[factors:].astype(F32)
    return (packed_ref[:factors],), rows[2:3] + rows[3:4], rows[0:1] + rows[1:2]


def joined(top_ref, bottom_ref):
    half = top_ref.shape[0] - PACKED
    rows = top_ref[half:].astype(F32)
    return (top_ref[:half], bottom_ref[:half]), rows[2:3] + rows[3:4], rows[0:1] + rows[1:2]


def pack(refs, total, tail, same):
    factors = total.shape[0]
    half = factors // len(refs)
    rest = jnp.where(same, 0.0, total).astype(BF16)
    diag = jnp.sum(jnp.where(same, total, 0.0), axis=0, keepdims=True)
    rows = [*split(tail), *split(diag), jnp.zeros((PACKED - 4, factors), BF16)]
    for n, ref in enumerate(refs):
        ref[:half] = rest[n * half : (n + 1) * half]
        ref[half:] = jnp.concatenate(rows, 0)


def through(a, rests, diag):
    rows = a.shape[0]
    high, low = split(a)
    depth = a.shape[1] // len(rests)

    def times(x):
        return sum(mul(x[:, n * depth : (n + 1) * depth], r) for n, r in enumerate(rests))

    if rows > 64:
        return times(high) + times(low) + a * diag
    both = times(jnp.concatenate([high, low], 0))
    return both[:rows] + both[rows:] + a * diag


def block_of(damped, terms, decay, gain):
    parts, day_count, factors = terms.shape

    def kernel(
        damped_ref, terms_ref, decay_ref, gain_ref, run_ref, last_ref, states_ref, tail_ref, packed_ref
    ):
        same = eye(factors)
        weights = gain_ref[...]
        dims = (((1,), (1,)), ((), ()))
        drive = terms_ref[0]
        for p in range(1, parts):
            drive = drive + terms_ref[p]
        high, low = split(drive)
        least = (drive - high.astype(F32) - low.astype(F32)).astype(BF16)
        offsets = sum(
            lax.dot_general(part, weights, dims, preferred_element_type=F32)
            for part in (high, low, least)
        )
        diagonal = jnp.where(same, decay_ref[...], 0.0)
        for d in range(day_count):
            step = diagonal - lax.dot_general(
                damped_ref[d], weights, dims, preferred_element_type=F32
            )
            if d == 0:
                running, state = step, offsets[0:1]
            else:
                run_ref[d - 1] = running
                step = split(step)
                running = product(running, step)
                state = product(state, step) + offsets[d : d + 1]
            states_ref[d : d + 1] = state
        last_ref[...] = running
        tail_ref[...] = state
        pack([packed_ref], running, state, same)

    return pl.pallas_call(
        kernel,
        in_specs=vmem(4),
        out_specs=vmem(5),
        out_shape=[
            shape(day_count - 1, factors, factors),
            shape(factors, factors),
            shape(day_count, factors),
            shape(1, factors),
            shape(factors + PACKED, factors, dtype=BF16),
        ],
        compiler_params=params(),
        cost_estimate=cost(50 * factors**3, 3 << 20),
        name="block",
    )(damped, terms, decay, gain)


def combined(upper, matrix, tail, other):
    factors = matrix.shape[0]

    def kernel(upper_ref, mine_ref, tail_ref, other_ref, sent_ref, kept_ref):
        same = eye(factors)
        rest, diag, other_tail = unpacked(other_ref)

        @pl.when(upper_ref[0] == 1)
        def _():
            mine = split(mine_ref[...])
            theirs = rest[0].astype(F32) + jnp.where(same, diag, 0.0)
            total = product(theirs, mine)
            pack([kept_ref, sent_ref], total, product(other_tail, mine) + tail_ref[...], same)

        @pl.when(upper_ref[0] == 0)
        def _():
            total = through(mine_ref[...], rest, diag)
            tail = through(tail_ref[...], rest, diag) + other_tail
            pack([sent_ref, kept_ref], total, tail, same)

    return pl.pallas_call(
        kernel,
        in_specs=[smem()] + vmem(3),
        out_specs=vmem(2),
        out_shape=[shape(factors // 2 + PACKED, factors, dtype=BF16)] * 2,
        compiler_params=params(),
        cost_estimate=cost(6 * factors**3, 1 << 20),
        name="combined",
    )(upper, matrix, tail, other)


def advanced(pair, upper, state, pieces, nothing=False):
    count = len(pieces)
    factors = state.shape[1]

    def kernel(pair_ref, upper_ref, state_ref, *refs):
        out_ref = refs[-1]
        out_ref[...] = state_ref[...]
        for turn in range(count):
            for m, core in itertools.product(range(count), range(2)):

                @pl.when(((pair_ref[0] ^ m) == turn) & (upper_ref[0] == core))
                def _():
                    rest, diag, tail = joined(refs[2 * m + core], refs[2 * m + 1 - core])
                    if nothing and turn == 0:
                        out_ref[...] = tail
                    else:
                        out_ref[...] = through(out_ref[...], rest, diag) + tail

    return pl.pallas_call(
        kernel,
        in_specs=[smem()] * 2 + vmem(2 * count + 1),
        out_specs=pl.BlockSpec(memory_space=VMEM),
        out_shape=shape(1, factors),
        compiler_params=params(),
        cost_estimate=cost(12 * factors**2, 1 << 18),
        name="advanced",
    )(pair, upper, state, *[a for piece in pieces for a in piece])


def prefixed(pair, upper, pieces, other, running, last, states):
    day_count, factors = states.shape
    count = len(pieces)

    def kernel(pair_ref, upper_ref, *refs):
        other_ref, run_ref, last_ref, states_ref = refs[2 * count : 2 * count + 4]
        high_ref, low_ref, add_ref, work, tail = refs[2 * count + 4 :]
        work[...] = jnp.where(eye(factors), 1.0, 0.0)
        tail[...] = jnp.zeros_like(tail)

        def follow(rest, diag, add):
            work[...] = through(work[...], rest, diag)
            tail[...] = through(tail[...], rest, diag) + add

        for turn in range(count - 1):
            for m, core in itertools.product(range(1, count), range(2)):
                now = ((pair_ref[0] ^ m) == turn) & (pair_ref[0] > turn)

                @pl.when(now & (upper_ref[0] == core))
                def _():
                    follow(*joined(refs[2 * m + core], refs[2 * m + 1 - core]))

        @pl.when(upper_ref[0] == 1)
        def _():
            follow(*unpacked(other_ref))

        for d in range(day_count):
            step = split(run_ref[d] if d < day_count - 1 else last_ref[...])
            place = slice(d * factors, (d + 1) * factors)
            high_ref[:, place], low_ref[:, place] = split(product(work[...], step))
            add_ref[:, place] = product(tail[...], step) + states_ref[d : d + 1]

    wide = day_count * factors
    return pl.pallas_call(
        kernel,
        in_specs=[smem()] * 2 + vmem(2 * count + 4),
        out_specs=vmem(3),
        out_shape=[
            shape(factors, wide, dtype=BF16),
            shape(factors, wide, dtype=BF16),
            shape(1, wide),
        ],
        scratch_shapes=[pltpu.VMEM((factors, factors), F32), pltpu.VMEM((1, factors), F32)],
        compiler_params=params(),
        cost_estimate=cost(36 * factors**3, 3 << 20),
        name="prefixed",
    )(pair, upper, *[a for piece in pieces for a in piece], other, running, last, states)


def filtered_of(state, arrived, high, low, add):
    factors, wide = high.shape
    day_count = wide // factors

    def kernel(state_ref, arrived_ref, high_ref, low_ref, add_ref, out_ref):
        entering = state_ref[...] + arrived_ref[...]
        row = product(entering, (high_ref[...], low_ref[...])) + add_ref[...]
        for d in range(day_count):
            out_ref[d : d + 1] = row[:, d * factors : (d + 1) * factors]

    return pl.pallas_call(
        kernel,
        in_specs=vmem(5),
        out_specs=pl.BlockSpec(memory_space=VMEM),
        out_shape=shape(day_count, factors),
        compiler_params=params(),
        cost_estimate=cost(6 * factors * wide, 1 << 20),
        name="filtered",
    )(state, arrived, high, low, add)


def prepared(index, days, own, smoother, loadings, tables):
    factors = smoother.shape[0]

    def kernel(
        index_ref, in_ref, load_hbm, prec_hbm, start_hbm, stop_hbm, off_hbm, high_ref, low_ref,
        load_ref, scale_ref, prec_ref, start_ref, stop_ref, off_ref, sems,
    ):
        mine = pl.ds(pl.multiple_of(index_ref[0] * own, own), own)
        copies = [
            pltpu.make_async_copy(source, target, sems.at[n])
            for n, (source, target) in enumerate(
                [
                    (prec_hbm.at[:, mine], prec_ref),
                    (start_hbm.at[:, mine], start_ref),
                    (stop_hbm.at[:, mine], stop_ref),
                    (off_hbm.at[:, mine], off_ref),
                    (load_hbm.at[mine], load_ref),
                ]
            )
        ]
        for copy in copies:
            copy.start()
        power = in_ref[...].T
        for p in range(POWERS):
            parts = split(power)
            high_ref[p], low_ref[p] = parts
            if p < POWERS - 1:
                power = product(power, parts)
        for copy in copies:
            copy.wait()
        day = lax.broadcasted_iota(jnp.int32, (days, 1), 0)
        active = activity(day, start_ref[...], stop_ref[...], off_ref[...])
        scale_ref[...] = jnp.where(active, jnp.sqrt(prec_ref[...]), 0.0)

    return pl.pallas_call(
        kernel,
        in_specs=[smem()] + vmem(1) + hbm(5),
        out_specs=vmem(4),
        out_shape=[
            shape(POWERS, factors, factors, dtype=BF16),
            shape(POWERS, factors, factors, dtype=BF16),
            shape(own, factors, dtype=BF16),
            shape(days, own),
        ],
        scratch_shapes=[
            pltpu.VMEM((1, own), F32),
            pltpu.VMEM((1, own), jnp.int32),
            pltpu.VMEM((1, own), jnp.int32),
            pltpu.VMEM((1, own), jnp.int32),
            pltpu.SemaphoreType.DMA((5,)),
        ],
        compiler_params=params(),
        cost_estimate=cost(24 * factors**3, 3 << 20),
        name="prepared",
    )(index, smoother, loadings, *tables)


def finish(index, day_count, gathered, ready, decay, series):
    days, own = series.shape
    factors = decay.shape[1]
    stride = 2 ** (POWERS - 1)
    blocks = days // stride

    def kernel(
        index_ref, gathered_ref, high_ref, low_ref, load_ref, scale_ref, decay_ref, series_ref,
        smooth_ref, score_ref, filt, work,
    ):
        me = index_ref[0]
        for m in range(days // day_count):
            filt[m * day_count : (m + 1) * day_count, :] = gathered_ref[m]
        filtered = filt[...]
        carried = filtered * decay_ref[...]
        carried = jnp.concatenate([jnp.zeros((1, factors), F32), carried[:-1]], 0)
        total = filtered - carried
        for p in range(POWERS - 1):
            reach = 2**p
            later = jnp.concatenate([total[reach:], jnp.zeros((reach, factors), F32)], 0)
            total = total + product(later, (high_ref[p], low_ref[p]))
        far = (high_ref[POWERS - 1], low_ref[POWERS - 1])
        row = total[(blocks - 1) * stride :]
        work[(blocks - 1) * stride :, :] = row
        for b in reversed(range(blocks - 1)):
            row = total[b * stride : (b + 1) * stride] + product(row, far)
            work[b * stride : (b + 1) * stride, :] = row
        work[...] += carried
        for d in range(day_count):
            smooth_ref[d : d + 1, :] = work[pl.ds(me * day_count + d, 1), :]
        fitted = lax.dot_general(
            work[...].astype(BF16), load_ref[...], (((1,), (1,)), ((), ())),
            preferred_element_type=F32,
        )
        residual = series_ref[...].astype(F32) - fitted
        score_ref[...] = (residual * scale_ref[...]).astype(BF16)

    return pl.pallas_call(
        kernel,
        in_specs=[smem()] + vmem(7),
        out_specs=vmem(2),
        out_shape=[shape(day_count, factors), shape(days, own, dtype=BF16)],
        scratch_shapes=[
            pltpu.VMEM((days, factors), F32),
            pltpu.VMEM((days, factors), F32),
        ],
        compiler_params=params(),
        cost_estimate=cost(2 * days * own * factors, 2 << 20),
        name="finish",
    )(index, gathered, *ready, decay, series)


def local(series, loadings, precision, start_day, stop_day, off_day, decay, gain, smoother):
    devices = lax.axis_size("tm")
    place = lax.axis_index("tm").astype(jnp.int32)
    index = place[None]
    days = series.shape[0]
    day_count = days // devices
    factors = loadings.shape[1]
    tables = [a.reshape(1, -1) for a in (precision, start_day, stop_day, off_day)]
    decay = decay.reshape(1, factors)

    def swapped(array, distance):
        return lax.ppermute(array, "tm", [(i, i ^ distance) for i in range(devices)])

    partial = partial_drive(index, devices, series, loadings, tables)
    partial, first_day = lax.optimization_barrier((partial, index * day_count))
    terms = lax.all_to_all(partial, "tm", 0, 0, tiled=True)
    damped = damped_of(first_day, day_count, loadings, tables, decay)
    running, last, states, tail, packed = block_of(damped, terms, decay, gain)

    upper = (place & 1)[None]
    other = swapped(packed, 1)
    sent, kept = combined(upper, last, tail, other)
    group = min(8, devices)
    pair = ((place % group) >> 1)[None]
    came = [swapped(sent, 2 * m) for m in range(1, group // 2)]
    pieces = [(sent, kept)] + [(half, swapped(half, 1)) for half in came]
    nothing = jnp.zeros((1, factors), F32)
    tail = advanced(pair, upper, nothing, pieces, True)
    smoother, tail = lax.optimization_barrier((smoother, tail))
    ready = prepared(index, days, series.shape[1], smoother, loadings, tables)
    ahead = prefixed(pair, upper, pieces, other, running, last, states)

    state = nothing
    arrived = jnp.where(place // group == 1, swapped(tail, group), 0.0)
    for g in range(1, devices // group - 1):
        state = state + arrived
        moved = advanced(pair, upper, state, pieces)
        pairs = [(g * group + j, (g + 1) * group + j) for j in range(group)]
        arrived = lax.ppermute(moved, "tm", pairs)

    ahead, ready = lax.optimization_barrier((ahead, ready))
    own = filtered_of(state, arrived, *ahead)[None]
    gathered = lax.all_to_all(
        jnp.broadcast_to(own, (devices, day_count, factors)), "tm", 0, 0, tiled=True
    )
    return tuple(finish(index, day_count, gathered, ready, decay, series))


def solution(mesh):
    in_specs = (
        P(None, ("spec", "tm")),
        P("spec", None),
        P("spec"),
        P("spec"),
        P("spec"),
        P("spec"),
        P(),
        P(),
        P(),
    )
    out_specs = (P("tm", "spec"), P(None, ("spec", "tm")))
    return jax.shard_map(local, mesh=mesh, in_specs=in_specs, out_specs=out_specs, check_vma=False)
```

```python
import itertools

import jax
import jax.numpy as jnp
from jax import lax
from jax.experimental import pallas as pl
from jax.experimental.pallas import tpu as pltpu
from jax.sharding import PartitionSpec as P

F32 = jnp.float32
BF16 = jnp.bfloat16
VMEM = pltpu.MemorySpace.VMEM
SMEM = pltpu.MemorySpace.SMEM
HBM = pltpu.MemorySpace.HBM
POWERS = 5


def params(mebibytes=48, **more):
    return pltpu.CompilerParams(vmem_limit_bytes=mebibytes << 20, **more)


def cost(flops, nbytes):
    return pl.CostEstimate(flops=flops, bytes_accessed=nbytes, transcendentals=0)


def vmem(count):
    return [pl.BlockSpec(memory_space=VMEM)] * count


def hbm(count):
    return [pl.BlockSpec(memory_space=HBM)] * count


def smem():
    return pl.BlockSpec(memory_space=SMEM)


def shape(*dims, dtype=F32):
    return jax.ShapeDtypeStruct(dims, dtype)


def mul(a, b):
    return jnp.dot(a, b, preferred_element_type=F32)


def split(a):
    high = a.astype(BF16)
    return high, (a - high.astype(F32)).astype(BF16)


def product(a, b):
    high, low = split(a)
    rows = a.shape[0]
    if rows > 64:
        return mul(high, b[0]) + mul(low, b[0]) + mul(high, b[1])
    both = mul(jnp.concatenate([high, low], 0), b[0])
    return both[:rows] + both[rows:] + mul(high, b[1])


def eye(factors):
    dims = (factors, factors)
    return lax.broadcasted_iota(jnp.int32, dims, 0) == lax.broadcasted_iota(jnp.int32, dims, 1)


def activity(day, start, stop, off):
    return (day >= start) & (day < stop) & (lax.rem(day, 7) != off)


def partial_drive(index, devices, series, loadings, tables):
    days, own = series.shape
    day_count = days // devices
    factors = loadings.shape[1]

    def kernel(
        index_ref, series_hbm, load_hbm, prec_hbm, start_hbm, stop_hbm, off_hbm, out_ref,
        series_ref, load_ref, prec_ref, start_ref, stop_ref, off_ref, sems,
    ):
        first = pl.multiple_of(index_ref[0] * own, own)
        mine = pl.ds(first, own)
        copies = [
            pltpu.make_async_copy(source, target, sems.at[n])
            for n, (source, target) in enumerate(
                [
                    (prec_hbm.at[:, mine], prec_ref),
                    (start_hbm.at[:, mine], start_ref),
                    (stop_hbm.at[:, mine], stop_ref),
                    (off_hbm.at[:, mine], off_ref),
                    (series_hbm, series_ref),
                    (load_hbm.at[mine], load_ref),
                ]
            )
        ]
        for copy in copies:
            copy.start()
        day = lax.broadcasted_iota(jnp.int32, (days, 1), 0)
        for copy in copies[:5]:
            copy.wait()
        active = activity(day, start_ref[...], stop_ref[...], off_ref[...])
        weights = jnp.where(active, prec_ref[...], 0.0)
        weighted = (weights * series_ref[...].astype(F32)).astype(BF16)
        copies[5].wait()
        drive = mul(weighted, load_ref[...])
        for p in range(devices):
            out_ref[p] = drive[p * day_count : (p + 1) * day_count]

    return pl.pallas_call(
        kernel,
        in_specs=[smem()] + hbm(6),
        out_specs=pl.BlockSpec(memory_space=VMEM),
        out_shape=shape(devices, day_count, factors),
        scratch_shapes=[
            pltpu.VMEM((days, own), BF16),
            pltpu.VMEM((own, factors), BF16),
            pltpu.VMEM((1, own), F32),
            pltpu.VMEM((1, own), jnp.int32),
            pltpu.VMEM((1, own), jnp.int32),
            pltpu.VMEM((1, own), jnp.int32),
            pltpu.SemaphoreType.DMA((6,)),
        ],
        compiler_params=params(63),
        cost_estimate=cost(2 * days * own * factors, 1 << 20),
        name="partial_drive",
    )(index, series, loadings, *tables)


def damped_of(first_day, day_count, loadings, tables, decay):
    providers, factors = loadings.shape
    unit = providers // 16
    sizes = [unit, unit, 2 * unit, 6 * unit, 6 * unit]
    parts = [slice(sum(sizes[:n]), sum(sizes[: n + 1])) for n in range(len(sizes))]

    def kernel(
        day_ref, decay_ref, load_hbm, prec_hbm, start_hbm, stop_hbm, off_hbm, out_ref, acc, load_ref,
        prec_ref, start_ref, stop_ref, off_ref, sems,
    ):
        pairs = [
            (prec_hbm, prec_ref),
            (start_hbm, start_ref),
            (stop_hbm, stop_ref),
            (off_hbm, off_ref),
        ]
        pairs += [(load_hbm.at[part], load_ref.at[part]) for part in parts]
        copies = [
            pltpu.make_async_copy(source, target, sems.at[n])
            for n, (source, target) in enumerate(pairs)
        ]
        for copy in copies:
            copy.start()
        column = jnp.sum(jnp.where(eye(factors), decay_ref[...], 0.0), axis=1, keepdims=True)
        for copy in copies[:4]:
            copy.wait()
        for n, part in enumerate(parts):
            copies[4 + n].wait()
            block = load_ref[part]
            scaled = (block.T.astype(F32) * prec_ref[:, part]).astype(BF16)
            for d in range(day_count):
                active = activity(
                    day_ref[0] + d, start_ref[:, part], stop_ref[:, part], off_ref[:, part]
                )
                mask = active.astype(F32).astype(BF16)
                term = mul(scaled * mask, block)
                if n == 0:
                    acc[d] = term
                elif n < len(parts) - 1:
                    acc[d] += term
                else:
                    out_ref[d] = ((acc[d] + term) * column).astype(BF16)

    return pl.pallas_call(
        kernel,
        in_specs=[smem()] + vmem(1) + hbm(5),
        out_specs=pl.BlockSpec(memory_space=VMEM),
        out_shape=shape(day_count, factors, factors, dtype=BF16),
        scratch_shapes=[
            pltpu.VMEM((day_count, factors, factors), F32),
            pltpu.VMEM((providers, factors), BF16),
            pltpu.VMEM((1, providers), F32),
            pltpu.VMEM((1, providers), jnp.int32),
            pltpu.VMEM((1, providers), jnp.int32),
            pltpu.VMEM((1, providers), jnp.int32),
            pltpu.SemaphoreType.DMA((4 + len(parts),)),
        ],
        compiler_params=params(),
        cost_estimate=cost(2 * day_count * providers * factors * factors, 10 << 20),
        name="damped",
    )(first_day, decay, loadings, *tables)


PACKED = 16


def unpacked(packed_ref):
    factors = packed_ref.shape[1]
    rows = packed_ref[factors:].astype(F32)
    return (packed_ref[:factors],), rows[2:3] + rows[3:4], rows[0:1] + rows[1:2]


def joined(top_ref, bottom_ref):
    half = top_ref.shape[0] - PACKED
    rows = top_ref[half:].astype(F32)
    return (top_ref[:half], bottom_ref[:half]), rows[2:3] + rows[3:4], rows[0:1] + rows[1:2]


def pack(refs, total, tail, same):
    factors = total.shape[0]
    half = factors // len(refs)
    rest = jnp.where(same, 0.0, total).astype(BF16)
    diag = jnp.sum(jnp.where(same, total, 0.0), axis=0, keepdims=True)
    rows = [*split(tail), *split(diag), jnp.zeros((PACKED - 4, factors), BF16)]
    for n, ref in enumerate(refs):
        ref[:half] = rest[n * half : (n + 1) * half]
        ref[half:] = jnp.concatenate(rows, 0)


def through(a, rests, diag):
    rows = a.shape[0]
    high, low = split(a)
    depth = a.shape[1] // len(rests)

    def times(x):
        return sum(mul(x[:, n * depth : (n + 1) * depth], r) for n, r in enumerate(rests))

    if rows > 64:
        return times(high) + times(low) + a * diag
    both = times(jnp.concatenate([high, low], 0))
    return both[:rows] + both[rows:] + a * diag


def block_of(damped, terms, decay, gain):
    parts, day_count, factors = terms.shape

    def kernel(
        damped_ref, terms_ref, decay_ref, gain_ref, run_ref, last_ref, states_ref, tail_ref, packed_ref
    ):
        same = eye(factors)
        weights = gain_ref[...]
        dims = (((1,), (1,)), ((), ()))
        drive = terms_ref[0]
        for p in range(1, parts):
            drive = drive + terms_ref[p]
        high, low = split(drive)
        least = (drive - high.astype(F32) - low.astype(F32)).astype(BF16)
        offsets = sum(
            lax.dot_general(part, weights, dims, preferred_element_type=F32)
            for part in (high, low, least)
        )
        diagonal = jnp.where(same, decay_ref[...], 0.0)
        for d in range(day_count):
            step = diagonal - lax.dot_general(
                damped_ref[d], weights, dims, preferred_element_type=F32
            )
            if d == 0:
                running, state = step, offsets[0:1]
            else:
                run_ref[d - 1] = running
                step = split(step)
                running = product(running, step)
                state = product(state, step) + offsets[d : d + 1]
            states_ref[d : d + 1] = state
        last_ref[...] = running
        tail_ref[...] = state
        pack([packed_ref], running, state, same)

    return pl.pallas_call(
        kernel,
        in_specs=vmem(4),
        out_specs=vmem(5),
        out_shape=[
            shape(day_count - 1, factors, factors),
            shape(factors, factors),
            shape(day_count, factors),
            shape(1, factors),
            shape(factors + PACKED, factors, dtype=BF16),
        ],
        compiler_params=params(),
        cost_estimate=cost(50 * factors**3, 3 << 20),
        name="block",
    )(damped, terms, decay, gain)


def combined(upper, matrix, tail, other):
    factors = matrix.shape[0]

    def kernel(upper_ref, mine_ref, tail_ref, other_ref, sent_ref, kept_ref):
        same = eye(factors)
        rest, diag, other_tail = unpacked(other_ref)

        @pl.when(upper_ref[0] == 1)
        def _():
            mine = split(mine_ref[...])
            theirs = rest[0].astype(F32) + jnp.where(same, diag, 0.0)
            total = product(theirs, mine)
            pack([kept_ref, sent_ref], total, product(other_tail, mine) + tail_ref[...], same)

        @pl.when(upper_ref[0] == 0)
        def _():
            total = through(mine_ref[...], rest, diag)
            tail = through(tail_ref[...], rest, diag) + other_tail
            pack([sent_ref, kept_ref], total, tail, same)

    return pl.pallas_call(
        kernel,
        in_specs=[smem()] + vmem(3),
        out_specs=vmem(2),
        out_shape=[shape(factors // 2 + PACKED, factors, dtype=BF16)] * 2,
        compiler_params=params(),
        cost_estimate=cost(6 * factors**3, 1 << 20),
        name="combined",
    )(upper, matrix, tail, other)


def advanced(pair, upper, state, pieces, nothing=False):
    count = len(pieces)
    factors = state.shape[1]

    def kernel(pair_ref, upper_ref, state_ref, *refs):
        out_ref = refs[-1]
        out_ref[...] = state_ref[...]
        for turn in range(count):
            for m, core in itertools.product(range(count), range(2)):

                @pl.when(((pair_ref[0] ^ m) == turn) & (upper_ref[0] == core))
                def _():
                    rest, diag, tail = joined(refs[2 * m + core], refs[2 * m + 1 - core])
                    if nothing and turn == 0:
                        out_ref[...] = tail
                    else:
                        out_ref[...] = through(out_ref[...], rest, diag) + tail

    return pl.pallas_call(
        kernel,
        in_specs=[smem()] * 2 + vmem(2 * count + 1),
        out_specs=pl.BlockSpec(memory_space=VMEM),
        out_shape=shape(1, factors),
        compiler_params=params(),
        cost_estimate=cost(12 * factors**2, 1 << 18),
        name="advanced",
    )(pair, upper, state, *[a for piece in pieces for a in piece])


def prefixed(pair, upper, pieces, other, running, last, states):
    day_count, factors = states.shape
    count = len(pieces)

    def kernel(pair_ref, upper_ref, *refs):
        other_ref, run_ref, last_ref, states_ref = refs[2 * count : 2 * count + 4]
        high_ref, low_ref, add_ref, work, tail = refs[2 * count + 4 :]
        work[...] = jnp.where(eye(factors), 1.0, 0.0)
        tail[...] = jnp.zeros_like(tail)

        def follow(rest, diag, add):
            work[...] = through(work[...], rest, diag)
            tail[...] = through(tail[...], rest, diag) + add

        for turn in range(count - 1):
            for m, core in itertools.product(range(1, count), range(2)):
                now = ((pair_ref[0] ^ m) == turn) & (pair_ref[0] > turn)

                @pl.when(now & (upper_ref[0] == core))
                def _():
                    follow(*joined(refs[2 * m + core], refs[2 * m + 1 - core]))

        @pl.when(upper_ref[0] == 1)
        def _():
            follow(*unpacked(other_ref))

        for d in range(day_count):
            step = split(run_ref[d] if d < day_count - 1 else last_ref[...])
            place = slice(d * factors, (d + 1) * factors)
            high_ref[:, place], low_ref[:, place] = split(product(work[...], step))
            add_ref[:, place] = product(tail[...], step) + states_ref[d : d + 1]

    wide = day_count * factors
    return pl.pallas_call(
        kernel,
        in_specs=[smem()] * 2 + vmem(2 * count + 4),
        out_specs=vmem(3),
        out_shape=[
            shape(factors, wide, dtype=BF16),
            shape(factors, wide, dtype=BF16),
            shape(1, wide),
        ],
        scratch_shapes=[pltpu.VMEM((factors, factors), F32), pltpu.VMEM((1, factors), F32)],
        compiler_params=params(),
        cost_estimate=cost(36 * factors**3, 3 << 20),
        name="prefixed",
    )(pair, upper, *[a for piece in pieces for a in piece], other, running, last, states)


def filtered_of(state, arrived, high, low, add):
    factors, wide = high.shape
    day_count = wide // factors

    def kernel(state_ref, arrived_ref, high_ref, low_ref, add_ref, out_ref):
        entering = state_ref[...] + arrived_ref[...]
        row = product(entering, (high_ref[...], low_ref[...])) + add_ref[...]
        for d in range(day_count):
            out_ref[d : d + 1] = row[:, d * factors : (d + 1) * factors]

    return pl.pallas_call(
        kernel,
        in_specs=vmem(5),
        out_specs=pl.BlockSpec(memory_space=VMEM),
        out_shape=shape(day_count, factors),
        compiler_params=params(),
        cost_estimate=cost(6 * factors * wide, 1 << 20),
        name="filtered",
    )(state, arrived, high, low, add)


def prepared(index, days, own, smoother, loadings, tables):
    factors = smoother.shape[0]

    def kernel(
        index_ref, in_ref, load_hbm, prec_hbm, start_hbm, stop_hbm, off_hbm, high_ref, low_ref,
        load_ref, scale_ref, prec_ref, start_ref, stop_ref, off_ref, sems,
    ):
        mine = pl.ds(pl.multiple_of(index_ref[0] * own, own), own)
        copies = [
            pltpu.make_async_copy(source, target, sems.at[n])
            for n, (source, target) in enumerate(
                [
                    (prec_hbm.at[:, mine], prec_ref),
                    (start_hbm.at[:, mine], start_ref),
                    (stop_hbm.at[:, mine], stop_ref),
                    (off_hbm.at[:, mine], off_ref),
                    (load_hbm.at[mine], load_ref),
                ]
            )
        ]
        for copy in copies:
            copy.start()
        power = in_ref[...].T
        for p in range(POWERS):
            parts = split(power)
            high_ref[p], low_ref[p] = parts
            if p < POWERS - 1:
                power = product(power, parts)
        for copy in copies:
            copy.wait()
        day = lax.broadcasted_iota(jnp.int32, (days, 1), 0)
        active = activity(day, start_ref[...], stop_ref[...], off_ref[...])
        scale_ref[...] = jnp.where(active, jnp.sqrt(prec_ref[...]), 0.0)

    return pl.pallas_call(
        kernel,
        in_specs=[smem()] + vmem(1) + hbm(5),
        out_specs=vmem(4),
        out_shape=[
            shape(POWERS, factors, factors, dtype=BF16),
            shape(POWERS, factors, factors, dtype=BF16),
            shape(own, factors, dtype=BF16),
            shape(days, own),
        ],
        scratch_shapes=[
            pltpu.VMEM((1, own), F32),
            pltpu.VMEM((1, own), jnp.int32),
            pltpu.VMEM((1, own), jnp.int32),
            pltpu.VMEM((1, own), jnp.int32),
            pltpu.SemaphoreType.DMA((5,)),
        ],
        compiler_params=params(),
        cost_estimate=cost(24 * factors**3, 3 << 20),
        name="prepared",
    )(index, smoother, loadings, *tables)


def finish(index, day_count, gathered, ready, decay, series):
    days, own = series.shape
    factors = decay.shape[1]
    stride = 2 ** (POWERS - 1)
    blocks = days // stride

    def kernel(
        index_ref, gathered_ref, high_ref, low_ref, load_ref, scale_ref, decay_ref, series_ref,
        smooth_ref, score_ref, filt, work,
    ):
        me = index_ref[0]
        for m in range(days // day_count):
            filt[m * day_count : (m + 1) * day_count, :] = gathered_ref[m]
        filtered = filt[...]
        carried = filtered * decay_ref[...]
        carried = jnp.concatenate([jnp.zeros((1, factors), F32), carried[:-1]], 0)
        total = filtered - carried
        for p in range(POWERS - 1):
            reach = 2**p
            later = jnp.concatenate([total[reach:], jnp.zeros((reach, factors), F32)], 0)
            total = total + product(later, (high_ref[p], low_ref[p]))
        far = (high_ref[POWERS - 1], low_ref[POWERS - 1])
        row = total[(blocks - 1) * stride :]
        work[(blocks - 1) * stride :, :] = row
        for b in reversed(range(blocks - 1)):
            row = total[b * stride : (b + 1) * stride] + product(row, far)
            work[b * stride : (b + 1) * stride, :] = row
        work[...] += carried
        for d in range(day_count):
            smooth_ref[d : d + 1, :] = work[pl.ds(me * day_count + d, 1), :]
        fitted = lax.dot_general(
            work[...].astype(BF16), load_ref[...], (((1,), (1,)), ((), ())),
            preferred_element_type=F32,
        )
        residual = series_ref[...].astype(F32) - fitted
        score_ref[...] = (residual * scale_ref[...]).astype(BF16)

    return pl.pallas_call(
        kernel,
        in_specs=[smem()] + vmem(7),
        out_specs=vmem(2),
        out_shape=[shape(day_count, factors), shape(days, own, dtype=BF16)],
        scratch_shapes=[
            pltpu.VMEM((days, factors), F32),
            pltpu.VMEM((days, factors), F32),
        ],
        compiler_params=params(),
        cost_estimate=cost(2 * days * own * factors, 2 << 20),
        name="finish",
    )(index, gathered, *ready, decay, series)


def local(series, loadings, precision, start_day, stop_day, off_day, decay, gain, smoother):
    devices = lax.axis_size("tm")
    place = lax.axis_index("tm").astype(jnp.int32)
    index = place[None]
    days = series.shape[0]
    day_count = days // devices
    factors = loadings.shape[1]
    tables = [a.reshape(1, -1) for a in (precision, start_day, stop_day, off_day)]
    decay = decay.reshape(1, factors)

    def swapped(array, distance):
        return lax.ppermute(array, "tm", [(i, i ^ distance) for i in range(devices)])

    partial = partial_drive(index, devices, series, loadings, tables)
    partial, first_day = lax.optimization_barrier((partial, index * day_count))
    terms = lax.all_to_all(partial, "tm", 0, 0, tiled=True)
    damped = damped_of(first_day, day_count, loadings, tables, decay)
    running, last, states, tail, packed = block_of(damped, terms, decay, gain)

    upper = (place & 1)[None]
    other = swapped(packed, 1)
    sent, kept = combined(upper, last, tail, other)
    group = min(8, devices)
    pair = ((place % group) >> 1)[None]
    came = [swapped(sent, 2 * m) for m in range(1, group // 2)]
    pieces = [(sent, kept)] + [(half, swapped(half, 1)) for half in came]
    nothing = jnp.zeros((1, factors), F32)
    tail = advanced(pair, upper, nothing, pieces, True)
    smoother, tail = lax.optimization_barrier((smoother, tail))
    ready = prepared(index, days, series.shape[1], smoother, loadings, tables)
    ahead = prefixed(pair, upper, pieces, other, running, last, states)

    state = nothing
    arrived = jnp.where(place // group == 1, swapped(tail, group), 0.0)
    for g in range(1, devices // group - 1):
        state = state + arrived
        moved = advanced(pair, upper, state, pieces)
        pairs = [(g * group + j, (g + 1) * group + j) for j in range(group)]
        arrived = lax.ppermute(moved, "tm", pairs)

    ahead, ready = lax.optimization_barrier((ahead, ready))
    own = filtered_of(state, arrived, *ahead)[None]
    gathered = lax.all_to_all(
        jnp.broadcast_to(own, (devices, day_count, factors)), "tm", 0, 0, tiled=True
    )
    return tuple(finish(index, day_count, gathered, ready, decay, series))


def solution(mesh):
    in_specs = (
        P(None, ("spec", "tm")),
        P("spec", None),
        P("spec"),
        P("spec"),
        P("spec"),
        P("spec"),
        P(),
        P(),
        P(),
    )
    out_specs = (P("tm", "spec"), P(None, ("spec", "tm")))
    return jax.shard_map(local, mesh=mesh, in_specs=in_specs, out_specs=out_specs, check_vma=False)
```

```python
import itertools

import jax
import jax.numpy as jnp
from jax import lax
from jax.experimental import pallas as pl
from jax.experimental.pallas import tpu as pltpu
from jax.sharding import PartitionSpec as P

F32 = jnp.float32
BF16 = jnp.bfloat16
VMEM = pltpu.MemorySpace.VMEM
SMEM = pltpu.MemorySpace.SMEM
HBM = pltpu.MemorySpace.HBM
POWERS = 5


def params(mebibytes=48, **more):
    return pltpu.CompilerParams(vmem_limit_bytes=mebibytes << 20, **more)


def cost(flops, nbytes):
    return pl.CostEstimate(flops=flops, bytes_accessed=nbytes, transcendentals=0)


def vmem(count):
    return [pl.BlockSpec(memory_space=VMEM)] * count


def hbm(count):
    return [pl.BlockSpec(memory_space=HBM)] * count


def smem():
    return pl.BlockSpec(memory_space=SMEM)


def shape(*dims, dtype=F32):
    return jax.ShapeDtypeStruct(dims, dtype)


def mul(a, b):
    return jnp.dot(a, b, preferred_element_type=F32)


def split(a):
    high = a.astype(BF16)
    return high, (a - high.astype(F32)).astype(BF16)


def product(a, b):
    high, low = split(a)
    rows = a.shape[0]
    if rows > 64:
        return mul(high, b[0]) + mul(low, b[0]) + mul(high, b[1])
    both = mul(jnp.concatenate([high, low], 0), b[0])
    return both[:rows] + both[rows:] + mul(high, b[1])


def eye(factors):
    dims = (factors, factors)
    return lax.broadcasted_iota(jnp.int32, dims, 0) == lax.broadcasted_iota(jnp.int32, dims, 1)


def activity(day, start, stop, off):
    return (day >= start) & (day < stop) & (lax.rem(day, 7) != off)


def partial_drive(index, devices, series, loadings, tables):
    days, own = series.shape
    day_count = days // devices
    factors = loadings.shape[1]

    def kernel(
        index_ref, series_hbm, load_hbm, prec_hbm, start_hbm, stop_hbm, off_hbm, out_ref,
        series_ref, load_ref, prec_ref, start_ref, stop_ref, off_ref, sems,
    ):
        first = pl.multiple_of(index_ref[0] * own, own)
        mine = pl.ds(first, own)
        copies = [
            pltpu.make_async_copy(source, target, sems.at[n])
            for n, (source, target) in enumerate(
                [
                    (prec_hbm.at[:, mine], prec_ref),
                    (start_hbm.at[:, mine], start_ref),
                    (stop_hbm.at[:, mine], stop_ref),
                    (off_hbm.at[:, mine], off_ref),
                    (series_hbm, series_ref),
                    (load_hbm.at[mine], load_ref),
                ]
            )
        ]
        for copy in copies:
            copy.start()
        day = lax.broadcasted_iota(jnp.int32, (days, 1), 0)
        for copy in copies[:5]:
            copy.wait()
        active = activity(day, start_ref[...], stop_ref[...], off_ref[...])
        weights = jnp.where(active, prec_ref[...], 0.0)
        weighted = (weights * series_ref[...].astype(F32)).astype(BF16)
        copies[5].wait()
        drive = mul(weighted, load_ref[...])
        for p in range(devices):
            out_ref[p] = drive[p * day_count : (p + 1) * day_count]

    return pl.pallas_call(
        kernel,
        in_specs=[smem()] + hbm(6),
        out_specs=pl.BlockSpec(memory_space=VMEM),
        out_shape=shape(devices, day_count, factors),
        scratch_shapes=[
            pltpu.VMEM((days, own), BF16),
            pltpu.VMEM((own, factors), BF16),
            pltpu.VMEM((1, own), F32),
            pltpu.VMEM((1, own), jnp.int32),
            pltpu.VMEM((1, own), jnp.int32),
            pltpu.VMEM((1, own), jnp.int32),
            pltpu.SemaphoreType.DMA((6,)),
        ],
        compiler_params=params(63),
        cost_estimate=cost(2 * days * own * factors, 1 << 20),
        name="partial_drive",
    )(index, series, loadings, *tables)


def damped_of(first_day, day_count, loadings, tables, decay):
    providers, factors = loadings.shape
    unit = providers // 16
    sizes = [unit, 3 * unit, 6 * unit, 6 * unit]
    parts = [slice(sum(sizes[:n]), sum(sizes[: n + 1])) for n in range(len(sizes))]

    def kernel(
        day_ref, decay_ref, load_hbm, prec_hbm, start_hbm, stop_hbm, off_hbm, out_ref, acc, load_ref,
        prec_ref, start_ref, stop_ref, off_ref, sems,
    ):
        pairs = [
            (prec_hbm, prec_ref),
            (start_hbm, start_ref),
            (stop_hbm, stop_ref),
            (off_hbm, off_ref),
        ]
        pairs += [(load_hbm.at[part], load_ref.at[part]) for part in parts]
        copies = [
            pltpu.make_async_copy(source, target, sems.at[n])
            for n, (source, target) in enumerate(pairs)
        ]
        for copy in copies:
            copy.start()
        column = jnp.sum(jnp.where(eye(factors), decay_ref[...], 0.0), axis=1, keepdims=True)
        for copy in copies[:4]:
            copy.wait()
        for n, part in enumerate(parts):
            copies[4 + n].wait()
            block = load_ref[part]
            scaled = (block.T.astype(F32) * prec_ref[:, part]).astype(BF16)
            for d in range(day_count):
                active = activity(
                    day_ref[0] + d, start_ref[:, part], stop_ref[:, part], off_ref[:, part]
                )
                mask = active.astype(F32).astype(BF16)
                term = mul(scaled * mask, block)
                if n == 0:
                    acc[d] = term
                elif n < len(parts) - 1:
                    acc[d] += term
                else:
                    out_ref[d] = ((acc[d] + term) * column).astype(BF16)

    return pl.pallas_call(
        kernel,
        in_specs=[smem()] + vmem(1) + hbm(5),
        out_specs=pl.BlockSpec(memory_space=VMEM),
        out_shape=shape(day_count, factors, factors, dtype=BF16),
        scratch_shapes=[
            pltpu.VMEM((day_count, factors, factors), F32),
            pltpu.VMEM((providers, factors), BF16),
            pltpu.VMEM((1, providers), F32),
            pltpu.VMEM((1, providers), jnp.int32),
            pltpu.VMEM((1, providers), jnp.int32),
            pltpu.VMEM((1, providers), jnp.int32),
            pltpu.SemaphoreType.DMA((4 + len(parts),)),
        ],
        compiler_params=params(),
        cost_estimate=cost(2 * day_count * providers * factors * factors, 10 << 20),
        name="damped",
    )(first_day, decay, loadings, *tables)


PACKED = 16


def unpacked(packed_ref):
    factors = packed_ref.shape[1]
    rows = packed_ref[factors:].astype(F32)
    return (packed_ref[:factors],), rows[2:3] + rows[3:4], rows[0:1] + rows[1:2]


def joined(top_ref, bottom_ref):
    half = top_ref.shape[0] - PACKED
    rows = top_ref[half:].astype(F32)
    return (top_ref[:half], bottom_ref[:half]), rows[2:3] + rows[3:4], rows[0:1] + rows[1:2]


def pack(refs, total, tail, same):
    factors = total.shape[0]
    half = factors // len(refs)
    rest = jnp.where(same, 0.0, total).astype(BF16)
    diag = jnp.sum(jnp.where(same, total, 0.0), axis=0, keepdims=True)
    rows = [*split(tail), *split(diag), jnp.zeros((PACKED - 4, factors), BF16)]
    for n, ref in enumerate(refs):
        ref[:half] = rest[n * half : (n + 1) * half]
        ref[half:] = jnp.concatenate(rows, 0)


def through(a, rests, diag):
    rows = a.shape[0]
    high, low = split(a)
    depth = a.shape[1] // len(rests)

    def times(x):
        return sum(mul(x[:, n * depth : (n + 1) * depth], r) for n, r in enumerate(rests))

    if rows > 64:
        return times(high) + times(low) + a * diag
    both = times(jnp.concatenate([high, low], 0))
    return both[:rows] + both[rows:] + a * diag


def block_of(damped, terms, decay, gain):
    parts, day_count, factors = terms.shape

    def kernel(
        damped_ref, terms_ref, decay_ref, gain_ref, run_ref, last_ref, states_ref, tail_ref, packed_ref
    ):
        same = eye(factors)
        weights = gain_ref[...]
        dims = (((1,), (1,)), ((), ()))
        drive = terms_ref[0]
        for p in range(1, parts):
            drive = drive + terms_ref[p]
        high, low = split(drive)
        least = (drive - high.astype(F32) - low.astype(F32)).astype(BF16)
        offsets = sum(
            lax.dot_general(part, weights, dims, preferred_element_type=F32)
            for part in (high, low, least)
        )
        diagonal = jnp.where(same, decay_ref[...], 0.0)
        for d in range(day_count):
            step = diagonal - lax.dot_general(
                damped_ref[d], weights, dims, preferred_element_type=F32
            )
            if d == 0:
                running, state = step, offsets[0:1]
            else:
                run_ref[d - 1] = running
                step = split(step)
                running = product(running, step)
                state = product(state, step) + offsets[d : d + 1]
            states_ref[d : d + 1] = state
        last_ref[...] = running
        tail_ref[...] = state
        pack([packed_ref], running, state, same)

    return pl.pallas_call(
        kernel,
        in_specs=vmem(4),
        out_specs=vmem(5),
        out_shape=[
            shape(day_count - 1, factors, factors),
            shape(factors, factors),
            shape(day_count, factors),
            shape(1, factors),
            shape(factors + PACKED, factors, dtype=BF16),
        ],
        compiler_params=params(),
        cost_estimate=cost(50 * factors**3, 3 << 20),
        name="block",
    )(damped, terms, decay, gain)


def combined(upper, matrix, tail, other):
    factors = matrix.shape[0]

    def kernel(upper_ref, mine_ref, tail_ref, other_ref, sent_ref, kept_ref):
        same = eye(factors)
        rest, diag, other_tail = unpacked(other_ref)

        @pl.when(upper_ref[0] == 1)
        def _():
            mine = split(mine_ref[...])
            theirs = rest[0].astype(F32) + jnp.where(same, diag, 0.0)
            total = product(theirs, mine)
            pack([kept_ref, sent_ref], total, product(other_tail, mine) + tail_ref[...], same)

        @pl.when(upper_ref[0] == 0)
        def _():
            total = through(mine_ref[...], rest, diag)
            tail = through(tail_ref[...], rest, diag) + other_tail
            pack([sent_ref, kept_ref], total, tail, same)

    return pl.pallas_call(
        kernel,
        in_specs=[smem()] + vmem(3),
        out_specs=vmem(2),
        out_shape=[shape(factors // 2 + PACKED, factors, dtype=BF16)] * 2,
        compiler_params=params(),
        cost_estimate=cost(6 * factors**3, 1 << 20),
        name="combined",
    )(upper, matrix, tail, other)


def advanced(pair, upper, state, pieces, nothing=False):
    count = len(pieces)
    factors = state.shape[1]

    def kernel(pair_ref, upper_ref, state_ref, *refs):
        out_ref = refs[-1]
        out_ref[...] = state_ref[...]
        for turn in range(count):
            for m, core in itertools.product(range(count), range(2)):

                @pl.when(((pair_ref[0] ^ m) == turn) & (upper_ref[0] == core))
                def _():
                    rest, diag, tail = joined(refs[2 * m + core], refs[2 * m + 1 - core])
                    if nothing and turn == 0:
                        out_ref[...] = tail
                    else:
                        out_ref[...] = through(out_ref[...], rest, diag) + tail

    return pl.pallas_call(
        kernel,
        in_specs=[smem()] * 2 + vmem(2 * count + 1),
        out_specs=pl.BlockSpec(memory_space=VMEM),
        out_shape=shape(1, factors),
        compiler_params=params(),
        cost_estimate=cost(12 * factors**2, 1 << 18),
        name="advanced",
    )(pair, upper, state, *[a for piece in pieces for a in piece])


def prefixed(pair, upper, pieces, other, running, last, states):
    day_count, factors = states.shape
    count = len(pieces)

    def kernel(pair_ref, upper_ref, *refs):
        other_ref, run_ref, last_ref, states_ref = refs[2 * count : 2 * count + 4]
        high_ref, low_ref, add_ref, work, tail = refs[2 * count + 4 :]
        work[...] = jnp.where(eye(factors), 1.0, 0.0)
        tail[...] = jnp.zeros_like(tail)

        def follow(rest, diag, add):
            work[...] = through(work[...], rest, diag)
            tail[...] = through(tail[...], rest, diag) + add

        for turn in range(count - 1):
            for m, core in itertools.product(range(1, count), range(2)):
                now = ((pair_ref[0] ^ m) == turn) & (pair_ref[0] > turn)

                @pl.when(now & (upper_ref[0] == core))
                def _():
                    follow(*joined(refs[2 * m + core], refs[2 * m + 1 - core]))

        @pl.when(upper_ref[0] == 1)
        def _():
            follow(*unpacked(other_ref))

        for d in range(day_count):
            step = split(run_ref[d] if d < day_count - 1 else last_ref[...])
            place = slice(d * factors, (d + 1) * factors)
            high_ref[:, place], low_ref[:, place] = split(product(work[...], step))
            add_ref[:, place] = product(tail[...], step) + states_ref[d : d + 1]

    wide = day_count * factors
    return pl.pallas_call(
        kernel,
        in_specs=[smem()] * 2 + vmem(2 * count + 4),
        out_specs=vmem(3),
        out_shape=[
            shape(factors, wide, dtype=BF16),
            shape(factors, wide, dtype=BF16),
            shape(1, wide),
        ],
        scratch_shapes=[pltpu.VMEM((factors, factors), F32), pltpu.VMEM((1, factors), F32)],
        compiler_params=params(),
        cost_estimate=cost(36 * factors**3, 3 << 20),
        name="prefixed",
    )(pair, upper, *[a for piece in pieces for a in piece], other, running, last, states)


def filtered_of(state, arrived, high, low, add):
    factors, wide = high.shape
    day_count = wide // factors

    def kernel(state_ref, arrived_ref, high_ref, low_ref, add_ref, out_ref):
        entering = state_ref[...] + arrived_ref[...]
        row = product(entering, (high_ref[...], low_ref[...])) + add_ref[...]
        for d in range(day_count):
            out_ref[d : d + 1] = row[:, d * factors : (d + 1) * factors]

    return pl.pallas_call(
        kernel,
        in_specs=vmem(5),
        out_specs=pl.BlockSpec(memory_space=VMEM),
        out_shape=shape(day_count, factors),
        compiler_params=params(),
        cost_estimate=cost(6 * factors * wide, 1 << 20),
        name="filtered",
    )(state, arrived, high, low, add)


def prepared(index, days, own, smoother, loadings, tables):
    factors = smoother.shape[0]

    def kernel(
        index_ref, in_ref, load_hbm, prec_hbm, start_hbm, stop_hbm, off_hbm, high_ref, low_ref,
        load_ref, scale_ref, prec_ref, start_ref, stop_ref, off_ref, sems,
    ):
        mine = pl.ds(pl.multiple_of(index_ref[0] * own, own), own)
        copies = [
            pltpu.make_async_copy(source, target, sems.at[n])
            for n, (source, target) in enumerate(
                [
                    (prec_hbm.at[:, mine], prec_ref),
                    (start_hbm.at[:, mine], start_ref),
                    (stop_hbm.at[:, mine], stop_ref),
                    (off_hbm.at[:, mine], off_ref),
                    (load_hbm.at[mine], load_ref),
                ]
            )
        ]
        for copy in copies:
            copy.start()
        power = in_ref[...].T
        for p in range(POWERS):
            parts = split(power)
            high_ref[p], low_ref[p] = parts
            if p < POWERS - 1:
                power = product(power, parts)
        for copy in copies:
            copy.wait()
        day = lax.broadcasted_iota(jnp.int32, (days, 1), 0)
        active = activity(day, start_ref[...], stop_ref[...], off_ref[...])
        scale_ref[...] = jnp.where(active, jnp.sqrt(prec_ref[...]), 0.0)

    return pl.pallas_call(
        kernel,
        in_specs=[smem()] + vmem(1) + hbm(5),
        out_specs=vmem(4),
        out_shape=[
            shape(POWERS, factors, factors, dtype=BF16),
            shape(POWERS, factors, factors, dtype=BF16),
            shape(own, factors, dtype=BF16),
            shape(days, own),
        ],
        scratch_shapes=[
            pltpu.VMEM((1, own), F32),
            pltpu.VMEM((1, own), jnp.int32),
            pltpu.VMEM((1, own), jnp.int32),
            pltpu.VMEM((1, own), jnp.int32),
            pltpu.SemaphoreType.DMA((5,)),
        ],
        compiler_params=params(),
        cost_estimate=cost(24 * factors**3, 3 << 20),
        name="prepared",
    )(index, smoother, loadings, *tables)


def finish(index, day_count, gathered, ready, decay, series):
    days, own = series.shape
    factors = decay.shape[1]
    stride = 2 ** (POWERS - 1)
    blocks = days // stride

    def kernel(
        index_ref, gathered_ref, high_ref, low_ref, load_ref, scale_ref, decay_ref, series_ref,
        smooth_ref, score_ref, filt, work,
    ):
        me = index_ref[0]
        for m in range(days // day_count):
            filt[m * day_count : (m + 1) * day_count, :] = gathered_ref[m]
        filtered = filt[...]
        carried = filtered * decay_ref[...]
        carried = jnp.concatenate([jnp.zeros((1, factors), F32), carried[:-1]], 0)
        total = filtered - carried
        for p in range(POWERS - 1):
            reach = 2**p
            later = jnp.concatenate([total[reach:], jnp.zeros((reach, factors), F32)], 0)
            total = total + product(later, (high_ref[p], low_ref[p]))
        far = (high_ref[POWERS - 1], low_ref[POWERS - 1])
        row = total[(blocks - 1) * stride :]
        work[(blocks - 1) * stride :, :] = row
        for b in reversed(range(blocks - 1)):
            row = total[b * stride : (b + 1) * stride] + product(row, far)
            work[b * stride : (b + 1) * stride, :] = row
        work[...] += carried
        for d in range(day_count):
            smooth_ref[d : d + 1, :] = work[pl.ds(me * day_count + d, 1), :]
        fitted = lax.dot_general(
            work[...].astype(BF16), load_ref[...], (((1,), (1,)), ((), ())),
            preferred_element_type=F32,
        )
        residual = series_ref[...].astype(F32) - fitted
        score_ref[...] = (residual * scale_ref[...]).astype(BF16)

    return pl.pallas_call(
        kernel,
        in_specs=[smem()] + vmem(7),
        out_specs=vmem(2),
        out_shape=[shape(day_count, factors), shape(days, own, dtype=BF16)],
        scratch_shapes=[
            pltpu.VMEM((days, factors), F32),
            pltpu.VMEM((days, factors), F32),
        ],
        compiler_params=params(),
        cost_estimate=cost(2 * days * own * factors, 2 << 20),
        name="finish",
    )(index, gathered, *ready, decay, series)


def local(series, loadings, precision, start_day, stop_day, off_day, decay, gain, smoother):
    devices = lax.axis_size("tm")
    place = lax.axis_index("tm").astype(jnp.int32)
    index = place[None]
    days = series.shape[0]
    day_count = days // devices
    factors = loadings.shape[1]
    tables = [a.reshape(1, -1) for a in (precision, start_day, stop_day, off_day)]
    decay = decay.reshape(1, factors)

    def swapped(array, distance):
        return lax.ppermute(array, "tm", [(i, i ^ distance) for i in range(devices)])

    partial = partial_drive(index, devices, series, loadings, tables)
    partial, first_day = lax.optimization_barrier((partial, index * day_count))
    terms = lax.all_to_all(partial, "tm", 0, 0, tiled=True)
    damped = damped_of(first_day, day_count, loadings, tables, decay)
    running, last, states, tail, packed = block_of(damped, terms, decay, gain)

    upper = (place & 1)[None]
    other = swapped(packed, 1)
    sent, kept = combined(upper, last, tail, other)
    group = min(8, devices)
    pair = ((place % group) >> 1)[None]
    came = [swapped(sent, 2 * m) for m in range(1, group // 2)]
    pieces = [(sent, kept)] + [(half, swapped(half, 1)) for half in came]
    nothing = jnp.zeros((1, factors), F32)
    tail = advanced(pair, upper, nothing, pieces, True)
    smoother, tail = lax.optimization_barrier((smoother, tail))
    ready = prepared(index, days, series.shape[1], smoother, loadings, tables)
    ahead = prefixed(pair, upper, pieces, other, running, last, states)

    state = nothing
    arrived = jnp.where(place // group == 1, swapped(tail, group), 0.0)
    for g in range(1, devices // group - 1):
        state = state + arrived
        moved = advanced(pair, upper, state, pieces)
        pairs = [(g * group + j, (g + 1) * group + j) for j in range(group)]
        arrived = lax.ppermute(moved, "tm", pairs)

    ahead, ready = lax.optimization_barrier((ahead, ready))
    own = filtered_of(state, arrived, *ahead)[None]
    gathered = lax.all_to_all(
        jnp.broadcast_to(own, (devices, day_count, factors)), "tm", 0, 0, tiled=True
    )
    return tuple(finish(index, day_count, gathered, ready, decay, series))


def solution(mesh):
    in_specs = (
        P(None, ("spec", "tm")),
        P("spec", None),
        P("spec"),
        P("spec"),
        P("spec"),
        P("spec"),
        P(),
        P(),
        P(),
    )
    out_specs = (P("tm", "spec"), P(None, ("spec", "tm")))
    return jax.shard_map(local, mesh=mesh, in_specs=in_specs, out_specs=out_specs, check_vma=False)
```
